512 devices in a mesh: band: 32 (over y_hi, z), gx: 8 (over x, core), gy: 2 (over y_lo).
Axes of the slice: x: 4, y: 4 (y_hi: 2, y_lo: 2; y = y_hi * 2 + y_lo), z: 16, core: 2. Of those that a mesh axis runs over, the one named last changes fastest.
Arguments:
- orbitals: float32 [256, 48, 16, 128], P('band', 'gx', 'gy'), may hold values from -120 to 120
- potential: float32 [48, 16, 128], P('gx', 'gy'), may hold values from -6 to 2
Outputs:
- rotated: float32 [256, 48, 16, 128], P('band', 'gx', 'gy')
- gram: float32 [256, 256], P('band')
The draws below stay inside these ranges and needn't reach their ends.
All inputs are finite; a program needn't handle non-finite values.
Results may differ from the reference program's by a relative error of at most 0.0095.
Values may be sent and summed in bfloat16 or wider, within the bound.
A program may use at most 64 MiB of HBM per device.

```python
import math
import jax
import jax.numpy as jnp
from jax import lax

NB = 256
NZ = 128
NX = 48
NY = 16


def draw_orbitals(key, part):
    keys = jax.random.split(jax.random.fold_in(key, 11), 3)
    base = jnp.clip(jax.random.normal(keys[0], (NB, NX, NY, NZ), jnp.float32), -5.0, 5.0)
    mixed = base + 0.7 * jnp.roll(base, -1, 0)
    cell_scale = jnp.exp(jax.random.uniform(keys[1], (1, NX, NY, NZ), jnp.float32, 0.0, math.log(10.0)))
    orbital_scale = jnp.exp(jax.random.uniform(keys[2], (NB, 1, 1, 1), jnp.float32, 0.0, math.log(10.0)))
    return (0.1 * orbital_scale * cell_scale * mixed).astype(jnp.float32)


def levels(rng, extent, cuts, smallest, largest):
    level = 1.0
    for axis_at, parts in cuts:
        steps = jax.random.uniform(jax.random.fold_in(jax.random.fold_in(rng, 6), axis_at), (parts,), jnp.float32, smallest / len(cuts), largest / len(cuts))
        level = level * jnp.repeat(jnp.exp(steps), extent[axis_at] // parts).reshape((-1,) + (1,) * (len(extent) - 1 - axis_at))
    return level


def setup_inputs(seed: int = 0) -> dict:
    key_list = jax.random.split(jax.random.key(seed), 3)
    return {
        "orbitals": draw_orbitals(jax.random.fold_in(key_list[2], 71), 0),
        "potential": jnp.clip(-6.0 + 8.0 * jax.random.uniform(key_list[1], (NX, NY, NZ), jnp.float32) ** levels(key_list[1], (NX, NY, NZ), ((0, 8), (1, 2)), -0.2, 0.2), -6.0, 2.0),
    }


stencil_coeffs = (-5369.0 / 1800.0, 12.0 / 7.0, -15.0 / 56.0, 10.0 / 189.0, -1.0 / 112.0, 2.0 / 1925.0, -1.0 / 16632.0)
spacing = 0.5
low_edge = 5.0
high_edge = 46.0
bottom_edge = -6.5

def filter_scalars():
    half = (high_edge - low_edge) / 2.0
    center = (high_edge + low_edge) / 2.0
    sigma = half / (bottom_edge - center)
    sigma_two = 1.0 / (2.0 / sigma - sigma)
    return (half, center, sigma, sigma_two)

def apply_ham(field, potential):
    laplace = 3.0 * stencil_coeffs[0] * field
    for shift_by in range(1, 7):
        for axis_id in range(3):
            laplace = laplace + stencil_coeffs[shift_by] * (jnp.roll(field, shift_by, axis_id) + jnp.roll(field, -shift_by, axis_id))
    return -0.5 / spacing ** 2 * laplace + potential * field

def filter_one(field, potential):
    half, center, sigma, sigma_two = filter_scalars()
    first = sigma / half * (apply_ham(field, potential) - center * field)
    second = 2.0 * sigma_two / half * (apply_ham(first, potential) - center * first) - sigma * sigma_two * field
    return second.astype(jnp.bfloat16)

def reference(orbitals, potential):
    filtered = lax.map(lambda field: filter_one(field, potential), orbitals)
    flat_rows = filtered.reshape(NB, -1)
    total_cells = flat_rows.shape[1]
    gram = jnp.dot(flat_rows.astype(jnp.float32), flat_rows.T.astype(jnp.float32), preferred_element_type=jnp.float32) / total_cells
    lower = jnp.linalg.cholesky(gram)
    inv_lower = jax.scipy.linalg.solve_triangular(lower, jnp.eye(NB, dtype=jnp.float32), lower=True)
    coeffs = inv_lower.T.astype(jnp.bfloat16)
    rotated = jnp.dot(coeffs.T.astype(jnp.float32), flat_rows.astype(jnp.float32), preferred_element_type=jnp.float32)
    return (rotated.reshape(orbitals.shape), gram)
```

```python
import functools

import jax
import jax.numpy as jnp
from jax import lax
from jax.experimental import pallas as pl
from jax.experimental.pallas import tpu as pltpu
from jax.sharding import PartitionSpec as P

stencil_coeffs = (
    -5369.0 / 1800.0,
    12.0 / 7.0,
    -15.0 / 56.0,
    10.0 / 189.0,
    -1.0 / 112.0,
    2.0 / 1925.0,
    -1.0 / 16632.0,
)
spacing = 0.5
low_edge = 5.0
high_edge = 46.0
bottom_edge = -6.5


def extended(shard, sides, width):
    for axis, dim in sides:
        devices, length = (lax.axis_size(axis), shard.shape[dim])
        up = [(i, (i + 1) % devices) for i in range(devices)]
        down = [(j, i) for i, j in up]
        last = lax.slice_in_dim(shard, length - width, length, axis=dim)
        leading = lax.slice_in_dim(shard, 0, width, axis=dim)
        before = lax.ppermute(last, axis, up)
        after = lax.ppermute(leading, axis, down)
        shard = jnp.concatenate([before, shard, after], axis=dim)
    return shard


def filter_scalars():
    half = (high_edge - low_edge) / 2.0
    center = (high_edge + low_edge) / 2.0
    sigma = half / (bottom_edge - center)
    sigma_two = 1.0 / (2.0 / sigma - sigma)
    return (half, center, sigma, sigma_two)


def apply_ham(field, potential):
    padded = extended(field, (("gx", 1), ("gy", 2)), 6)
    size_x = field.shape[1]
    size_y = field.shape[2]
    laplace = 3.0 * stencil_coeffs[0] * field
    for shift_by in range(1, 7):
        coeff = stencil_coeffs[shift_by]
        laplace = laplace + coeff * (
            padded[:, 6 + shift_by : 6 + shift_by + size_x, 6 : 6 + size_y]
            + padded[:, 6 - shift_by : 6 - shift_by + size_x, 6 : 6 + size_y]
        )
        laplace = laplace + coeff * (
            padded[:, 6 : 6 + size_x, 6 + shift_by : 6 + shift_by + size_y]
            + padded[:, 6 : 6 + size_x, 6 - shift_by : 6 - shift_by + size_y]
        )
        laplace = laplace + coeff * (jnp.roll(field, shift_by, 3) + jnp.roll(field, -shift_by, 3))
    return -0.5 / spacing**2 * laplace + potential[None] * field


def finish_coeffs(gram):
    count = gram.shape[0]
    lower = jnp.linalg.cholesky(gram)
    inv_lower = jax.scipy.linalg.solve_triangular(
        lower, jnp.eye(count, dtype=jnp.float32), lower=True
    )
    return inv_lower.T.astype(jnp.bfloat16)


MESH = pl.DeviceIdType.MESH
BANDS = 32
OWNERS = 24
PLACES = 16
GRID_Y = 2
FULL = 256


def owner_band(share):
    return (share // 3) * 4 + share % 3


def band_share(band):
    return (band // 4) * 3 + band % 4


def place_of(index):
    return {"gx": index // GRID_Y, "gy": index % GRID_Y}


def await_arrivals(buffer, sem):
    pltpu.make_async_copy(buffer, buffer, sem).wait()


def gram_kernel(
    cells,
    mine_ref,
    gram_ref,
    share_ref,
    shares,
    partial,
    pieces,
    piece,
    rows,
    total,
    strips,
    strip,
    blocks,
    send_sem,
    recv_sem,
    local_sem,
):
    band = lax.axis_index("band")
    place = lax.axis_index("gx") * GRID_Y + lax.axis_index("gy")
    owns = band % 4 != 3

    barrier = pltpu.get_barrier_semaphore()

    def greet_band(step, carry):
        pl.semaphore_signal(
            barrier, 1, device_id={"band": (band + step) % BANDS}, device_id_type=MESH
        )
        return carry

    def greet_place(step, carry):
        pl.semaphore_signal(
            barrier, 1, device_id=place_of((place + step) % PLACES), device_id_type=MESH
        )
        return carry

    lax.fori_loop(1, BANDS, greet_band, 0)
    lax.fori_loop(1, PLACES, greet_place, 0)
    pl.semaphore_wait(barrier, BANDS - 1 + PLACES - 1)

    def remote(source, target, phase, device):
        return pltpu.make_async_remote_copy(
            src_ref=source,
            dst_ref=target,
            send_sem=send_sem.at[phase],
            recv_sem=recv_sem.at[phase],
            device_id=device,
            device_id_type=MESH,
        )

    def cell_share(step, carry):
        other = (band + step) % BANDS

        @pl.when(other % 4 != 3)
        def _():
            at = pl.multiple_of(band_share(other) * 16, 16)
            to = pl.multiple_of(band * 16, 16)
            remote(
                mine_ref.at[pl.ds(at, 16)], shares.at[pl.ds(to, 16)], 0, {"band": other}
            ).start()

        return carry

    lax.fori_loop(1, BANDS, cell_share, 0)

    @pl.when(owns)
    def _():
        at = pl.multiple_of(band_share(band) * 16, 16)
        to = pl.multiple_of(band * 16, 16)
        own = pltpu.make_async_copy(
            mine_ref.at[pl.ds(at, 16)], shares.at[pl.ds(to, 16)], local_sem
        )
        own.start()
        own.wait()
        await_arrivals(shares.at[pl.ds(0, 16 * (BANDS - 1))], recv_sem.at[0])
        spread = shares[...].astype(jnp.float32).reshape(BANDS, 2, 8, 128)
        halves = [spread[:, half].reshape(FULL, 128) for half in range(2)]
        both = jnp.concatenate(halves, axis=1).astype(jnp.bfloat16)
        share_ref[...] = both
        local = lax.dot_general(
            both, both, (((1,), (1,)), ((), ())), preferred_element_type=jnp.float32
        )
        partial[...] = local.astype(jnp.bfloat16)

        def send_piece(step, carry):
            other = (place + step) % PLACES
            at = pl.multiple_of(other * 16, 16)
            remote(
                partial.at[pl.ds(at, 16)], pieces.at[place], 1, place_of(other)
            ).start()
            return carry

        lax.fori_loop(1, PLACES, send_piece, 0)
        at = pl.multiple_of(place * 16, 16)
        pieces[place] = partial[pl.ds(at, 16)]
        await_arrivals(pieces.at[pl.ds(0, PLACES - 1)], recv_sem.at[1])
        summed = jnp.sum(pieces[...].astype(jnp.float32), axis=0)
        halved = jnp.concatenate([summed[:, :128], summed[:, 128:]], axis=0)
        piece[...] = halved.reshape(BANDS, 1, 128)

        def send_row(step, carry):
            other = (band + step) % BANDS
            remote(
                piece.at[other], rows.at[band_share(band)], 2, {"band": other}
            ).start()
            return carry

        lax.fori_loop(1, BANDS, send_row, 0)
        rows[band_share(band)] = piece[band]
        await_arrivals(rows.at[pl.ds(0, OWNERS - 1)], recv_sem.at[2])

    @pl.when(jnp.logical_not(owns))
    def _():
        share_ref[...] = jnp.zeros_like(share_ref)
        await_arrivals(rows, recv_sem.at[2])

    total[...] = jnp.sum(rows[...], axis=0) / cells

    def send_total(step, carry):
        other = (band + step) % BANDS
        remote(total, strips.at[band], 3, {"band": other}).start()
        return carry

    lax.fori_loop(1, BANDS, send_total, 0)
    strips[band] = total[...]
    await_arrivals(strips.at[pl.ds(0, BANDS - 1)], recv_sem.at[3])
    strip[...] = strips[...].reshape(BANDS, 128)

    def send_strip(step, carry):
        other = (place + step) % PLACES
        remote(strip, blocks.at[place], 4, place_of(other)).start()
        return carry

    lax.fori_loop(1, PLACES, send_strip, 0)
    blocks[place] = strip[...]
    await_arrivals(blocks.at[pl.ds(0, PLACES - 1)], recv_sem.at[4])
    found = blocks[...]
    gram_ref[:, :128] = found[:, :16].reshape(FULL, 128)
    gram_ref[:, 128:] = found[:, 16:].reshape(FULL, 128)

    @pl.when(owns)
    def _():
        await_arrivals(mine_ref.at[pl.ds(0, 16 * (OWNERS - 1))], send_sem.at[0])
        await_arrivals(pieces.at[pl.ds(0, PLACES - 1)], send_sem.at[1])
        await_arrivals(piece.at[pl.ds(0, BANDS - 1)], send_sem.at[2])

    @pl.when(jnp.logical_not(owns))
    def _():
        await_arrivals(mine_ref, send_sem.at[0])

    await_arrivals(strips.at[pl.ds(0, BANDS - 1)], send_sem.at[3])
    await_arrivals(blocks.at[pl.ds(0, PLACES - 1)], send_sem.at[4])


def gather_gram(mine, cells):
    return pl.pallas_call(
        functools.partial(gram_kernel, cells),
        out_shape=(
            jax.ShapeDtypeStruct((FULL, FULL), jnp.float32),
            jax.ShapeDtypeStruct((FULL, FULL), jnp.bfloat16),
        ),
        in_specs=[pl.BlockSpec(memory_space=pltpu.VMEM)],
        out_specs=(pl.BlockSpec(memory_space=pltpu.VMEM),) * 2,
        scratch_shapes=[
            pltpu.VMEM((BANDS * 16, 128), jnp.bfloat16),
            pltpu.VMEM((FULL, FULL), jnp.bfloat16),
            pltpu.VMEM((PLACES, 16, FULL), jnp.bfloat16),
            pltpu.VMEM((BANDS, 1, 128), jnp.float32),
            pltpu.VMEM((OWNERS, 1, 128), jnp.float32),
            pltpu.VMEM((1, 128), jnp.float32),
            pltpu.VMEM((BANDS, 1, 128), jnp.float32),
            pltpu.VMEM((BANDS, 128), jnp.float32),
            pltpu.VMEM((PLACES, BANDS, 128), jnp.float32),
            pltpu.SemaphoreType.DMA((5,)),
            pltpu.SemaphoreType.DMA((5,)),
            pltpu.SemaphoreType.DMA,
        ],
        compiler_params=pltpu.CompilerParams(collective_id=1, has_side_effects=True),
        name="gram_exchange",
    )(mine)


def rotate_kernel(coeffs_ref, share_ref, out_ref, parcels, arrived, send_sem, recv_sem, local_sem):
    band = lax.axis_index("band")
    owns = band % 4 != 3
    barrier = pltpu.get_barrier_semaphore()

    def greet_band(step, carry):
        pl.semaphore_signal(
            barrier, 1, device_id={"band": (band + step) % BANDS}, device_id_type=MESH
        )
        return carry

    lax.fori_loop(1, BANDS, greet_band, 0)

    @pl.when(owns)
    def _():
        turned = lax.dot_general(
            coeffs_ref[...],
            share_ref[...],
            (((0,), (0,)), ((), ())),
            preferred_element_type=jnp.float32,
        )
        halves = [turned[:, 128 * h : 128 * h + 128].reshape(BANDS, 1, 8, 128) for h in range(2)]
        parcels[...] = (
            jnp.concatenate(halves, axis=1).reshape(BANDS * 16, 128).astype(jnp.bfloat16)
        )

    pl.semaphore_wait(barrier, BANDS - 1)

    @pl.when(owns)
    def _():
        to = pl.multiple_of(band_share(band) * 16, 16)

        def send_parcel(step, carry):
            other = (band + step) % BANDS
            at = pl.multiple_of(other * 16, 16)
            pltpu.make_async_remote_copy(
                src_ref=parcels.at[pl.ds(at, 16)],
                dst_ref=arrived.at[pl.ds(to, 16)],
                send_sem=send_sem,
                recv_sem=recv_sem,
                device_id={"band": other},
                device_id_type=MESH,
            ).start()
            return carry

        lax.fori_loop(1, BANDS, send_parcel, 0)
        at = pl.multiple_of(band * 16, 16)
        own = pltpu.make_async_copy(
            parcels.at[pl.ds(at, 16)], arrived.at[pl.ds(to, 16)], local_sem
        )
        own.start()
        own.wait()
        await_arrivals(arrived.at[pl.ds(0, 16 * (OWNERS - 1))], recv_sem)

    @pl.when(jnp.logical_not(owns))
    def _():
        await_arrivals(arrived, recv_sem)

    found = arrived[...].astype(jnp.float32).reshape(6, 8, 8, 128)
    for at in range(6):
        out_ref[:, at] = jnp.swapaxes(found[at], 0, 1)

    @pl.when(owns)
    def _():
        await_arrivals(parcels.at[pl.ds(0, 16 * (BANDS - 1))], send_sem)


def rotate(coeffs, share):
    return pl.pallas_call(
        rotate_kernel,
        out_shape=jax.ShapeDtypeStruct((8, 6, 8, 128), jnp.float32),
        in_specs=[pl.BlockSpec(memory_space=pltpu.VMEM)] * 2,
        out_specs=pl.BlockSpec(memory_space=pltpu.VMEM),
        scratch_shapes=[
            pltpu.VMEM((BANDS * 16, 128), jnp.bfloat16),
            pltpu.VMEM((OWNERS * 16, 128), jnp.bfloat16),
            pltpu.SemaphoreType.DMA,
            pltpu.SemaphoreType.DMA,
            pltpu.SemaphoreType.DMA,
        ],
        compiler_params=pltpu.CompilerParams(collective_id=2, has_side_effects=True),
        name="rotation_exchange",
    )(coeffs, share)


def body(orbitals, potential):
    half, center, sigma, sigma_two = filter_scalars()
    first = sigma / half * (apply_ham(orbitals, potential) - center * orbitals)
    second = (
        2.0 * sigma_two / half * (apply_ham(first, potential) - center * first)
        - sigma * sigma_two * orbitals
    )
    local_count = orbitals.shape[0]
    mine = second.astype(jnp.bfloat16).transpose(1, 2, 0, 3).reshape(-1, 128)
    total_cells = mine.shape[0] * 16 * lax.axis_size("gx") * lax.axis_size("gy")
    gram, share = gather_gram(mine, float(total_cells))
    coeffs = finish_coeffs(gram)
    rotated = rotate(coeffs, share)
    gram_rows = lax.dynamic_slice_in_dim(gram, lax.axis_index("band") * local_count, local_count, 0)
    return (rotated, gram_rows)


def solution(mesh):
    return jax.shard_map(
        body,
        mesh=mesh,
        in_specs=(P("band", "gx", "gy", None), P("gx", "gy", None)),
        out_specs=(P("band", "gx", "gy", None), P("band", None)),
        check_vma=False,
    )
```

```python
import functools

import jax
import jax.numpy as jnp
from jax import lax
from jax.experimental import pallas as pl
from jax.experimental.pallas import tpu as pltpu
from jax.sharding import PartitionSpec as P

stencil_coeffs = (
    -5369.0 / 1800.0,
    12.0 / 7.0,
    -15.0 / 56.0,
    10.0 / 189.0,
    -1.0 / 112.0,
    2.0 / 1925.0,
    -1.0 / 16632.0,
)
spacing = 0.5
low_edge = 5.0
high_edge = 46.0
bottom_edge = -6.5


def filter_scalars():
    half = (high_edge - low_edge) / 2.0
    center = (high_edge + low_edge) / 2.0
    sigma = half / (bottom_edge - center)
    sigma_two = 1.0 / (2.0 / sigma - sigma)
    return (half, center, sigma, sigma_two)


def finish_coeffs(gram):
    count = gram.shape[0]
    lower = jnp.linalg.cholesky(gram)
    inv_lower = jax.scipy.linalg.solve_triangular(
        lower, jnp.eye(count, dtype=jnp.float32), lower=True
    )
    return inv_lower.T.astype(jnp.bfloat16)


MESH = pl.DeviceIdType.MESH
BANDS = 32
OWNERS = 24
PLACES = 16
GRID_Y = 2
FULL = 256


def owner_band(share):
    return (share // 3) * 4 + share % 3


def band_share(band):
    return (band // 4) * 3 + band % 4


def place_of(index):
    return {"gx": index // GRID_Y, "gy": index % GRID_Y}


def await_arrivals(buffer, sem):
    pltpu.make_async_copy(buffer, buffer, sem).wait()


def kinetic(wide, other, at):
    own = wide[6 + at]
    around = other[at]
    column = jnp.concatenate([around, own, around], axis=0)
    total = 3.0 * stencil_coeffs[0] * own
    for m in range(1, 7):
        near = wide[6 + at + m] + wide[6 + at - m]
        near = near + (column[8 + m : 16 + m] + column[8 - m : 16 - m])
        near = near + (pltpu.roll(own, m, 2) + pltpu.roll(own, 128 - m, 2))
        total = total + stencil_coeffs[m] * near
    return own, -0.5 / spacing**2 * total


def gram_kernel(
    cells,
    orbitals_ref,
    potential_ref,
    gram_ref,
    share_ref,
    mine_ref,
    outgoing,
    halos,
    base,
    slope,
    other_side,
    shares,
    partial,
    pieces,
    piece,
    rows,
    total,
    strips,
    strip,
    blocks,
    halo_send,
    halo_recv,
    send_sem,
    recv_sem,
    local_sem,
):
    band = lax.axis_index("band")
    place = lax.axis_index("gx") * GRID_Y + lax.axis_index("gy")
    owns = band % 4 != 3

    barrier = pltpu.get_barrier_semaphore()

    def greet_band(step, carry):
        pl.semaphore_signal(
            barrier, 1, device_id={"band": (band + step) % BANDS}, device_id_type=MESH
        )
        return carry

    def greet_place(step, carry):
        pl.semaphore_signal(
            barrier, 1, device_id=place_of((place + step) % PLACES), device_id_type=MESH
        )
        return carry

    lax.fori_loop(1, BANDS, greet_band, 0)
    lax.fori_loop(1, PLACES, greet_place, 0)

    def turn(at, carry):
        plane = jnp.swapaxes(orbitals_ref[:, at], 0, 1)
        base[6 + at] = plane
        rows_at = pl.ds(pl.multiple_of(at * 64, 64), 64)
        outgoing[0, rows_at] = plane.reshape(64, 128).astype(jnp.bfloat16)
        return carry

    lax.fori_loop(0, 6, turn, 0)
    pl.semaphore_wait(barrier, BANDS - 1 + PLACES - 1)

    place_x, place_y = lax.axis_index("gx"), lax.axis_index("gy")
    sides = (
        {"gx": (place_x + 1) % 8},
        {"gx": (place_x + 7) % 8},
        {"gy": 1 - place_y},
    )

    def halo_copy(turn_at, side):
        return pltpu.make_async_remote_copy(
            src_ref=outgoing.at[turn_at],
            dst_ref=halos.at[turn_at, side],
            send_sem=halo_send.at[turn_at, side],
            recv_sem=halo_recv.at[turn_at, side],
            device_id=sides[side],
            device_id_type=MESH,
        )

    def halo_take(turn_at, wide):
        for side in range(3):
            halo_copy(turn_at, side).wait_recv()

        def widen(at, carry):
            rows_at = pl.ds(pl.multiple_of(at * 64, 64), 64)
            for side, target, offset in ((0, wide, 0), (1, wide, 12), (2, other_side, 0)):
                block = halos[turn_at, side, rows_at]
                target[at + offset] = block.astype(jnp.float32).reshape(8, 8, 128)
            return carry

        lax.fori_loop(0, 6, widen, 0)

    half, center, sigma, sigma_two = filter_scalars()
    for side in (2, 0, 1):
        halo_copy(0, side).start()
    halo_take(0, base)

    def first_step(at, carry):
        own, moved = kinetic(base, other_side, at)
        shifted = (potential_ref[at] - center)[:, None, :]
        result = sigma / half * (moved + shifted * own)
        slope[6 + at] = result
        rows_at = pl.ds(pl.multiple_of(at * 64, 64), 64)
        outgoing[1, rows_at] = result.reshape(64, 128).astype(jnp.bfloat16)
        return carry

    lax.fori_loop(0, 6, first_step, 0)
    for side in (2, 0, 1):
        halo_copy(1, side).start()
    halo_take(1, slope)

    def second_step(at, carry):
        own, moved = kinetic(slope, other_side, at)
        shifted = (potential_ref[at] - center)[:, None, :]
        result = 2.0 * sigma_two / half * (moved + shifted * own) - sigma * sigma_two * base[6 + at]
        rows_at = pl.ds(pl.multiple_of(at * 64, 64), 64)
        mine_ref[rows_at] = result.reshape(64, 128).astype(jnp.bfloat16)
        return carry

    lax.fori_loop(0, 6, second_step, 0)

    def remote(source, target, phase, device):
        return pltpu.make_async_remote_copy(
            src_ref=source,
            dst_ref=target,
            send_sem=send_sem.at[phase],
            recv_sem=recv_sem.at[phase],
            device_id=device,
            device_id_type=MESH,
        )

    def cell_share(step, carry):
        other = (band + step) % BANDS

        @pl.when(other % 4 != 3)
        def _():
            at = pl.multiple_of(band_share(other) * 16, 16)
            to = pl.multiple_of(band * 16, 16)
            remote(
                mine_ref.at[pl.ds(at, 16)], shares.at[pl.ds(to, 16)], 0, {"band": other}
            ).start()

        return carry

    lax.fori_loop(1, BANDS, cell_share, 0)

    @pl.when(owns)
    def _():
        at = pl.multiple_of(band_share(band) * 16, 16)
        to = pl.multiple_of(band * 16, 16)
        own = pltpu.make_async_copy(
            mine_ref.at[pl.ds(at, 16)], shares.at[pl.ds(to, 16)], local_sem
        )
        own.start()
        own.wait()
        await_arrivals(shares.at[pl.ds(0, 16 * (BANDS - 1))], recv_sem.at[0])
        spread = shares[...].astype(jnp.float32).reshape(BANDS, 2, 8, 128)
        halves = [spread[:, half].reshape(FULL, 128) for half in range(2)]
        both = jnp.concatenate(halves, axis=1).astype(jnp.bfloat16)
        share_ref[...] = both
        local = lax.dot_general(
            both, both, (((1,), (1,)), ((), ())), preferred_element_type=jnp.float32
        )
        partial[...] = local.astype(jnp.bfloat16)

        def send_piece(step, carry):
            other = (place + step) % PLACES
            at = pl.multiple_of(other * 16, 16)
            remote(
                partial.at[pl.ds(at, 16)], pieces.at[place], 1, place_of(other)
            ).start()
            return carry

        lax.fori_loop(1, PLACES, send_piece, 0)
        at = pl.multiple_of(place * 16, 16)
        pieces[place] = partial[pl.ds(at, 16)]
        await_arrivals(pieces.at[pl.ds(0, PLACES - 1)], recv_sem.at[1])
        summed = jnp.sum(pieces[...].astype(jnp.float32), axis=0)
        halved = jnp.concatenate([summed[:, :128], summed[:, 128:]], axis=0)
        piece[...] = halved.reshape(BANDS, 1, 128)

        def send_row(step, carry):
            other = (band + step) % BANDS
            remote(
                piece.at[other], rows.at[band_share(band)], 2, {"band": other}
            ).start()
            return carry

        lax.fori_loop(1, BANDS, send_row, 0)
        rows[band_share(band)] = piece[band]
        await_arrivals(rows.at[pl.ds(0, OWNERS - 1)], recv_sem.at[2])

    @pl.when(jnp.logical_not(owns))
    def _():
        share_ref[...] = jnp.zeros_like(share_ref)
        await_arrivals(rows, recv_sem.at[2])

    total[...] = jnp.sum(rows[...], axis=0) / cells

    def send_total(step, carry):
        other = (band + step) % BANDS
        remote(total, strips.at[band], 3, {"band": other}).start()
        return carry

    lax.fori_loop(1, BANDS, send_total, 0)
    strips[band] = total[...]
    await_arrivals(strips.at[pl.ds(0, BANDS - 1)], recv_sem.at[3])
    strip[...] = strips[...].reshape(BANDS, 128)

    def send_strip(step, carry):
        other = (place + step) % PLACES
        remote(strip, blocks.at[place], 4, place_of(other)).start()
        return carry

    lax.fori_loop(1, PLACES, send_strip, 0)
    blocks[place] = strip[...]
    await_arrivals(blocks.at[pl.ds(0, PLACES - 1)], recv_sem.at[4])
    found = blocks[...]
    gram_ref[:, :128] = found[:, :16].reshape(FULL, 128)
    gram_ref[:, 128:] = found[:, 16:].reshape(FULL, 128)

    @pl.when(owns)
    def _():
        await_arrivals(mine_ref.at[pl.ds(0, 16 * (OWNERS - 1))], send_sem.at[0])
        await_arrivals(pieces.at[pl.ds(0, PLACES - 1)], send_sem.at[1])
        await_arrivals(piece.at[pl.ds(0, BANDS - 1)], send_sem.at[2])

    @pl.when(jnp.logical_not(owns))
    def _():
        await_arrivals(mine_ref, send_sem.at[0])

    for turn_at in range(2):
        for side in range(3):
            halo_copy(turn_at, side).wait_send()
    await_arrivals(strips.at[pl.ds(0, BANDS - 1)], send_sem.at[3])
    await_arrivals(blocks.at[pl.ds(0, PLACES - 1)], send_sem.at[4])


def gather_gram(orbitals, potential, cells):
    return pl.pallas_call(
        functools.partial(gram_kernel, cells),
        out_shape=(
            jax.ShapeDtypeStruct((FULL, FULL), jnp.float32),
            jax.ShapeDtypeStruct((FULL, FULL), jnp.bfloat16),
        ),
        in_specs=[pl.BlockSpec(memory_space=pltpu.VMEM)] * 2,
        out_specs=(pl.BlockSpec(memory_space=pltpu.VMEM),) * 2,
        scratch_shapes=[
            pltpu.VMEM((384, 128), jnp.bfloat16),
            pltpu.VMEM((2, 384, 128), jnp.bfloat16),
            pltpu.VMEM((2, 3, 384, 128), jnp.bfloat16),
            pltpu.VMEM((18, 8, 8, 128), jnp.float32),
            pltpu.VMEM((18, 8, 8, 128), jnp.float32),
            pltpu.VMEM((6, 8, 8, 128), jnp.float32),
            pltpu.VMEM((BANDS * 16, 128), jnp.bfloat16),
            pltpu.VMEM((FULL, FULL), jnp.bfloat16),
            pltpu.VMEM((PLACES, 16, FULL), jnp.bfloat16),
            pltpu.VMEM((BANDS, 1, 128), jnp.float32),
            pltpu.VMEM((OWNERS, 1, 128), jnp.float32),
            pltpu.VMEM((1, 128), jnp.float32),
            pltpu.VMEM((BANDS, 1, 128), jnp.float32),
            pltpu.VMEM((BANDS, 128), jnp.float32),
            pltpu.VMEM((PLACES, BANDS, 128), jnp.float32),
            pltpu.SemaphoreType.DMA((2, 3)),
            pltpu.SemaphoreType.DMA((2, 3)),
            pltpu.SemaphoreType.DMA((5,)),
            pltpu.SemaphoreType.DMA((5,)),
            pltpu.SemaphoreType.DMA,
        ],
        compiler_params=pltpu.CompilerParams(collective_id=1, has_side_effects=True),
        name="gram_exchange",
    )(orbitals, potential)


def rotate_kernel(coeffs_ref, share_ref, out_ref, parcels, arrived, send_sem, recv_sem, local_sem):
    band = lax.axis_index("band")
    owns = band % 4 != 3
    barrier = pltpu.get_barrier_semaphore()

    def greet_band(step, carry):
        pl.semaphore_signal(
            barrier, 1, device_id={"band": (band + step) % BANDS}, device_id_type=MESH
        )
        return carry

    lax.fori_loop(1, BANDS, greet_band, 0)

    @pl.when(owns)
    def _():
        turned = lax.dot_general(
            coeffs_ref[...],
            share_ref[...],
            (((0,), (0,)), ((), ())),
            preferred_element_type=jnp.float32,
        )
        halves = [turned[:, 128 * h : 128 * h + 128].reshape(BANDS, 1, 8, 128) for h in range(2)]
        parcels[...] = (
            jnp.concatenate(halves, axis=1).reshape(BANDS * 16, 128).astype(jnp.bfloat16)
        )

    pl.semaphore_wait(barrier, BANDS - 1)

    @pl.when(owns)
    def _():
        to = pl.multiple_of(band_share(band) * 16, 16)

        def send_parcel(step, carry):
            other = (band + step) % BANDS
            at = pl.multiple_of(other * 16, 16)
            pltpu.make_async_remote_copy(
                src_ref=parcels.at[pl.ds(at, 16)],
                dst_ref=arrived.at[pl.ds(to, 16)],
                send_sem=send_sem,
                recv_sem=recv_sem,
                device_id={"band": other},
                device_id_type=MESH,
            ).start()
            return carry

        lax.fori_loop(1, BANDS, send_parcel, 0)
        at = pl.multiple_of(band * 16, 16)
        own = pltpu.make_async_copy(
            parcels.at[pl.ds(at, 16)], arrived.at[pl.ds(to, 16)], local_sem
        )
        own.start()
        own.wait()
        await_arrivals(arrived.at[pl.ds(0, 16 * (OWNERS - 1))], recv_sem)

    @pl.when(jnp.logical_not(owns))
    def _():
        await_arrivals(arrived, recv_sem)

    found = arrived[...].astype(jnp.float32).reshape(6, 8, 8, 128)
    for at in range(6):
        out_ref[:, at] = jnp.swapaxes(found[at], 0, 1)

    @pl.when(owns)
    def _():
        await_arrivals(parcels.at[pl.ds(0, 16 * (BANDS - 1))], send_sem)


def rotate(coeffs, share):
    return pl.pallas_call(
        rotate_kernel,
        out_shape=jax.ShapeDtypeStruct((8, 6, 8, 128), jnp.float32),
        in_specs=[pl.BlockSpec(memory_space=pltpu.VMEM)] * 2,
        out_specs=pl.BlockSpec(memory_space=pltpu.VMEM),
        scratch_shapes=[
            pltpu.VMEM((BANDS * 16, 128), jnp.bfloat16),
            pltpu.VMEM((OWNERS * 16, 128), jnp.bfloat16),
            pltpu.SemaphoreType.DMA,
            pltpu.SemaphoreType.DMA,
            pltpu.SemaphoreType.DMA,
        ],
        compiler_params=pltpu.CompilerParams(collective_id=2, has_side_effects=True),
        name="rotation_exchange",
    )(coeffs, share)


def body(orbitals, potential):
    local_count = orbitals.shape[0]
    spots = orbitals.shape[1] * orbitals.shape[2] * orbitals.shape[3]
    total_cells = spots * lax.axis_size("gx") * lax.axis_size("gy")
    gram, share = gather_gram(orbitals, potential, float(total_cells))
    coeffs = finish_coeffs(gram)
    rotated = rotate(coeffs, share)
    gram_rows = lax.dynamic_slice_in_dim(gram, lax.axis_index("band") * local_count, local_count, 0)
    return (rotated, gram_rows)


def solution(mesh):
    return jax.shard_map(
        body,
        mesh=mesh,
        in_specs=(P("band", "gx", "gy", None), P("gx", "gy", None)),
        out_specs=(P("band", "gx", "gy", None), P("band", None)),
        check_vma=False,
    )
```

```python
import functools

import jax
import jax.numpy as jnp
from jax import lax
from jax.experimental import pallas as pl
from jax.experimental.pallas import tpu as pltpu
from jax.sharding import PartitionSpec as P

stencil_coeffs = (
    -5369.0 / 1800.0,
    12.0 / 7.0,
    -15.0 / 56.0,
    10.0 / 189.0,
    -1.0 / 112.0,
    2.0 / 1925.0,
    -1.0 / 16632.0,
)
spacing = 0.5
low_edge = 5.0
high_edge = 46.0
bottom_edge = -6.5


def filter_scalars():
    half = (high_edge - low_edge) / 2.0
    center = (high_edge + low_edge) / 2.0
    sigma = half / (bottom_edge - center)
    sigma_two = 1.0 / (2.0 / sigma - sigma)
    return (half, center, sigma, sigma_two)


MESH = pl.DeviceIdType.MESH
BANDS = 32
OWNERS = 24
PLACES = 16
GRID_Y = 2
FULL = 256


def owner_band(share):
    return (share // 3) * 4 + share % 3


def band_share(band):
    return (band // 4) * 3 + band % 4


def place_of(index):
    return {"gx": index // GRID_Y, "gy": index % GRID_Y}


def await_arrivals(buffer, sem):
    pltpu.make_async_copy(buffer, buffer, sem).wait()


def kinetic(wide, other, at):
    own = wide[6 + at]
    around = other[at]
    column = jnp.concatenate([around, own, around], axis=0)
    total = 3.0 * stencil_coeffs[0] * own
    for m in range(1, 7):
        near = wide[6 + at + m] + wide[6 + at - m]
        near = near + (column[8 + m : 16 + m] + column[8 - m : 16 - m])
        near = near + (pltpu.roll(own, m, 2) + pltpu.roll(own, 128 - m, 2))
        total = total + stencil_coeffs[m] * near
    return own, -0.5 / spacing**2 * total


def gram_kernel(
    cells,
    orbitals_ref,
    potential_ref,
    gram_ref,
    share_ref,
    mine_ref,
    outgoing,
    halos,
    base,
    slope,
    other_side,
    shares,
    partial,
    pieces,
    piece,
    rows,
    total,
    strips,
    strip,
    blocks,
    halo_send,
    halo_recv,
    send_sem,
    recv_sem,
    local_sem,
):
    band = lax.axis_index("band")
    place = lax.axis_index("gx") * GRID_Y + lax.axis_index("gy")
    owns = band % 4 != 3

    barrier = pltpu.get_barrier_semaphore()

    def greet_band(step, carry):
        pl.semaphore_signal(
            barrier, 1, device_id={"band": (band + step) % BANDS}, device_id_type=MESH
        )
        return carry

    def greet_place(step, carry):
        pl.semaphore_signal(
            barrier, 1, device_id=place_of((place + step) % PLACES), device_id_type=MESH
        )
        return carry

    lax.fori_loop(1, BANDS, greet_band, 0)
    lax.fori_loop(1, PLACES, greet_place, 0)

    def turn(at, carry):
        plane = jnp.swapaxes(orbitals_ref[:, at], 0, 1)
        base[6 + at] = plane
        rows_at = pl.ds(pl.multiple_of(at * 64, 64), 64)
        outgoing[0, rows_at] = plane.reshape(64, 128).astype(jnp.bfloat16)
        return carry

    lax.fori_loop(0, 6, turn, 0)
    pl.semaphore_wait(barrier, BANDS - 1 + PLACES - 1)

    place_x, place_y = lax.axis_index("gx"), lax.axis_index("gy")
    sides = (
        {"gx": (place_x + 1) % 8},
        {"gx": (place_x + 7) % 8},
        {"gy": 1 - place_y},
    )

    def halo_copy(turn_at, side):
        return pltpu.make_async_remote_copy(
            src_ref=outgoing.at[turn_at],
            dst_ref=halos.at[turn_at, side],
            send_sem=halo_send.at[turn_at, side],
            recv_sem=halo_recv.at[turn_at, side],
            device_id=sides[side],
            device_id_type=MESH,
        )

    def halo_take(turn_at, wide):
        for side in range(3):
            halo_copy(turn_at, side).wait_recv()

        def widen(at, carry):
            rows_at = pl.ds(pl.multiple_of(at * 64, 64), 64)
            for side, target, offset in ((0, wide, 0), (1, wide, 12), (2, other_side, 0)):
                block = halos[turn_at, side, rows_at]
                target[at + offset] = block.astype(jnp.float32).reshape(8, 8, 128)
            return carry

        lax.fori_loop(0, 6, widen, 0)

    half, center, sigma, sigma_two = filter_scalars()
    for side in (2, 0, 1):
        halo_copy(0, side).start()
    halo_take(0, base)

    def first_step(at, carry):
        own, moved = kinetic(base, other_side, at)
        shifted = (potential_ref[at] - center)[:, None, :]
        result = sigma / half * (moved + shifted * own)
        slope[6 + at] = result
        rows_at = pl.ds(pl.multiple_of(at * 64, 64), 64)
        outgoing[1, rows_at] = result.reshape(64, 128).astype(jnp.bfloat16)
        return carry

    lax.fori_loop(0, 6, first_step, 0)
    for side in (2, 0, 1):
        halo_copy(1, side).start()
    halo_take(1, slope)

    def second_step(at, carry):
        own, moved = kinetic(slope, other_side, at)
        shifted = (potential_ref[at] - center)[:, None, :]
        result = 2.0 * sigma_two / half * (moved + shifted * own) - sigma * sigma_two * base[6 + at]
        rows_at = pl.ds(pl.multiple_of(at * 64, 64), 64)
        mine_ref[rows_at] = result.reshape(64, 128).astype(jnp.bfloat16)
        return carry

    lax.fori_loop(0, 6, second_step, 0)

    def remote(source, target, phase, device):
        return pltpu.make_async_remote_copy(
            src_ref=source,
            dst_ref=target,
            send_sem=send_sem.at[phase],
            recv_sem=recv_sem.at[phase],
            device_id=device,
            device_id_type=MESH,
        )

    def cell_share(step, carry):
        other = (band + step) % BANDS

        @pl.when(other % 4 != 3)
        def _():
            at = pl.multiple_of(band_share(other) * 16, 16)
            to = pl.multiple_of(band * 16, 16)
            remote(
                mine_ref.at[pl.ds(at, 16)], shares.at[pl.ds(to, 16)], 0, {"band": other}
            ).start()

        return carry

    lax.fori_loop(1, BANDS, cell_share, 0)

    @pl.when(owns)
    def _():
        at = pl.multiple_of(band_share(band) * 16, 16)
        to = pl.multiple_of(band * 16, 16)
        own = pltpu.make_async_copy(
            mine_ref.at[pl.ds(at, 16)], shares.at[pl.ds(to, 16)], local_sem
        )
        own.start()
        own.wait()
        await_arrivals(shares.at[pl.ds(0, 16 * (BANDS - 1))], recv_sem.at[0])
        spread = shares[...].astype(jnp.float32).reshape(BANDS, 2, 8, 128)
        halves = [spread[:, half].reshape(FULL, 128) for half in range(2)]
        both = jnp.concatenate(halves, axis=1).astype(jnp.bfloat16)
        share_ref[...] = both
        local = lax.dot_general(
            both, both, (((1,), (1,)), ((), ())), preferred_element_type=jnp.float32
        )
        partial[...] = local.astype(jnp.bfloat16)

        def send_piece(step, carry):
            other = (place + step) % PLACES
            at = pl.multiple_of(other * 16, 16)
            remote(
                partial.at[pl.ds(at, 16)], pieces.at[place], 1, place_of(other)
            ).start()
            return carry

        lax.fori_loop(1, PLACES, send_piece, 0)
        at = pl.multiple_of(place * 16, 16)
        pieces[place] = partial[pl.ds(at, 16)]
        await_arrivals(pieces.at[pl.ds(0, PLACES - 1)], recv_sem.at[1])
        summed = jnp.sum(pieces[...].astype(jnp.float32), axis=0)
        halved = jnp.concatenate([summed[:, :128], summed[:, 128:]], axis=0)
        piece[...] = halved.reshape(BANDS, 1, 128)

        def send_row(step, carry):
            other = (band + step) % BANDS
            remote(
                piece.at[other], rows.at[band_share(band)], 2, {"band": other}
            ).start()
            return carry

        lax.fori_loop(1, BANDS, send_row, 0)
        rows[band_share(band)] = piece[band]
        await_arrivals(rows.at[pl.ds(0, OWNERS - 1)], recv_sem.at[2])

    @pl.when(jnp.logical_not(owns))
    def _():
        share_ref[...] = jnp.zeros_like(share_ref)
        await_arrivals(rows, recv_sem.at[2])

    total[...] = jnp.sum(rows[...], axis=0) / cells

    def send_total(step, carry):
        other = (band + step) % BANDS
        remote(total, strips.at[band], 3, {"band": other}).start()
        return carry

    lax.fori_loop(1, BANDS, send_total, 0)
    strips[band] = total[...]
    await_arrivals(strips.at[pl.ds(0, BANDS - 1)], recv_sem.at[3])
    strip[...] = strips[...].reshape(BANDS, 128)

    def send_strip(step, carry):
        other = (place + step) % PLACES
        remote(strip, blocks.at[place], 4, place_of(other)).start()
        return carry

    lax.fori_loop(1, PLACES, send_strip, 0)
    blocks[place] = strip[...]
    await_arrivals(blocks.at[pl.ds(0, PLACES - 1)], recv_sem.at[4])
    found = blocks[...]
    gram_ref[:, :128] = found[:, :16].reshape(FULL, 128)
    gram_ref[:, 128:] = found[:, 16:].reshape(FULL, 128)

    @pl.when(owns)
    def _():
        await_arrivals(mine_ref.at[pl.ds(0, 16 * (OWNERS - 1))], send_sem.at[0])
        await_arrivals(pieces.at[pl.ds(0, PLACES - 1)], send_sem.at[1])
        await_arrivals(piece.at[pl.ds(0, BANDS - 1)], send_sem.at[2])

    @pl.when(jnp.logical_not(owns))
    def _():
        await_arrivals(mine_ref, send_sem.at[0])

    for turn_at in range(2):
        for side in range(3):
            halo_copy(turn_at, side).wait_send()
    await_arrivals(strips.at[pl.ds(0, BANDS - 1)], send_sem.at[3])
    await_arrivals(blocks.at[pl.ds(0, PLACES - 1)], send_sem.at[4])


def gather_gram(orbitals, potential, cells):
    return pl.pallas_call(
        functools.partial(gram_kernel, cells),
        out_shape=(
            jax.ShapeDtypeStruct((FULL, FULL), jnp.float32),
            jax.ShapeDtypeStruct((FULL, FULL), jnp.bfloat16),
        ),
        in_specs=[pl.BlockSpec(memory_space=pltpu.VMEM)] * 2,
        out_specs=(pl.BlockSpec(memory_space=pltpu.VMEM),) * 2,
        scratch_shapes=[
            pltpu.VMEM((384, 128), jnp.bfloat16),
            pltpu.VMEM((2, 384, 128), jnp.bfloat16),
            pltpu.VMEM((2, 3, 384, 128), jnp.bfloat16),
            pltpu.VMEM((18, 8, 8, 128), jnp.float32),
            pltpu.VMEM((18, 8, 8, 128), jnp.float32),
            pltpu.VMEM((6, 8, 8, 128), jnp.float32),
            pltpu.VMEM((BANDS * 16, 128), jnp.bfloat16),
            pltpu.VMEM((FULL, FULL), jnp.bfloat16),
            pltpu.VMEM((PLACES, 16, FULL), jnp.bfloat16),
            pltpu.VMEM((BANDS, 1, 128), jnp.float32),
            pltpu.VMEM((OWNERS, 1, 128), jnp.float32),
            pltpu.VMEM((1, 128), jnp.float32),
            pltpu.VMEM((BANDS, 1, 128), jnp.float32),
            pltpu.VMEM((BANDS, 128), jnp.float32),
            pltpu.VMEM((PLACES, BANDS, 128), jnp.float32),
            pltpu.SemaphoreType.DMA((2, 3)),
            pltpu.SemaphoreType.DMA((2, 3)),
            pltpu.SemaphoreType.DMA((5,)),
            pltpu.SemaphoreType.DMA((5,)),
            pltpu.SemaphoreType.DMA,
        ],
        compiler_params=pltpu.CompilerParams(collective_id=1, has_side_effects=True),
        name="gram_exchange",
    )(orbitals, potential)


def split_parts(value):
    high = value.astype(jnp.bfloat16)
    rest = value - high.astype(jnp.float32)
    middle = rest.astype(jnp.bfloat16)
    return high, middle, (rest - middle.astype(jnp.float32)).astype(jnp.bfloat16)


def inverse_factor(matrix, rows_buf, cols_buf, panel_buf):
    size = matrix.shape[1]
    width = panel_buf.shape[0]
    lane = lax.broadcasted_iota(jnp.int32, (1, size), 1)
    done = []
    for begin in range(0, size, width):
        end = begin + width
        head = matrix[:width]
        rows_buf[...] = head
        for j in range(width):
            cols_buf[j] = jnp.broadcast_to(head[:, begin + j : begin + j + 1], (width, size))
        entry = {}
        for j in range(width):
            for i in range(j, width):
                entry[i, j] = cols_buf[j, i : i + 1, :]
        inside = (lane >= begin) & (lane < end)
        row = [
            jnp.where(inside, (lane == begin + i).astype(jnp.float32), rows_buf[i : i + 1, :])
            for i in range(width)
        ]
        for p in range(width):
            scale = lax.rsqrt(entry[p, p])
            for i in range(p + 1, width):
                entry[i, p] = entry[i, p] * scale
            lead = row[p] * scale
            for i in range(p + 1, width):
                for j in range(p + 1, i + 1):
                    entry[i, j] = entry[i, j] - entry[i, p] * entry[j, p]
                row[i] = row[i] - entry[i, p] * lead
            panel_buf[p : p + 1, :] = lead
        panel = panel_buf[...]
        done.append(jnp.where(jnp.broadcast_to(lane < end, (width, size)), panel, 0.0))
        if end < size:
            high, middle, low = split_parts(panel)
            update = lax.dot_general(
                jnp.concatenate([high, high, middle, high, low, middle], axis=0),
                jnp.concatenate([high, middle, high, low, high, middle], axis=0),
                (((0,), (0,)), ((), ())),
                preferred_element_type=jnp.float32,
            )
            rest = jnp.where(jnp.broadcast_to(inside, (size - end, size)), 0.0, matrix[width:])
            matrix = rest - update[end:]
    return jnp.concatenate(done, axis=0)


def full_dot(left, right, left_dim, right_dim):
    return lax.dot_general(
        left,
        right,
        (((left_dim,), (right_dim,)), ((), ())),
        preferred_element_type=jnp.float32,
        precision=lax.Precision.HIGHEST,
    )


def fill_inverse(gram_ref, inverse_ref, buffers):
    upper = inverse_factor(gram_ref[:128, :128], *buffers)
    lower_left = full_dot(gram_ref[128:, :128], upper, 1, 1)
    remaining = gram_ref[128:, 128:] - full_dot(lower_left, lower_left, 1, 1)
    carried = full_dot(lower_left, upper, 1, 0)
    lower = inverse_factor(remaining, *buffers)
    inverse_ref[:128, :128] = upper.astype(jnp.bfloat16)
    inverse_ref[:128, 128:] = jnp.zeros((128, 128), jnp.bfloat16)
    inverse_ref[128:, 128:] = lower.astype(jnp.bfloat16)
    inverse_ref[128:, :128] = (-full_dot(lower, carried, 1, 0)).astype(jnp.bfloat16)


def rotate_kernel(
    gram_ref,
    share_ref,
    out_ref,
    inverse,
    rows_buf,
    cols_buf,
    panel_buf,
    parcels,
    arrived,
    send_sem,
    recv_sem,
    local_sem,
):
    band = lax.axis_index("band")
    owns = band % 4 != 3
    barrier = pltpu.get_barrier_semaphore()

    def greet_band(step, carry):
        pl.semaphore_signal(
            barrier, 1, device_id={"band": (band + step) % BANDS}, device_id_type=MESH
        )
        return carry

    lax.fori_loop(1, BANDS, greet_band, 0)

    @pl.when(owns)
    def _():
        fill_inverse(gram_ref, inverse, (rows_buf, cols_buf, panel_buf))
        turned = lax.dot_general(
            inverse[...],
            share_ref[...],
            (((1,), (0,)), ((), ())),
            preferred_element_type=jnp.float32,
        )
        halves = [turned[:, 128 * h : 128 * h + 128].reshape(BANDS, 1, 8, 128) for h in range(2)]
        parcels[...] = (
            jnp.concatenate(halves, axis=1).reshape(BANDS * 16, 128).astype(jnp.bfloat16)
        )

    pl.semaphore_wait(barrier, BANDS - 1)

    @pl.when(owns)
    def _():
        to = pl.multiple_of(band_share(band) * 16, 16)

        def send_parcel(step, carry):
            other = (band + step) % BANDS
            at = pl.multiple_of(other * 16, 16)
            pltpu.make_async_remote_copy(
                src_ref=parcels.at[pl.ds(at, 16)],
                dst_ref=arrived.at[pl.ds(to, 16)],
                send_sem=send_sem,
                recv_sem=recv_sem,
                device_id={"band": other},
                device_id_type=MESH,
            ).start()
            return carry

        lax.fori_loop(1, BANDS, send_parcel, 0)
        at = pl.multiple_of(band * 16, 16)
        own = pltpu.make_async_copy(
            parcels.at[pl.ds(at, 16)], arrived.at[pl.ds(to, 16)], local_sem
        )
        own.start()
        own.wait()
        await_arrivals(arrived.at[pl.ds(0, 16 * (OWNERS - 1))], recv_sem)

    @pl.when(jnp.logical_not(owns))
    def _():
        await_arrivals(arrived, recv_sem)

    found = arrived[...].astype(jnp.float32).reshape(6, 8, 8, 128)
    for at in range(6):
        out_ref[:, at] = jnp.swapaxes(found[at], 0, 1)

    @pl.when(owns)
    def _():
        await_arrivals(parcels.at[pl.ds(0, 16 * (BANDS - 1))], send_sem)


def rotate(gram, share):
    return pl.pallas_call(
        rotate_kernel,
        out_shape=jax.ShapeDtypeStruct((8, 6, 8, 128), jnp.float32),
        in_specs=[pl.BlockSpec(memory_space=pltpu.VMEM)] * 2,
        out_specs=pl.BlockSpec(memory_space=pltpu.VMEM),
        scratch_shapes=[
            pltpu.VMEM((FULL, FULL), jnp.bfloat16),
            pltpu.VMEM((16, 128), jnp.float32),
            pltpu.VMEM((16, 16, 128), jnp.float32),
            pltpu.VMEM((16, 128), jnp.float32),
            pltpu.VMEM((BANDS * 16, 128), jnp.bfloat16),
            pltpu.VMEM((OWNERS * 16, 128), jnp.bfloat16),
            pltpu.SemaphoreType.DMA,
            pltpu.SemaphoreType.DMA,
            pltpu.SemaphoreType.DMA,
        ],
        compiler_params=pltpu.CompilerParams(collective_id=2, has_side_effects=True),
        name="rotation_exchange",
    )(gram, share)


def body(orbitals, potential):
    local_count = orbitals.shape[0]
    spots = orbitals.shape[1] * orbitals.shape[2] * orbitals.shape[3]
    total_cells = spots * lax.axis_size("gx") * lax.axis_size("gy")
    gram, share = gather_gram(orbitals, potential, float(total_cells))
    rotated = rotate(gram, share)
    gram_rows = lax.dynamic_slice_in_dim(gram, lax.axis_index("band") * local_count, local_count, 0)
    return (rotated, gram_rows)


def solution(mesh):
    return jax.shard_map(
        body,
        mesh=mesh,
        in_specs=(P("band", "gx", "gy", None), P("gx", "gy", None)),
        out_specs=(P("band", "gx", "gy", None), P("band", None)),
        check_vma=False,
    )
```

```python
import functools

import jax
import jax.numpy as jnp
from jax import lax
from jax.experimental import pallas as pl
from jax.experimental.pallas import tpu as pltpu
from jax.sharding import PartitionSpec as P

stencil_coeffs = (
    -5369.0 / 1800.0,
    12.0 / 7.0,
    -15.0 / 56.0,
    10.0 / 189.0,
    -1.0 / 112.0,
    2.0 / 1925.0,
    -1.0 / 16632.0,
)
spacing = 0.5
low_edge = 5.0
high_edge = 46.0
bottom_edge = -6.5


def filter_scalars():
    half = (high_edge - low_edge) / 2.0
    center = (high_edge + low_edge) / 2.0
    sigma = half / (bottom_edge - center)
    sigma_two = 1.0 / (2.0 / sigma - sigma)
    return (half, center, sigma, sigma_two)


MESH = pl.DeviceIdType.MESH
BANDS = 32
OWNERS = 24
LAYERS = 16
SENDERS = 12
PLANE = 32
GRID_X = 8
GRID_Y = 4
FULL = 256


def owner_band(share):
    return (share // 3) * 4 + share % 3


def band_share(band):
    return (band // 4) * 3 + band % 4


def far_first(step, count):
    reach = (step + 1) // 2
    return count // 2 + reach * (2 * (step % 2) - 1)


def band_partner(band, step):
    side = (band // LAYERS + 1 + step) % 2
    return side * LAYERS + (band % LAYERS + far_first(step // 2, LAYERS)) % LAYERS


def layer_partner(band, step):
    return (band // LAYERS) * LAYERS + (band % LAYERS + far_first(step, LAYERS)) % LAYERS


def plane_partner(place, step):
    across = (place // GRID_Y + far_first(step // GRID_Y, GRID_X)) % GRID_X
    return across * GRID_Y + (place + far_first(step % GRID_Y, GRID_Y)) % GRID_Y


def plane_device(place, layer):
    row = place % GRID_Y
    return {"band": (row // 2) * LAYERS + layer, "gx": place // GRID_Y, "gy": row % 2}


def await_arrivals(buffer, sem):
    pltpu.make_async_copy(buffer, buffer, sem).wait()


def kinetic(wide, other, at):
    own = wide[6 + at]
    around = other[at]
    column = jnp.concatenate([around, own, around], axis=0)
    total = 3.0 * stencil_coeffs[0] * own
    for m in range(1, 7):
        near = wide[6 + at + m] + wide[6 + at - m]
        near = near + (column[8 + m : 16 + m] + column[8 - m : 16 - m])
        near = near + (pltpu.roll(own, m, 2) + pltpu.roll(own, 128 - m, 2))
        total = total + stencil_coeffs[m] * near
    return own, -0.5 / spacing**2 * total


def gram_kernel(
    cells,
    orbitals_ref,
    potential_ref,
    gram_ref,
    share_ref,
    mine_ref,
    outgoing,
    halos,
    base,
    slope,
    other_side,
    shares,
    partial,
    pieces,
    piece,
    layers,
    total,
    blocks,
    halo_send,
    halo_recv,
    send_sem,
    recv_sem,
    local_sem,
):
    band = lax.axis_index("band")
    layer = band % LAYERS
    place = lax.axis_index("gx") * GRID_Y + (band // LAYERS) * 2 + lax.axis_index("gy")
    owns = band % 4 != 3

    barrier = pltpu.get_barrier_semaphore()

    def greet(device):
        pl.semaphore_signal(barrier, 1, device_id=device, device_id_type=MESH)

    def greet_band(step, carry):
        greet({"band": band_partner(band, step)})
        return carry

    def greet_plane(step, carry):
        other = plane_partner(place, step)
        alike = (other // GRID_Y == lax.axis_index("gx")) & (other % 2 == lax.axis_index("gy"))

        @pl.when(jnp.logical_not(alike))
        def _():
            greet(plane_device(other, layer))

        return carry

    lax.fori_loop(0, BANDS - 1, greet_band, 0)
    lax.fori_loop(0, PLANE - 1, greet_plane, 0)

    def turn(at, carry):
        plane = jnp.swapaxes(orbitals_ref[:, at], 0, 1)
        base[6 + at] = plane
        rows_at = pl.ds(pl.multiple_of(at * 64, 64), 64)
        outgoing[0, rows_at] = plane.reshape(64, 128).astype(jnp.bfloat16)
        return carry

    lax.fori_loop(0, 6, turn, 0)
    pl.semaphore_wait(barrier, BANDS - 1 + PLANE - 2)

    place_x, place_y = lax.axis_index("gx"), lax.axis_index("gy")
    sides = (
        {"gx": (place_x + 1) % 8},
        {"gx": (place_x + 7) % 8},
        {"gy": 1 - place_y},
    )

    def halo_copy(turn_at, side):
        return pltpu.make_async_remote_copy(
            src_ref=outgoing.at[turn_at],
            dst_ref=halos.at[turn_at, side],
            send_sem=halo_send.at[turn_at, side],
            recv_sem=halo_recv.at[turn_at, side],
            device_id=sides[side],
            device_id_type=MESH,
        )

    def halo_take(turn_at, wide):
        for side in range(3):
            halo_copy(turn_at, side).wait_recv()

        def widen(at, carry):
            rows_at = pl.ds(pl.multiple_of(at * 64, 64), 64)
            for side, target, offset in ((0, wide, 0), (1, wide, 12), (2, other_side, 0)):
                block = halos[turn_at, side, rows_at]
                target[at + offset] = block.astype(jnp.float32).reshape(8, 8, 128)
            return carry

        lax.fori_loop(0, 6, widen, 0)

    half, center, sigma, sigma_two = filter_scalars()
    for side in (2, 0, 1):
        halo_copy(0, side).start()
    halo_take(0, base)

    def first_step(at, carry):
        own, moved = kinetic(base, other_side, at)
        shifted = (potential_ref[at] - center)[:, None, :]
        result = sigma / half * (moved + shifted * own)
        slope[6 + at] = result
        rows_at = pl.ds(pl.multiple_of(at * 64, 64), 64)
        outgoing[1, rows_at] = result.reshape(64, 128).astype(jnp.bfloat16)
        return carry

    lax.fori_loop(0, 6, first_step, 0)
    for side in (2, 0, 1):
        halo_copy(1, side).start()
    halo_take(1, slope)

    def second_step(at, carry):
        own, moved = kinetic(slope, other_side, at)
        shifted = (potential_ref[at] - center)[:, None, :]
        result = 2.0 * sigma_two / half * (moved + shifted * own) - sigma * sigma_two * base[6 + at]
        rows_at = pl.ds(pl.multiple_of(at * 64, 64), 64)
        mine_ref[rows_at] = result.reshape(64, 128).astype(jnp.bfloat16)
        return carry

    lax.fori_loop(0, 6, second_step, 0)

    def remote(source, target, phase, device):
        return pltpu.make_async_remote_copy(
            src_ref=source,
            dst_ref=target,
            send_sem=send_sem.at[phase],
            recv_sem=recv_sem.at[phase],
            device_id=device,
            device_id_type=MESH,
        )

    def cell_share(step, carry):
        other = band_partner(band, step)

        @pl.when(other % 4 != 3)
        def _():
            at = pl.multiple_of(band_share(other) * 16, 16)
            to = pl.multiple_of(band * 16, 16)
            remote(
                mine_ref.at[pl.ds(at, 16)], shares.at[pl.ds(to, 16)], 0, {"band": other}
            ).start()

        return carry

    lax.fori_loop(0, BANDS - 1, cell_share, 0)

    @pl.when(owns)
    def _():
        at = pl.multiple_of(band_share(band) * 16, 16)
        to = pl.multiple_of(band * 16, 16)
        own = pltpu.make_async_copy(
            mine_ref.at[pl.ds(at, 16)], shares.at[pl.ds(to, 16)], local_sem
        )
        own.start()
        own.wait()
        await_arrivals(shares.at[pl.ds(0, 16 * (BANDS - 1))], recv_sem.at[0])
        spread = shares[...].astype(jnp.float32).reshape(BANDS, 2, 8, 128)
        halves = [spread[:, half].reshape(FULL, 128) for half in range(2)]
        both = jnp.concatenate(halves, axis=1).astype(jnp.bfloat16)
        share_ref[...] = both
        local = lax.dot_general(
            both, both, (((1,), (1,)), ((), ())), preferred_element_type=jnp.float32
        )
        sides = [local[:, 128 * h : 128 * h + 128].reshape(PLANE, 1, 8, 128) for h in range(2)]
        partial[...] = (
            jnp.concatenate(sides, axis=1).reshape(PLANE, 16, 128).astype(jnp.bfloat16)
        )

        def send_piece(step, carry):
            other = plane_partner(place, step)
            remote(
                partial.at[other], pieces.at[place], 1, plane_device(other, layer)
            ).start()
            return carry

        lax.fori_loop(0, PLANE - 1, send_piece, 0)
        pieces[place] = partial[place]
        await_arrivals(pieces.at[pl.ds(0, PLANE - 1)], recv_sem.at[1])
        piece[...] = jnp.sum(pieces[...].astype(jnp.float32), axis=0).astype(jnp.bfloat16)
        at_layer = band_share(layer)

        def send_layer(step, carry):
            remote(
                piece, layers.at[at_layer], 2, {"band": layer_partner(band, step)}
            ).start()
            return carry

        lax.fori_loop(0, LAYERS - 1, send_layer, 0)
        layers[at_layer] = piece[...]
        await_arrivals(layers.at[pl.ds(0, SENDERS - 1)], recv_sem.at[2])

    @pl.when(jnp.logical_not(owns))
    def _():
        share_ref[...] = jnp.zeros_like(share_ref)
        await_arrivals(layers, recv_sem.at[2])

    total[...] = jnp.sum(layers[...].astype(jnp.float32), axis=0) / cells

    def send_total(step, carry):
        other = plane_partner(place, step)
        remote(total, blocks.at[place], 3, plane_device(other, layer)).start()
        return carry

    lax.fori_loop(0, PLANE - 1, send_total, 0)
    blocks[place] = total[...]
    await_arrivals(blocks.at[pl.ds(0, PLANE - 1)], recv_sem.at[3])
    found = blocks[...]
    gram_ref[:, :128] = found[:, :8].reshape(FULL, 128)
    gram_ref[:, 128:] = found[:, 8:].reshape(FULL, 128)

    @pl.when(owns)
    def _():
        await_arrivals(mine_ref.at[pl.ds(0, 16 * (OWNERS - 1))], send_sem.at[0])
        await_arrivals(pieces.at[pl.ds(0, PLANE - 1)], send_sem.at[1])
        await_arrivals(pieces.at[pl.ds(0, LAYERS - 1)], send_sem.at[2])

    @pl.when(jnp.logical_not(owns))
    def _():
        await_arrivals(mine_ref, send_sem.at[0])

    for turn_at in range(2):
        for side in range(3):
            halo_copy(turn_at, side).wait_send()
    await_arrivals(blocks.at[pl.ds(0, PLANE - 1)], send_sem.at[3])


def gather_gram(orbitals, potential, cells):
    return pl.pallas_call(
        functools.partial(gram_kernel, cells),
        out_shape=(
            jax.ShapeDtypeStruct((FULL, FULL), jnp.float32),
            jax.ShapeDtypeStruct((FULL, FULL), jnp.bfloat16),
        ),
        in_specs=[pl.BlockSpec(memory_space=pltpu.VMEM)] * 2,
        out_specs=(pl.BlockSpec(memory_space=pltpu.VMEM),) * 2,
        scratch_shapes=[
            pltpu.VMEM((384, 128), jnp.bfloat16),
            pltpu.VMEM((2, 384, 128), jnp.bfloat16),
            pltpu.VMEM((2, 3, 384, 128), jnp.bfloat16),
            pltpu.VMEM((18, 8, 8, 128), jnp.float32),
            pltpu.VMEM((18, 8, 8, 128), jnp.float32),
            pltpu.VMEM((6, 8, 8, 128), jnp.float32),
            pltpu.VMEM((BANDS * 16, 128), jnp.bfloat16),
            pltpu.VMEM((PLANE, 16, 128), jnp.bfloat16),
            pltpu.VMEM((PLANE, 16, 128), jnp.bfloat16),
            pltpu.VMEM((16, 128), jnp.bfloat16),
            pltpu.VMEM((SENDERS, 16, 128), jnp.bfloat16),
            pltpu.VMEM((16, 128), jnp.float32),
            pltpu.VMEM((PLANE, 16, 128), jnp.float32),
            pltpu.SemaphoreType.DMA((2, 3)),
            pltpu.SemaphoreType.DMA((2, 3)),
            pltpu.SemaphoreType.DMA((4,)),
            pltpu.SemaphoreType.DMA((4,)),
            pltpu.SemaphoreType.DMA,
        ],
        compiler_params=pltpu.CompilerParams(collective_id=1, has_side_effects=True),
        name="gram_exchange",
    )(orbitals, potential)


def split_parts(value):
    high = value.astype(jnp.bfloat16)
    rest = value - high.astype(jnp.float32)
    middle = rest.astype(jnp.bfloat16)
    return high, middle, (rest - middle.astype(jnp.float32)).astype(jnp.bfloat16)


def inverse_factor(matrix, rows_buf, cols_buf, panel_buf):
    size = matrix.shape[1]
    width = panel_buf.shape[0]
    lane = lax.broadcasted_iota(jnp.int32, (1, size), 1)
    done = []
    for begin in range(0, size, width):
        end = begin + width
        head = matrix[:width]
        rows_buf[...] = head
        for j in range(width):
            cols_buf[j] = jnp.broadcast_to(head[:, begin + j : begin + j + 1], (width, size))
        entry = {}
        for j in range(width):
            for i in range(j, width):
                entry[i, j] = cols_buf[j, i : i + 1, :]
        inside = (lane >= begin) & (lane < end)
        row = [
            jnp.where(inside, (lane == begin + i).astype(jnp.float32), rows_buf[i : i + 1, :])
            for i in range(width)
        ]
        for p in range(width):
            scale = lax.rsqrt(entry[p, p])
            for i in range(p + 1, width):
                entry[i, p] = entry[i, p] * scale
            lead = row[p] * scale
            for i in range(p + 1, width):
                for j in range(p + 1, i + 1):
                    entry[i, j] = entry[i, j] - entry[i, p] * entry[j, p]
                row[i] = row[i] - entry[i, p] * lead
            panel_buf[p : p + 1, :] = lead
        panel = panel_buf[...]
        done.append(jnp.where(jnp.broadcast_to(lane < end, (width, size)), panel, 0.0))
        if end < size:
            high, middle, low = split_parts(panel)
            update = lax.dot_general(
                jnp.concatenate([high, high, middle, high, low, middle], axis=0),
                jnp.concatenate([high, middle, high, low, high, middle], axis=0),
                (((0,), (0,)), ((), ())),
                preferred_element_type=jnp.float32,
            )
            rest = jnp.where(jnp.broadcast_to(inside, (size - end, size)), 0.0, matrix[width:])
            matrix = rest - update[end:]
    return jnp.concatenate(done, axis=0)


def full_dot(left, right, left_dim, right_dim):
    return lax.dot_general(
        left,
        right,
        (((left_dim,), (right_dim,)), ((), ())),
        preferred_element_type=jnp.float32,
        precision=lax.Precision.HIGHEST,
    )


def fill_inverse(gram_ref, inverse_ref, buffers):
    upper = inverse_factor(gram_ref[:128, :128], *buffers)
    lower_left = full_dot(gram_ref[128:, :128], upper, 1, 1)
    remaining = gram_ref[128:, 128:] - full_dot(lower_left, lower_left, 1, 1)
    carried = full_dot(lower_left, upper, 1, 0)
    lower = inverse_factor(remaining, *buffers)
    inverse_ref[:128, :128] = upper.astype(jnp.bfloat16)
    inverse_ref[:128, 128:] = jnp.zeros((128, 128), jnp.bfloat16)
    inverse_ref[128:, 128:] = lower.astype(jnp.bfloat16)
    inverse_ref[128:, :128] = (-full_dot(lower, carried, 1, 0)).astype(jnp.bfloat16)


def rotate_kernel(
    gram_ref,
    share_ref,
    out_ref,
    inverse,
    rows_buf,
    cols_buf,
    panel_buf,
    parcels,
    arrived,
    send_sem,
    recv_sem,
    local_sem,
):
    band = lax.axis_index("band")
    owns = band % 4 != 3
    barrier = pltpu.get_barrier_semaphore()

    def greet_band(step, carry):
        pl.semaphore_signal(
            barrier, 1, device_id={"band": band_partner(band, step)}, device_id_type=MESH
        )
        return carry

    lax.fori_loop(0, BANDS - 1, greet_band, 0)

    @pl.when(owns)
    def _():
        fill_inverse(gram_ref, inverse, (rows_buf, cols_buf, panel_buf))
        turned = lax.dot_general(
            inverse[...],
            share_ref[...],
            (((1,), (0,)), ((), ())),
            preferred_element_type=jnp.float32,
        )
        halves = [turned[:, 128 * h : 128 * h + 128].reshape(BANDS, 1, 8, 128) for h in range(2)]
        parcels[...] = (
            jnp.concatenate(halves, axis=1).reshape(BANDS * 16, 128).astype(jnp.bfloat16)
        )

    pl.semaphore_wait(barrier, BANDS - 1)

    @pl.when(owns)
    def _():
        to = pl.multiple_of(band_share(band) * 16, 16)

        def send_parcel(step, carry):
            other = band_partner(band, step)
            at = pl.multiple_of(other * 16, 16)
            pltpu.make_async_remote_copy(
                src_ref=parcels.at[pl.ds(at, 16)],
                dst_ref=arrived.at[pl.ds(to, 16)],
                send_sem=send_sem,
                recv_sem=recv_sem,
                device_id={"band": other},
                device_id_type=MESH,
            ).start()
            return carry

        lax.fori_loop(0, BANDS - 1, send_parcel, 0)
        at = pl.multiple_of(band * 16, 16)
        own = pltpu.make_async_copy(
            parcels.at[pl.ds(at, 16)], arrived.at[pl.ds(to, 16)], local_sem
        )
        own.start()
        own.wait()
        await_arrivals(arrived.at[pl.ds(0, 16 * (OWNERS - 1))], recv_sem)

    @pl.when(jnp.logical_not(owns))
    def _():
        await_arrivals(arrived, recv_sem)

    found = arrived[...].astype(jnp.float32).reshape(6, 8, 8, 128)
    for at in range(6):
        out_ref[:, at] = jnp.swapaxes(found[at], 0, 1)

    @pl.when(owns)
    def _():
        await_arrivals(parcels.at[pl.ds(0, 16 * (BANDS - 1))], send_sem)


def rotate(gram, share):
    return pl.pallas_call(
        rotate_kernel,
        out_shape=jax.ShapeDtypeStruct((8, 6, 8, 128), jnp.float32),
        in_specs=[pl.BlockSpec(memory_space=pltpu.VMEM)] * 2,
        out_specs=pl.BlockSpec(memory_space=pltpu.VMEM),
        scratch_shapes=[
            pltpu.VMEM((FULL, FULL), jnp.bfloat16),
            pltpu.VMEM((16, 128), jnp.float32),
            pltpu.VMEM((16, 16, 128), jnp.float32),
            pltpu.VMEM((16, 128), jnp.float32),
            pltpu.VMEM((BANDS * 16, 128), jnp.bfloat16),
            pltpu.VMEM((OWNERS * 16, 128), jnp.bfloat16),
            pltpu.SemaphoreType.DMA,
            pltpu.SemaphoreType.DMA,
            pltpu.SemaphoreType.DMA,
        ],
        compiler_params=pltpu.CompilerParams(collective_id=2, has_side_effects=True),
        name="rotation_exchange",
    )(gram, share)


def body(orbitals, potential):
    local_count = orbitals.shape[0]
    spots = orbitals.shape[1] * orbitals.shape[2] * orbitals.shape[3]
    total_cells = spots * lax.axis_size("gx") * lax.axis_size("gy")
    gram, share = gather_gram(orbitals, potential, float(total_cells))
    rotated = rotate(gram, share)
    gram_rows = lax.dynamic_slice_in_dim(gram, lax.axis_index("band") * local_count, local_count, 0)
    return (rotated, gram_rows)


def solution(mesh):
    return jax.shard_map(
        body,
        mesh=mesh,
        in_specs=(P("band", "gx", "gy", None), P("gx", "gy", None)),
        out_specs=(P("band", "gx", "gy", None), P("band", None)),
        check_vma=False,
    )
```

```python
import functools

import jax
import jax.numpy as jnp
from jax import lax
from jax.experimental import pallas as pl
from jax.experimental.pallas import tpu as pltpu
from jax.sharding import PartitionSpec as P

stencil_coeffs = (
    -5369.0 / 1800.0,
    12.0 / 7.0,
    -15.0 / 56.0,
    10.0 / 189.0,
    -1.0 / 112.0,
    2.0 / 1925.0,
    -1.0 / 16632.0,
)
spacing = 0.5
low_edge = 5.0
high_edge = 46.0
bottom_edge = -6.5


def filter_scalars():
    half = (high_edge - low_edge) / 2.0
    center = (high_edge + low_edge) / 2.0
    sigma = half / (bottom_edge - center)
    sigma_two = 1.0 / (2.0 / sigma - sigma)
    return (half, center, sigma, sigma_two)


MESH = pl.DeviceIdType.MESH
BANDS = 32
OWNERS = 24
LAYERS = 16
SENDERS = 12
PLANE = 32
GRID_X = 8
GRID_Y = 4
FULL = 256


def owner_band(share):
    return (share // 3) * 4 + share % 3


def band_share(band):
    return (band // 4) * 3 + band % 4


def far_first(step, count):
    reach = (step + 1) // 2
    return count // 2 + reach * (2 * (step % 2) - 1)


def band_partner(band, step):
    side = (band // LAYERS + 1 + step) % 2
    return side * LAYERS + (band % LAYERS + far_first(step // 2, LAYERS)) % LAYERS


def layer_partner(band, step):
    return (band // LAYERS) * LAYERS + (band % LAYERS + far_first(step, LAYERS)) % LAYERS


def plane_partner(place, step):
    across = (place // GRID_Y + far_first(step // GRID_Y, GRID_X)) % GRID_X
    return across * GRID_Y + (place + far_first(step % GRID_Y, GRID_Y)) % GRID_Y


def plane_device(place, layer):
    row = place % GRID_Y
    return {"band": (row // 2) * LAYERS + layer, "gx": place // GRID_Y, "gy": row % 2}


def await_arrivals(buffer, sem):
    pltpu.make_async_copy(buffer, buffer, sem).wait()


def split_parts(value):
    high = value.astype(jnp.bfloat16)
    rest = value - high.astype(jnp.float32)
    middle = rest.astype(jnp.bfloat16)
    return high, middle, (rest - middle.astype(jnp.float32)).astype(jnp.bfloat16)


def inverse_factor(matrix, rows_buf, cols_buf, panel_buf):
    size = matrix.shape[1]
    width = panel_buf.shape[0]
    lane = lax.broadcasted_iota(jnp.int32, (1, size), 1)
    done = []
    for begin in range(0, size, width):
        end = begin + width
        head = matrix[:width]
        rows_buf[...] = head
        for j in range(width):
            cols_buf[j] = jnp.broadcast_to(head[:, begin + j : begin + j + 1], (width, size))
        entry = {}
        for j in range(width):
            for i in range(j, width):
                entry[i, j] = cols_buf[j, i : i + 1, :]
        inside = (lane >= begin) & (lane < end)
        row = [
            jnp.where(inside, (lane == begin + i).astype(jnp.float32), rows_buf[i : i + 1, :])
            for i in range(width)
        ]
        for p in range(width):
            scale = lax.rsqrt(entry[p, p])
            for i in range(p + 1, width):
                entry[i, p] = entry[i, p] * scale
            lead = row[p] * scale
            for i in range(p + 1, width):
                for j in range(p + 1, i + 1):
                    entry[i, j] = entry[i, j] - entry[i, p] * entry[j, p]
                row[i] = row[i] - entry[i, p] * lead
            panel_buf[p : p + 1, :] = lead
        panel = panel_buf[...]
        done.append(jnp.where(jnp.broadcast_to(lane < end, (width, size)), panel, 0.0))
        if end < size:
            high, middle, low = split_parts(panel)
            update = lax.dot_general(
                jnp.concatenate([high, high, middle, high, low, middle], axis=0),
                jnp.concatenate([high, middle, high, low, high, middle], axis=0),
                (((0,), (0,)), ((), ())),
                preferred_element_type=jnp.float32,
            )
            rest = jnp.where(jnp.broadcast_to(inside, (size - end, size)), 0.0, matrix[width:])
            matrix = rest - update[end:]
    return jnp.concatenate(done, axis=0)


def full_dot(left, right, left_dim, right_dim):
    return lax.dot_general(
        left,
        right,
        (((left_dim,), (right_dim,)), ((), ())),
        preferred_element_type=jnp.float32,
        precision=lax.Precision.HIGHEST,
    )


def kinetic(wide, other, at):
    own = wide[6 + at]
    around = other[at]
    column = jnp.concatenate([around, own, around], axis=0)
    total = 3.0 * stencil_coeffs[0] * own
    for m in range(1, 7):
        near = wide[6 + at + m] + wide[6 + at - m]
        near = near + (column[8 + m : 16 + m] + column[8 - m : 16 - m])
        near = near + (pltpu.roll(own, m, 2) + pltpu.roll(own, 128 - m, 2))
        total = total + stencil_coeffs[m] * near
    return own, -0.5 / spacing**2 * total


def filter_rotate_kernel(
    cells,
    orbitals_ref,
    potential_ref,
    rotated_ref,
    gram_ref,
    gram,
    share,
    inverse,
    rows_buf,
    cols_buf,
    panel_buf,
    parcels,
    arrived,
    mine_ref,
    outgoing,
    halos,
    base,
    slope,
    other_side,
    shares,
    partial,
    pieces,
    piece,
    layers,
    total,
    blocks,
    halo_send,
    halo_recv,
    send_sem,
    recv_sem,
    local_sem,
):
    band = lax.axis_index("band")
    layer = band % LAYERS
    place = lax.axis_index("gx") * GRID_Y + (band // LAYERS) * 2 + lax.axis_index("gy")
    owns = band % 4 != 3

    barrier = pltpu.get_barrier_semaphore()

    def greet(device):
        pl.semaphore_signal(barrier, 1, device_id=device, device_id_type=MESH)

    def greet_band(step, carry):
        greet({"band": band_partner(band, step)})
        return carry

    def greet_plane(step, carry):
        other = plane_partner(place, step)
        alike = (other // GRID_Y == lax.axis_index("gx")) & (other % 2 == lax.axis_index("gy"))

        @pl.when(jnp.logical_not(alike))
        def _():
            greet(plane_device(other, layer))

        return carry

    lax.fori_loop(0, BANDS - 1, greet_band, 0)
    lax.fori_loop(0, PLANE - 1, greet_plane, 0)

    def turn(at, carry):
        plane = jnp.swapaxes(orbitals_ref[:, at], 0, 1)
        base[6 + at] = plane
        rows_at = pl.ds(pl.multiple_of(at * 64, 64), 64)
        outgoing[0, rows_at] = plane.reshape(64, 128).astype(jnp.bfloat16)
        return carry

    lax.fori_loop(0, 6, turn, 0)
    pl.semaphore_wait(barrier, BANDS - 1 + PLANE - 2)

    place_x, place_y = lax.axis_index("gx"), lax.axis_index("gy")
    sides = (
        {"gx": (place_x + 1) % 8},
        {"gx": (place_x + 7) % 8},
        {"gy": 1 - place_y},
    )

    def halo_copy(turn_at, side):
        return pltpu.make_async_remote_copy(
            src_ref=outgoing.at[turn_at],
            dst_ref=halos.at[turn_at, side],
            send_sem=halo_send.at[turn_at, side],
            recv_sem=halo_recv.at[turn_at, side],
            device_id=sides[side],
            device_id_type=MESH,
        )

    def halo_take(turn_at, wide):
        for side in range(3):
            halo_copy(turn_at, side).wait_recv()

        def widen(at, carry):
            rows_at = pl.ds(pl.multiple_of(at * 64, 64), 64)
            for side, target, offset in ((0, wide, 0), (1, wide, 12), (2, other_side, 0)):
                block = halos[turn_at, side, rows_at]
                target[at + offset] = block.astype(jnp.float32).reshape(8, 8, 128)
            return carry

        lax.fori_loop(0, 6, widen, 0)

    half, center, sigma, sigma_two = filter_scalars()
    for side in (2, 0, 1):
        halo_copy(0, side).start()
    halo_take(0, base)

    def first_step(at, carry):
        own, moved = kinetic(base, other_side, at)
        shifted = (potential_ref[at] - center)[:, None, :]
        result = sigma / half * (moved + shifted * own)
        slope[6 + at] = result
        rows_at = pl.ds(pl.multiple_of(at * 64, 64), 64)
        outgoing[1, rows_at] = result.reshape(64, 128).astype(jnp.bfloat16)
        return carry

    lax.fori_loop(0, 6, first_step, 0)
    for side in (2, 0, 1):
        halo_copy(1, side).start()
    halo_take(1, slope)

    def second_step(at, carry):
        own, moved = kinetic(slope, other_side, at)
        shifted = (potential_ref[at] - center)[:, None, :]
        result = 2.0 * sigma_two / half * (moved + shifted * own) - sigma * sigma_two * base[6 + at]
        rows_at = pl.ds(pl.multiple_of(at * 64, 64), 64)
        mine_ref[rows_at] = result.reshape(64, 128).astype(jnp.bfloat16)
        return carry

    lax.fori_loop(0, 6, second_step, 0)

    def remote(source, target, phase, device):
        return pltpu.make_async_remote_copy(
            src_ref=source,
            dst_ref=target,
            send_sem=send_sem.at[phase],
            recv_sem=recv_sem.at[phase],
            device_id=device,
            device_id_type=MESH,
        )

    def cell_share(step, carry):
        other = band_partner(band, step)

        @pl.when(other % 4 != 3)
        def _():
            at = pl.multiple_of(band_share(other) * 16, 16)
            to = pl.multiple_of(band * 16, 16)
            remote(
                mine_ref.at[pl.ds(at, 16)], shares.at[pl.ds(to, 16)], 0, {"band": other}
            ).start()

        return carry

    lax.fori_loop(0, BANDS - 1, cell_share, 0)

    @pl.when(owns)
    def _():
        at = pl.multiple_of(band_share(band) * 16, 16)
        to = pl.multiple_of(band * 16, 16)
        own = pltpu.make_async_copy(
            mine_ref.at[pl.ds(at, 16)], shares.at[pl.ds(to, 16)], local_sem
        )
        own.start()
        own.wait()
        await_arrivals(shares.at[pl.ds(0, 16 * (BANDS - 1))], recv_sem.at[0])
        spread = shares[...].astype(jnp.float32).reshape(BANDS, 2, 8, 128)
        halves = [spread[:, half].reshape(FULL, 128) for half in range(2)]
        both = jnp.concatenate(halves, axis=1).astype(jnp.bfloat16)
        share[...] = both
        local = lax.dot_general(
            both, both, (((1,), (1,)), ((), ())), preferred_element_type=jnp.float32
        )
        sides = [local[:, 128 * h : 128 * h + 128].reshape(PLANE, 1, 8, 128) for h in range(2)]
        partial[...] = (
            jnp.concatenate(sides, axis=1).reshape(PLANE, 16, 128).astype(jnp.bfloat16)
        )

        def send_piece(step, carry):
            other = plane_partner(place, step)
            remote(
                partial.at[other], pieces.at[place], 1, plane_device(other, layer)
            ).start()
            return carry

        lax.fori_loop(0, PLANE - 1, send_piece, 0)
        pieces[place] = partial[place]
        await_arrivals(pieces.at[pl.ds(0, PLANE - 1)], recv_sem.at[1])
        piece[...] = jnp.sum(pieces[...].astype(jnp.float32), axis=0).astype(jnp.bfloat16)
        at_layer = band_share(layer)

        def send_layer(step, carry):
            remote(
                piece, layers.at[at_layer], 2, {"band": layer_partner(band, step)}
            ).start()
            return carry

        lax.fori_loop(0, LAYERS - 1, send_layer, 0)
        layers[at_layer] = piece[...]
        await_arrivals(layers.at[pl.ds(0, SENDERS - 1)], recv_sem.at[2])

    @pl.when(jnp.logical_not(owns))
    def _():
        await_arrivals(layers, recv_sem.at[2])

    total[...] = jnp.sum(layers[...].astype(jnp.float32), axis=0) / cells

    def send_total(step, carry):
        other = plane_partner(place, step)
        remote(total, blocks.at[place], 3, plane_device(other, layer)).start()
        return carry

    lax.fori_loop(0, PLANE - 1, send_total, 0)
    blocks[place] = total[...]
    await_arrivals(blocks.at[pl.ds(0, PLANE - 1)], recv_sem.at[3])
    found = blocks[...]
    gram[:, :128] = found[:, :8].reshape(FULL, 128)
    gram[:, 128:] = found[:, 8:].reshape(FULL, 128)
    gram_ref[...] = gram[pl.ds(pl.multiple_of(band * 8, 8), 8), :]

    @pl.when(owns)
    def _():
        to = pl.multiple_of(band_share(band) * 16, 16)

        def send_parcels(side, weights, cells_of):
            turned = jnp.dot(weights, cells_of, preferred_element_type=jnp.float32)
            halves = [
                turned[:, 128 * h : 128 * h + 128].reshape(LAYERS, 1, 8, 128) for h in range(2)
            ]
            base_row = side * LAYERS * 16
            parcels[base_row : base_row + LAYERS * 16] = (
                jnp.concatenate(halves, axis=1).reshape(LAYERS * 16, 128).astype(jnp.bfloat16)
            )

            def send_parcel(step, carry):
                other = side * LAYERS + (layer + far_first(step, LAYERS)) % LAYERS
                at = pl.multiple_of(other * 16, 16)

                @pl.when(other != band)
                def _():
                    remote(
                        parcels.at[pl.ds(at, 16)], arrived.at[pl.ds(to, 16)], 4, {"band": other}
                    ).start()

                return carry

            lax.fori_loop(0, LAYERS, send_parcel, 0)

        buffers = (rows_buf, cols_buf, panel_buf)
        upper = inverse_factor(gram[:128, :128], *buffers)
        send_parcels(0, upper.astype(jnp.bfloat16), share[:128])
        lower_left = full_dot(gram[128:, :128], upper, 1, 1)
        remaining = gram[128:, 128:] - full_dot(lower_left, lower_left, 1, 1)
        carried = full_dot(lower_left, upper, 1, 0)
        lower = inverse_factor(remaining, *buffers)
        inverse[:, 128:] = lower.astype(jnp.bfloat16)
        inverse[:, :128] = (-full_dot(lower, carried, 1, 0)).astype(jnp.bfloat16)
        send_parcels(1, inverse[...], share[...])
        at = pl.multiple_of(band * 16, 16)
        own = pltpu.make_async_copy(
            parcels.at[pl.ds(at, 16)], arrived.at[pl.ds(to, 16)], local_sem
        )
        own.start()
        own.wait()
        await_arrivals(arrived.at[pl.ds(0, 16 * (OWNERS - 1))], recv_sem.at[4])

    @pl.when(jnp.logical_not(owns))
    def _():
        await_arrivals(arrived, recv_sem.at[4])

    rotated_ref[...] = arrived[...]

    @pl.when(owns)
    def _():
        await_arrivals(parcels.at[pl.ds(0, 16 * (BANDS - 1))], send_sem.at[4])
        await_arrivals(mine_ref.at[pl.ds(0, 16 * (OWNERS - 1))], send_sem.at[0])
        await_arrivals(pieces.at[pl.ds(0, PLANE - 1)], send_sem.at[1])
        await_arrivals(pieces.at[pl.ds(0, LAYERS - 1)], send_sem.at[2])

    @pl.when(jnp.logical_not(owns))
    def _():
        await_arrivals(mine_ref, send_sem.at[0])

    for turn_at in range(2):
        for side in range(3):
            halo_copy(turn_at, side).wait_send()
    await_arrivals(blocks.at[pl.ds(0, PLANE - 1)], send_sem.at[3])


def filter_rotate(orbitals, potential, cells):
    return pl.pallas_call(
        functools.partial(filter_rotate_kernel, cells),
        out_shape=(
            jax.ShapeDtypeStruct((OWNERS * 16, 128), jnp.bfloat16),
            jax.ShapeDtypeStruct((8, FULL), jnp.float32),
        ),
        in_specs=[pl.BlockSpec(memory_space=pltpu.VMEM)] * 2,
        out_specs=(pl.BlockSpec(memory_space=pltpu.VMEM),) * 2,
        scratch_shapes=[
            pltpu.VMEM((FULL, FULL), jnp.float32),
            pltpu.VMEM((FULL, FULL), jnp.bfloat16),
            pltpu.VMEM((128, FULL), jnp.bfloat16),
            pltpu.VMEM((16, 128), jnp.float32),
            pltpu.VMEM((16, 16, 128), jnp.float32),
            pltpu.VMEM((16, 128), jnp.float32),
            pltpu.VMEM((BANDS * 16, 128), jnp.bfloat16),
            pltpu.VMEM((OWNERS * 16, 128), jnp.bfloat16),
            pltpu.VMEM((384, 128), jnp.bfloat16),
            pltpu.VMEM((2, 384, 128), jnp.bfloat16),
            pltpu.VMEM((2, 3, 384, 128), jnp.bfloat16),
            pltpu.VMEM((18, 8, 8, 128), jnp.float32),
            pltpu.VMEM((18, 8, 8, 128), jnp.float32),
            pltpu.VMEM((6, 8, 8, 128), jnp.float32),
            pltpu.VMEM((BANDS * 16, 128), jnp.bfloat16),
            pltpu.VMEM((PLANE, 16, 128), jnp.bfloat16),
            pltpu.VMEM((PLANE, 16, 128), jnp.bfloat16),
            pltpu.VMEM((16, 128), jnp.bfloat16),
            pltpu.VMEM((SENDERS, 16, 128), jnp.bfloat16),
            pltpu.VMEM((16, 128), jnp.float32),
            pltpu.VMEM((PLANE, 16, 128), jnp.float32),
            pltpu.SemaphoreType.DMA((2, 3)),
            pltpu.SemaphoreType.DMA((2, 3)),
            pltpu.SemaphoreType.DMA((5,)),
            pltpu.SemaphoreType.DMA((5,)),
            pltpu.SemaphoreType.DMA,
        ],
        compiler_params=pltpu.CompilerParams(collective_id=1, has_side_effects=True),
        name="filter_rotate",
    )(orbitals, potential)


def body(orbitals, potential):
    count, size_x, size_y, size_z = orbitals.shape
    total_cells = size_x * size_y * size_z * lax.axis_size("gx") * lax.axis_size("gy")
    tiles, gram_rows = filter_rotate(orbitals, potential, float(total_cells))
    rotated = tiles.astype(jnp.float32).reshape(size_x, size_y, count, size_z).transpose(2, 0, 1, 3)
    return (rotated, gram_rows)


def solution(mesh):
    return jax.shard_map(
        body,
        mesh=mesh,
        in_specs=(P("band", "gx", "gy", None), P("gx", "gy", None)),
        out_specs=(P("band", "gx", "gy", None), P("band", None)),
        check_vma=False,
    )
```

```python
import functools

import jax
import jax.numpy as jnp
from jax import lax
from jax.experimental import pallas as pl
from jax.experimental.pallas import tpu as pltpu
from jax.sharding import PartitionSpec as P

stencil_coeffs = (
    -5369.0 / 1800.0,
    12.0 / 7.0,
    -15.0 / 56.0,
    10.0 / 189.0,
    -1.0 / 112.0,
    2.0 / 1925.0,
    -1.0 / 16632.0,
)
spacing = 0.5
low_edge = 5.0
high_edge = 46.0
bottom_edge = -6.5


def filter_scalars():
    half = (high_edge - low_edge) / 2.0
    center = (high_edge + low_edge) / 2.0
    sigma = half / (bottom_edge - center)
    sigma_two = 1.0 / (2.0 / sigma - sigma)
    return (half, center, sigma, sigma_two)


MESH = pl.DeviceIdType.MESH
BANDS = 32
OWNERS = 24
LAYERS = 16
SENDERS = 12
PLANE = 32
GRID_X = 8
GRID_Y = 4
FULL = 256


def owner_band(share):
    return (share // 3) * 4 + share % 3


def band_share(band):
    return (band // 4) * 3 + band % 4


def far_first(step, count):
    reach = (step + 1) // 2
    return count // 2 + reach * (2 * (step % 2) - 1)


def spot(across, row, layer):
    return {"band": (row // 2) * LAYERS + layer, "gx": across, "gy": row % 2}


def plane_partner(place, step):
    across = (place // GRID_Y + far_first(step // GRID_Y, GRID_X)) % GRID_X
    return across * GRID_Y + (place + far_first(step % GRID_Y, GRID_Y)) % GRID_Y


def await_arrivals(buffer, sem):
    pltpu.make_async_copy(buffer, buffer, sem).wait()


def split_parts(value):
    high = value.astype(jnp.bfloat16)
    rest = value - high.astype(jnp.float32)
    middle = rest.astype(jnp.bfloat16)
    return high, middle, (rest - middle.astype(jnp.float32)).astype(jnp.bfloat16)


def inverse_factor(matrix, rows_buf, cols_buf, panel_buf):
    size = matrix.shape[1]
    width = panel_buf.shape[0]
    lane = lax.broadcasted_iota(jnp.int32, (1, size), 1)
    done = []
    for begin in range(0, size, width):
        end = begin + width
        head = matrix[:width]
        rows_buf[...] = head
        for j in range(width):
            cols_buf[j] = jnp.broadcast_to(head[:, begin + j : begin + j + 1], (width, size))
        entry = {}
        for j in range(width):
            for i in range(j, width):
                entry[i, j] = cols_buf[j, i : i + 1, :]
        inside = (lane >= begin) & (lane < end)
        row = [
            jnp.where(inside, (lane == begin + i).astype(jnp.float32), rows_buf[i : i + 1, :])
            for i in range(width)
        ]
        for p in range(width):
            scale = lax.rsqrt(entry[p, p])
            for i in range(p + 1, width):
                entry[i, p] = entry[i, p] * scale
            lead = row[p] * scale
            for i in range(p + 1, width):
                for j in range(p + 1, i + 1):
                    entry[i, j] = entry[i, j] - entry[i, p] * entry[j, p]
                row[i] = row[i] - entry[i, p] * lead
            panel_buf[p : p + 1, :] = lead
        panel = panel_buf[...]
        done.append(jnp.where(jnp.broadcast_to(lane < end, (width, size)), panel, 0.0))
        if end < size:
            high, middle, low = split_parts(panel)
            update = lax.dot_general(
                jnp.concatenate([high, high, middle, high, low, middle], axis=0),
                jnp.concatenate([high, middle, high, low, high, middle], axis=0),
                (((0,), (0,)), ((), ())),
                preferred_element_type=jnp.float32,
            )
            rest = jnp.where(jnp.broadcast_to(inside, (size - end, size)), 0.0, matrix[width:])
            matrix = rest - update[end:]
    return jnp.concatenate(done, axis=0)


def full_dot(left, right, left_dim, right_dim):
    return lax.dot_general(
        left,
        right,
        (((left_dim,), (right_dim,)), ((), ())),
        preferred_element_type=jnp.float32,
        precision=lax.Precision.HIGHEST,
    )


def kinetic(wide, other, at):
    own = wide[6 + at]
    around = other[at]
    column = jnp.concatenate([around, own, around], axis=0)
    total = 3.0 * stencil_coeffs[0] * own
    for m in range(1, 7):
        near = wide[6 + at + m] + wide[6 + at - m]
        near = near + (column[8 + m : 16 + m] + column[8 - m : 16 - m])
        near = near + (pltpu.roll(own, m, 2) + pltpu.roll(own, 128 - m, 2))
        total = total + stencil_coeffs[m] * near
    return own, -0.5 / spacing**2 * total


def filter_rotate_kernel(
    cells,
    orbitals_ref,
    potential_ref,
    rotated_ref,
    gram_ref,
    gram,
    share,
    inverse,
    rows_buf,
    cols_buf,
    panel_buf,
    parcels,
    arrived,
    mine_ref,
    outgoing,
    halos,
    base,
    slope,
    other_side,
    shares,
    partial,
    pieces,
    piece,
    layers,
    total,
    blocks,
    halo_send,
    halo_recv,
    send_sem,
    recv_sem,
    tokens,
):
    band = lax.axis_index("band")
    layer = band % LAYERS
    across = lax.axis_index("gx")
    half_y = lax.axis_index("gy")
    row = (band // LAYERS) * 2 + half_y
    place = across * GRID_Y + row
    owns = band % 4 != 3

    def near(step_x, step_y, step_z):
        return spot(
            (across + step_x) % GRID_X, (row + step_y) % GRID_Y, (layer + step_z) % LAYERS
        )

    barrier = pltpu.get_barrier_semaphore()
    greeted = [near(0, 0, step) for step in (3, -3, 2, -2, 1, -1)]
    greeted += [near(0, side, step) for step in (2, -2, 1, -1, 0) for side in (1, 3)]
    greeted += [near(1, 0, 0), near(-1, 0, 0)]
    for device in greeted:
        pl.semaphore_signal(barrier, 1, device_id=device, device_id_type=MESH)

    def send_tokens(kind, devices):
        for device in devices:
            pl.semaphore_signal(tokens.at[kind], 1, device_id=device, device_id_type=MESH)

    def turn(at, carry):
        plane = jnp.swapaxes(orbitals_ref[:, at], 0, 1)
        base[6 + at] = plane
        rows_at = pl.ds(pl.multiple_of(at * 64, 64), 64)
        outgoing[0, rows_at] = plane.reshape(64, 128).astype(jnp.bfloat16)
        return carry

    lax.fori_loop(0, 6, turn, 0)
    pl.semaphore_wait(barrier, len(greeted))
    send_tokens(0, (near(0, 0, 3), near(0, 0, -3)))

    sides = (near(1, 0, 0), near(-1, 0, 0), {"gy": 1 - half_y})

    def halo_copy(turn_at, side):
        return pltpu.make_async_remote_copy(
            src_ref=outgoing.at[turn_at],
            dst_ref=halos.at[turn_at, side],
            send_sem=halo_send.at[turn_at, side],
            recv_sem=halo_recv.at[turn_at, side],
            device_id=sides[side],
            device_id_type=MESH,
        )

    def halo_take(turn_at, wide):
        for side in range(3):
            halo_copy(turn_at, side).wait_recv()

        def widen(at, carry):
            rows_at = pl.ds(pl.multiple_of(at * 64, 64), 64)
            for side, target, offset in ((0, wide, 0), (1, wide, 12), (2, other_side, 0)):
                block = halos[turn_at, side, rows_at]
                target[at + offset] = block.astype(jnp.float32).reshape(8, 8, 128)
            return carry

        lax.fori_loop(0, 6, widen, 0)

    half, center, sigma, sigma_two = filter_scalars()
    for side in (2, 0, 1):
        halo_copy(0, side).start()
    halo_take(0, base)
    pl.semaphore_wait(tokens.at[0], 2)
    send_tokens(1, (near(0, 0, 5), near(0, 0, -5)))

    def first_step(at, carry):
        own, moved = kinetic(base, other_side, at)
        shifted = (potential_ref[at] - center)[:, None, :]
        result = sigma / half * (moved + shifted * own)
        slope[6 + at] = result
        rows_at = pl.ds(pl.multiple_of(at * 64, 64), 64)
        outgoing[1, rows_at] = result.reshape(64, 128).astype(jnp.bfloat16)
        return carry

    lax.fori_loop(0, 6, first_step, 0)
    for side in (2, 0, 1):
        halo_copy(1, side).start()
    halo_take(1, slope)
    send_tokens(2, (near(3, 0, 0), near(-3, 0, 0)))

    def second_step(at, carry):
        own, moved = kinetic(slope, other_side, at)
        shifted = (potential_ref[at] - center)[:, None, :]
        result = 2.0 * sigma_two / half * (moved + shifted * own) - sigma * sigma_two * base[6 + at]
        rows_at = pl.ds(pl.multiple_of(at * 64, 64), 64)
        mine_ref[rows_at] = result.reshape(64, 128).astype(jnp.bfloat16)
        return carry

    lax.fori_loop(0, 6, second_step, 0)

    def remote(source, target, phase, device):
        return pltpu.make_async_remote_copy(
            src_ref=source,
            dst_ref=target,
            send_sem=send_sem.at[phase],
            recv_sem=recv_sem.at[phase],
            device_id=device,
            device_id_type=MESH,
        )

    def cell_share(step, carry):
        to_row = (row + 1 + 2 * (step % 2)) % GRID_Y
        to_layer = (layer + far_first(step // 2, LAYERS)) % LAYERS
        other = (to_row // 2) * LAYERS + to_layer

        @pl.when(other % 4 != 3)
        def _():
            at = pl.multiple_of(band_share(other) * 16, 16)
            to = pl.multiple_of(band * 16, 16)
            remote(
                mine_ref.at[pl.ds(at, 16)],
                shares.at[pl.ds(to, 16)],
                0,
                {"band": other, "gy": 1 - half_y},
            ).start()

        return carry

    pl.semaphore_wait(tokens.at[1], 2)
    lax.fori_loop(0, BANDS, cell_share, 0)
    pl.semaphore_wait(tokens.at[2], 2)

    @pl.when(owns)
    def _():
        await_arrivals(shares, recv_sem.at[0])
        spread = shares[...].astype(jnp.float32).reshape(BANDS, 2, 8, 128)
        halves = [spread[:, half].reshape(FULL, 128) for half in range(2)]
        both = jnp.concatenate(halves, axis=1).astype(jnp.bfloat16)
        share[...] = both
        local = lax.dot_general(
            both, both, (((1,), (1,)), ((), ())), preferred_element_type=jnp.float32
        )
        sides = [local[:, 128 * h : 128 * h + 128].reshape(PLANE, 1, 8, 128) for h in range(2)]
        partial[...] = (
            jnp.concatenate(sides, axis=1).reshape(PLANE, 16, 128).astype(jnp.bfloat16)
        )

        def send_piece(step, carry):
            other = plane_partner(place, step)
            remote(
                partial.at[other],
                pieces.at[place],
                1,
                spot(other // GRID_Y, other % GRID_Y, layer),
            ).start()
            return carry

        lax.fori_loop(0, PLANE - 1, send_piece, 0)
        pieces[place] = partial[place]
        await_arrivals(pieces.at[pl.ds(0, PLANE - 1)], recv_sem.at[1])
        piece[...] = jnp.sum(pieces[...].astype(jnp.float32), axis=0).astype(jnp.bfloat16)
        at_layer = band_share(layer)

        def send_layer(step, carry):
            remote(
                piece,
                layers.at[at_layer],
                2,
                spot(across, row, (layer + far_first(step, LAYERS)) % LAYERS),
            ).start()
            return carry

        lax.fori_loop(0, LAYERS - 1, send_layer, 0)
        layers[at_layer] = piece[...]
        await_arrivals(layers.at[pl.ds(0, SENDERS - 1)], recv_sem.at[2])

    @pl.when(jnp.logical_not(owns))
    def _():
        await_arrivals(layers, recv_sem.at[2])

    total[...] = jnp.sum(layers[...].astype(jnp.float32), axis=0) / cells

    def send_total(step, carry):
        other = plane_partner(place, step)
        remote(
            total, blocks.at[place], 3, spot(other // GRID_Y, other % GRID_Y, layer)
        ).start()
        return carry

    lax.fori_loop(0, PLANE - 1, send_total, 0)
    blocks[place] = total[...]
    await_arrivals(blocks.at[pl.ds(0, PLANE - 1)], recv_sem.at[3])
    found = blocks[...]
    gram[:, :128] = found[:, :8].reshape(FULL, 128)
    gram[:, 128:] = found[:, 8:].reshape(FULL, 128)
    gram_ref[...] = gram[pl.ds(pl.multiple_of(band * 8, 8), 8), :]

    @pl.when(owns)
    def _():
        to = pl.multiple_of(band_share(band) * 16, 16)

        def send_parcels(side, weights, cells_of):
            turned = jnp.dot(weights, cells_of, preferred_element_type=jnp.float32)
            halves = [
                turned[:, 128 * h : 128 * h + 128].reshape(LAYERS, 1, 8, 128) for h in range(2)
            ]
            base_row = side * LAYERS * 16
            parcels[base_row : base_row + LAYERS * 16] = (
                jnp.concatenate(halves, axis=1).reshape(LAYERS * 16, 128).astype(jnp.bfloat16)
            )

            def send_parcel(step, carry):
                other = side * LAYERS + (layer + far_first(step, LAYERS)) % LAYERS
                at = pl.multiple_of(other * 16, 16)
                remote(
                    parcels.at[pl.ds(at, 16)],
                    arrived.at[pl.ds(to, 16)],
                    4,
                    {"band": other, "gy": 1 - half_y},
                ).start()
                return carry

            lax.fori_loop(0, LAYERS, send_parcel, 0)

        buffers = (rows_buf, cols_buf, panel_buf)
        upper = inverse_factor(gram[:128, :128], *buffers)
        send_parcels(0, upper.astype(jnp.bfloat16), share[:128])
        lower_left = full_dot(gram[128:, :128], upper, 1, 1)
        remaining = gram[128:, 128:] - full_dot(lower_left, lower_left, 1, 1)
        carried = full_dot(lower_left, upper, 1, 0)
        lower = inverse_factor(remaining, *buffers)
        inverse[:, 128:] = lower.astype(jnp.bfloat16)
        inverse[:, :128] = (-full_dot(lower, carried, 1, 0)).astype(jnp.bfloat16)
        send_parcels(1, inverse[...], share[...])

    await_arrivals(arrived, recv_sem.at[4])
    rotated_ref[...] = arrived[...]

    @pl.when(owns)
    def _():
        await_arrivals(parcels, send_sem.at[4])
        await_arrivals(pieces.at[pl.ds(0, PLANE - 1)], send_sem.at[1])
        await_arrivals(pieces.at[pl.ds(0, LAYERS - 1)], send_sem.at[2])

    await_arrivals(mine_ref, send_sem.at[0])
    for turn_at in range(2):
        for side in range(3):
            halo_copy(turn_at, side).wait_send()
    await_arrivals(blocks.at[pl.ds(0, PLANE - 1)], send_sem.at[3])


def filter_rotate(orbitals, potential, cells):
    return pl.pallas_call(
        functools.partial(filter_rotate_kernel, cells),
        out_shape=(
            jax.ShapeDtypeStruct((OWNERS * 16, 128), jnp.bfloat16),
            jax.ShapeDtypeStruct((8, FULL), jnp.float32),
        ),
        in_specs=[pl.BlockSpec(memory_space=pltpu.VMEM)] * 2,
        out_specs=(pl.BlockSpec(memory_space=pltpu.VMEM),) * 2,
        scratch_shapes=[
            pltpu.VMEM((FULL, FULL), jnp.float32),
            pltpu.VMEM((FULL, FULL), jnp.bfloat16),
            pltpu.VMEM((128, FULL), jnp.bfloat16),
            pltpu.VMEM((16, 128), jnp.float32),
            pltpu.VMEM((16, 16, 128), jnp.float32),
            pltpu.VMEM((16, 128), jnp.float32),
            pltpu.VMEM((BANDS * 16, 128), jnp.bfloat16),
            pltpu.VMEM((OWNERS * 16, 128), jnp.bfloat16),
            pltpu.VMEM((384, 128), jnp.bfloat16),
            pltpu.VMEM((2, 384, 128), jnp.bfloat16),
            pltpu.VMEM((2, 3, 384, 128), jnp.bfloat16),
            pltpu.VMEM((18, 8, 8, 128), jnp.float32),
            pltpu.VMEM((18, 8, 8, 128), jnp.float32),
            pltpu.VMEM((6, 8, 8, 128), jnp.float32),
            pltpu.VMEM((BANDS * 16, 128), jnp.bfloat16),
            pltpu.VMEM((PLANE, 16, 128), jnp.bfloat16),
            pltpu.VMEM((PLANE, 16, 128), jnp.bfloat16),
            pltpu.VMEM((16, 128), jnp.bfloat16),
            pltpu.VMEM((SENDERS, 16, 128), jnp.bfloat16),
            pltpu.VMEM((16, 128), jnp.float32),
            pltpu.VMEM((PLANE, 16, 128), jnp.float32),
            pltpu.SemaphoreType.DMA((2, 3)),
            pltpu.SemaphoreType.DMA((2, 3)),
            pltpu.SemaphoreType.DMA((5,)),
            pltpu.SemaphoreType.DMA((5,)),
            pltpu.SemaphoreType.REGULAR((3,)),
        ],
        compiler_params=pltpu.CompilerParams(collective_id=1, has_side_effects=True),
        name="filter_rotate",
    )(orbitals, potential)


def body(orbitals, potential):
    count, size_x, size_y, size_z = orbitals.shape
    total_cells = size_x * size_y * size_z * lax.axis_size("gx") * lax.axis_size("gy")
    tiles, gram_rows = filter_rotate(orbitals, potential, float(total_cells))
    rotated = tiles.astype(jnp.float32).reshape(size_x, size_y, count, size_z).transpose(2, 0, 1, 3)
    return (rotated, gram_rows)


def solution(mesh):
    return jax.shard_map(
        body,
        mesh=mesh,
        in_specs=(P("band", "gx", "gy", None), P("gx", "gy", None)),
        out_specs=(P("band", "gx", "gy", None), P("band", None)),
        check_vma=False,
    )
```

```python
import functools

import jax
import jax.numpy as jnp
from jax import lax
from jax.experimental import pallas as pl
from jax.experimental.pallas import tpu as pltpu
from jax.sharding import PartitionSpec as P

stencil_coeffs = (
    -5369.0 / 1800.0,
    12.0 / 7.0,
    -15.0 / 56.0,
    10.0 / 189.0,
    -1.0 / 112.0,
    2.0 / 1925.0,
    -1.0 / 16632.0,
)
spacing = 0.5
low_edge = 5.0
high_edge = 46.0
bottom_edge = -6.5


def filter_scalars():
    half = (high_edge - low_edge) / 2.0
    center = (high_edge + low_edge) / 2.0
    sigma = half / (bottom_edge - center)
    sigma_two = 1.0 / (2.0 / sigma - sigma)
    return (half, center, sigma, sigma_two)


MESH = pl.DeviceIdType.MESH
BANDS = 32
OWNERS = 24
LAYERS = 16
SENDERS = 12
PLANE = 32
HOLDERS = 24
GRID_X = 8
GRID_Y = 4
FULL = 256


def owner_band(share):
    return (share // 3) * 4 + share % 3


def band_share(band):
    return (band // 4) * 3 + band % 4


def far_first(step, count):
    reach = (step + 1) // 2
    return count // 2 + reach * (2 * (step % 2) - 1)


def spot(across, row, layer):
    return {"band": (row // 2) * LAYERS + layer, "gx": across, "gy": row % 2}


def plane_partner(place, step):
    across = (place // GRID_Y + far_first(step // GRID_Y, GRID_X)) % GRID_X
    return across * GRID_Y + (place + far_first(step % GRID_Y, GRID_Y)) % GRID_Y


def await_arrivals(buffer, sem):
    pltpu.make_async_copy(buffer, buffer, sem).wait()


def split_parts(value):
    high = value.astype(jnp.bfloat16)
    rest = value - high.astype(jnp.float32)
    middle = rest.astype(jnp.bfloat16)
    return high, middle, (rest - middle.astype(jnp.float32)).astype(jnp.bfloat16)


def inverse_factor(matrix, rows_buf, cols_buf, panel_buf):
    tile, size = 8, 128
    count = size // tile
    lane = lax.broadcasted_iota(jnp.int32, (tile, size), 1)

    def full(value):
        return jnp.broadcast_to(value, (tile, size))

    tiles = [matrix[tile * t : tile * t + tile] for t in range(count)]
    done = []
    for now in range(count):
        begin, slot = tile * now, now % 2
        head = tiles[now]
        rows_buf[slot] = head
        for j in range(tile):
            cols_buf[slot, j] = full(head[:, begin + j : begin + j + 1])
        inside = (lane >= begin) & (lane < begin + tile)
        entry = {
            (i, j): full(cols_buf[slot, j, i : i + 1, :])
            for j in range(tile)
            for i in range(j, tile)
        }
        row = [
            jnp.where(
                inside,
                (lane == begin + i).astype(jnp.float32),
                full(rows_buf[slot, i : i + 1, :]),
            )
            for i in range(tile)
        ]
        follows = now + 1 < count
        if follows:
            after = tiles[now + 1]
            column = [full(after[:, begin + p : begin + p + 1]) for p in range(tile)]
            after = jnp.where(inside, 0.0, after)
        scales = []
        for p in range(tile):
            scale = lax.rsqrt(entry[p, p])
            scales.append(scale)
            for i in range(p + 1, tile):
                entry[i, p] = entry[i, p] * scale
            row[p] = row[p] * scale
            if follows:
                column[p] = column[p] * scale
                after = after - column[p] * row[p]
            for i in range(p + 1, tile):
                for j in range(p + 1, i + 1):
                    entry[i, j] = entry[i, j] - entry[i, p] * entry[j, p]
                row[i] = row[i] - entry[i, p] * row[p]
                if follows:
                    column[i] = column[i] - column[p] * entry[i, p]
            panel_buf[slot, p : p + 1, :] = row[p][:1]
        if follows:
            tiles[now + 1] = after
        done.append(jnp.where(lane < begin + tile, panel_buf[slot], 0.0))
        if now + 2 < count:
            solved = [None] * tile
            for p in range(tile - 1, -1, -1):
                value = row[p]
                for i in range(p + 1, tile):
                    value = value - entry[i, p] * solved[i]
                solved[p] = value * scales[p]
            for t in range(now + 2, count):
                value = jnp.where(inside, 0.0, tiles[t])
                for p in range(tile):
                    value = value - full(tiles[t][:, begin + p : begin + p + 1]) * solved[p]
                tiles[t] = value
    return jnp.concatenate(done, axis=0)


def full_dot(left, right, left_dim, right_dim):
    a, b, c = split_parts(left)
    d, e, f = split_parts(right)
    return lax.dot_general(
        jnp.concatenate([a, a, b, a, c, b], axis=left_dim),
        jnp.concatenate([d, e, d, f, d, e], axis=right_dim),
        (((left_dim,), (right_dim,)), ((), ())),
        preferred_element_type=jnp.float32,
    )


def kinetic(wide, other, at):
    own = wide[6 + at]
    around = other[at]
    column = jnp.concatenate([around, own, around], axis=0)
    total = 3.0 * stencil_coeffs[0] * own
    for m in range(1, 7):
        near = wide[6 + at + m] + wide[6 + at - m]
        near = near + (column[8 + m : 16 + m] + column[8 - m : 16 - m])
        near = near + (pltpu.roll(own, m, 2) + pltpu.roll(own, 128 - m, 2))
        total = total + stencil_coeffs[m] * near
    return own, -0.5 / spacing**2 * total


def filter_rotate_kernel(
    cells,
    orbitals_ref,
    potential_ref,
    rotated_ref,
    gram_ref,
    gram,
    share,
    inverse,
    rows_buf,
    cols_buf,
    panel_buf,
    parcels,
    arrived,
    mine_ref,
    outgoing,
    halos,
    base,
    slope,
    other_side,
    shares,
    partial,
    pieces,
    piece,
    layers,
    total,
    blocks,
    halo_send,
    halo_recv,
    send_sem,
    recv_sem,
    tokens,
):
    band = lax.axis_index("band")
    layer = band % LAYERS
    across = lax.axis_index("gx")
    half_y = lax.axis_index("gy")
    row = (band // LAYERS) * 2 + half_y
    place = across * GRID_Y + row
    owns = band % 4 != 3

    def holds_piece(spot_x, spot_y):
        return (spot_x + spot_y) % 4 != 3

    def piece_of(spot_x, spot_y):
        return spot_x * 3 + (spot_x + spot_y) % 4

    holds = holds_piece(across, row)
    own_piece = piece_of(across, row)

    def near(step_x, step_y, step_z):
        return spot(
            (across + step_x) % GRID_X, (row + step_y) % GRID_Y, (layer + step_z) % LAYERS
        )

    barrier = pltpu.get_barrier_semaphore()
    greeted = [near(0, 0, step) for step in (3, -3, 2, -2, 1, -1)]
    greeted += [near(0, side, step) for step in (2, -2, 1, -1, 0) for side in (1, 3)]
    greeted += [near(1, 0, 0), near(-1, 0, 0)]
    for device in greeted:
        pl.semaphore_signal(barrier, 1, device_id=device, device_id_type=MESH)

    def send_tokens(kind, devices):
        for device in devices:
            pl.semaphore_signal(tokens.at[kind], 1, device_id=device, device_id_type=MESH)

    def turn(at, carry):
        plane = jnp.swapaxes(orbitals_ref[:, at], 0, 1)
        base[6 + at] = plane
        rows_at = pl.ds(pl.multiple_of(at * 64, 64), 64)
        outgoing[0, rows_at] = plane.reshape(64, 128).astype(jnp.bfloat16)
        return carry

    lax.fori_loop(0, 6, turn, 0)
    pl.semaphore_wait(barrier, len(greeted))
    send_tokens(0, (near(0, 0, 3), near(0, 0, -3)))

    sides = (near(1, 0, 0), near(-1, 0, 0), {"gy": 1 - half_y})

    def halo_copy(turn_at, side):
        return pltpu.make_async_remote_copy(
            src_ref=outgoing.at[turn_at],
            dst_ref=halos.at[turn_at, side],
            send_sem=halo_send.at[turn_at, side],
            recv_sem=halo_recv.at[turn_at, side],
            device_id=sides[side],
            device_id_type=MESH,
        )

    def halo_take(turn_at, wide):
        for side in range(3):
            halo_copy(turn_at, side).wait_recv()

        def widen(at, carry):
            rows_at = pl.ds(pl.multiple_of(at * 64, 64), 64)
            for side, target, offset in ((0, wide, 0), (1, wide, 12), (2, other_side, 0)):
                block = halos[turn_at, side, rows_at]
                target[at + offset] = block.astype(jnp.float32).reshape(8, 8, 128)
            return carry

        lax.fori_loop(0, 6, widen, 0)

    half, center, sigma, sigma_two = filter_scalars()
    for side in (2, 0, 1):
        halo_copy(0, side).start()
    halo_take(0, base)
    pl.semaphore_wait(tokens.at[0], 2)
    send_tokens(1, (near(0, 0, 5), near(0, 0, -5)))

    def first_step(at, carry):
        own, moved = kinetic(base, other_side, at)
        shifted = (potential_ref[at] - center)[:, None, :]
        result = sigma / half * (moved + shifted * own)
        slope[6 + at] = result
        rows_at = pl.ds(pl.multiple_of(at * 64, 64), 64)
        outgoing[1, rows_at] = result.reshape(64, 128).astype(jnp.bfloat16)
        return carry

    lax.fori_loop(0, 6, first_step, 0)
    for side in (2, 0, 1):
        halo_copy(1, side).start()
    halo_take(1, slope)
    send_tokens(2, (near(3, 0, 0), near(-3, 0, 0)))

    def second_step(at, carry):
        own, moved = kinetic(slope, other_side, at)
        shifted = (potential_ref[at] - center)[:, None, :]
        result = 2.0 * sigma_two / half * (moved + shifted * own) - sigma * sigma_two * base[6 + at]
        rows_at = pl.ds(pl.multiple_of(at * 64, 64), 64)
        mine_ref[rows_at] = result.reshape(64, 128).astype(jnp.bfloat16)
        return carry

    lax.fori_loop(0, 6, second_step, 0)

    def remote(source, target, phase, device):
        return pltpu.make_async_remote_copy(
            src_ref=source,
            dst_ref=target,
            send_sem=send_sem.at[phase],
            recv_sem=recv_sem.at[phase],
            device_id=device,
            device_id_type=MESH,
        )

    def cell_share(step, carry):
        to_row = (row + 1 + 2 * (step % 2)) % GRID_Y
        to_layer = (layer + far_first(step // 2, LAYERS)) % LAYERS
        other = (to_row // 2) * LAYERS + to_layer

        @pl.when(other % 4 != 3)
        def _():
            at = pl.multiple_of(band_share(other) * 16, 16)
            to = pl.multiple_of(band * 16, 16)
            remote(
                mine_ref.at[pl.ds(at, 16)],
                shares.at[pl.ds(to, 16)],
                0,
                {"band": other, "gy": 1 - half_y},
            ).start()

        return carry

    pl.semaphore_wait(tokens.at[1], 2)
    lax.fori_loop(0, BANDS, cell_share, 0)
    pl.semaphore_wait(tokens.at[2], 2)

    @pl.when(owns)
    def _():
        await_arrivals(shares, recv_sem.at[0])
        spread = shares[...].astype(jnp.float32).reshape(BANDS, 2, 8, 128)
        halves = [spread[:, half].reshape(FULL, 128) for half in range(2)]
        both = jnp.concatenate(halves, axis=1).astype(jnp.bfloat16)
        share[...] = both
        first = lax.dot_general(
            both[:128], both[:128], (((1,), (1,)), ((), ())), preferred_element_type=jnp.float32
        )
        second = lax.dot_general(
            both[128:], both, (((1,), (1,)), ((), ())), preferred_element_type=jnp.float32
        )
        blocked = jnp.concatenate([first, second[:, :128], second[:, 128:]], axis=0)
        partial[...] = blocked.astype(jnp.bfloat16).reshape(HOLDERS, 16, 128)

        def send_piece(step, carry):
            other = plane_partner(place, step)
            other_x, other_y = other // GRID_Y, other % GRID_Y

            @pl.when(holds_piece(other_x, other_y))
            def _():
                remote(
                    partial.at[piece_of(other_x, other_y)],
                    pieces.at[place],
                    1,
                    spot(other_x, other_y, layer),
                ).start()

            return carry

        lax.fori_loop(0, PLANE - 1, send_piece, 0)

    @pl.when(owns & holds)
    def _():
        pieces[place] = partial[own_piece]
        await_arrivals(pieces.at[pl.ds(0, PLANE - 1)], recv_sem.at[1])
        piece[...] = jnp.sum(pieces[...].astype(jnp.float32), axis=0).astype(jnp.bfloat16)
        at_layer = band_share(layer)

        def send_layer(step, carry):
            remote(
                piece,
                layers.at[at_layer],
                2,
                spot(across, row, (layer + far_first(step, LAYERS)) % LAYERS),
            ).start()
            return carry

        lax.fori_loop(0, LAYERS - 1, send_layer, 0)
        layers[at_layer] = piece[...]
        await_arrivals(layers.at[pl.ds(0, SENDERS - 1)], recv_sem.at[2])

    @pl.when(jnp.logical_not(owns) & holds)
    def _():
        await_arrivals(layers, recv_sem.at[2])

    @pl.when(holds)
    def _():
        total[...] = jnp.sum(layers[...].astype(jnp.float32), axis=0) / cells

        def send_total(step, carry):
            other = plane_partner(place, step)
            remote(
                total, blocks.at[own_piece], 3, spot(other // GRID_Y, other % GRID_Y, layer)
            ).start()
            return carry

        lax.fori_loop(0, PLANE - 1, send_total, 0)
        blocks[own_piece] = total[...]
        await_arrivals(blocks.at[pl.ds(0, HOLDERS - 1)], recv_sem.at[3])

    @pl.when(jnp.logical_not(holds))
    def _():
        await_arrivals(blocks.at[pl.ds(0, HOLDERS)], recv_sem.at[3])

    @pl.when(owns)
    def _():
        to = pl.multiple_of(band_share(band) * 16, 16)

        def send_parcels(side, weights, cells_of):
            turned = jnp.dot(weights, cells_of, preferred_element_type=jnp.float32)
            halves = [
                turned[:, 128 * h : 128 * h + 128].reshape(LAYERS, 1, 8, 128) for h in range(2)
            ]
            base_row = side * LAYERS * 16
            parcels[base_row : base_row + LAYERS * 16] = (
                jnp.concatenate(halves, axis=1).reshape(LAYERS * 16, 128).astype(jnp.bfloat16)
            )

            def send_parcel(step, carry):
                other = side * LAYERS + (layer + far_first(step, LAYERS)) % LAYERS
                at = pl.multiple_of(other * 16, 16)
                remote(
                    parcels.at[pl.ds(at, 16)],
                    arrived.at[pl.ds(to, 16)],
                    4,
                    {"band": other, "gy": 1 - half_y},
                ).start()
                return carry

            lax.fori_loop(0, LAYERS, send_parcel, 0)

        buffers = (rows_buf, cols_buf, panel_buf)
        corner = blocks[8:16].reshape(128, 128)
        upper = inverse_factor(blocks[0:8].reshape(128, 128), *buffers)
        send_parcels(0, upper.astype(jnp.bfloat16), share[:128])
        lower_left = full_dot(corner, upper, 1, 1)
        remaining = blocks[16:24].reshape(128, 128) - full_dot(lower_left, lower_left, 1, 1)
        carried = full_dot(lower_left, upper, 1, 0)
        lower = inverse_factor(remaining, *buffers)
        inverse[:, 128:] = lower.astype(jnp.bfloat16)
        inverse[:, :128] = (-full_dot(lower, carried, 1, 0)).astype(jnp.bfloat16)
        send_parcels(1, inverse[...], share[...])

    middle_block = blocks[8:16].reshape(128, 128)
    gram[:128, :128] = blocks[0:8].reshape(128, 128)
    gram[:128, 128:] = middle_block.T
    gram[128:, :128] = middle_block
    gram[128:, 128:] = blocks[16:24].reshape(128, 128)
    gram_ref[...] = gram[pl.ds(pl.multiple_of(band * 8, 8), 8), :]

    await_arrivals(arrived, recv_sem.at[4])
    rotated_ref[...] = arrived[...]

    @pl.when(owns)
    def _():
        await_arrivals(parcels, send_sem.at[4])

    @pl.when(owns & holds)
    def _():
        await_arrivals(partial.at[pl.ds(0, HOLDERS - 1)], send_sem.at[1])
        await_arrivals(pieces.at[pl.ds(0, LAYERS - 1)], send_sem.at[2])

    @pl.when(owns & jnp.logical_not(holds))
    def _():
        await_arrivals(partial, send_sem.at[1])

    await_arrivals(mine_ref, send_sem.at[0])
    for turn_at in range(2):
        for side in range(3):
            halo_copy(turn_at, side).wait_send()

    @pl.when(holds)
    def _():
        await_arrivals(blocks.at[pl.ds(0, PLANE - 1)], send_sem.at[3])


def filter_rotate(orbitals, potential, cells):
    return pl.pallas_call(
        functools.partial(filter_rotate_kernel, cells),
        out_shape=(
            jax.ShapeDtypeStruct((OWNERS * 16, 128), jnp.bfloat16),
            jax.ShapeDtypeStruct((8, FULL), jnp.float32),
        ),
        in_specs=[pl.BlockSpec(memory_space=pltpu.VMEM)] * 2,
        out_specs=(pl.BlockSpec(memory_space=pltpu.VMEM),) * 2,
        scratch_shapes=[
            pltpu.VMEM((FULL, FULL), jnp.float32),
            pltpu.VMEM((FULL, FULL), jnp.bfloat16),
            pltpu.VMEM((128, FULL), jnp.bfloat16),
            pltpu.VMEM((2, 8, 128), jnp.float32),
            pltpu.VMEM((2, 8, 8, 128), jnp.float32),
            pltpu.VMEM((2, 8, 128), jnp.float32),
            pltpu.VMEM((BANDS * 16, 128), jnp.bfloat16),
            pltpu.VMEM((OWNERS * 16, 128), jnp.bfloat16),
            pltpu.VMEM((384, 128), jnp.bfloat16),
            pltpu.VMEM((2, 384, 128), jnp.bfloat16),
            pltpu.VMEM((2, 3, 384, 128), jnp.bfloat16),
            pltpu.VMEM((18, 8, 8, 128), jnp.float32),
            pltpu.VMEM((18, 8, 8, 128), jnp.float32),
            pltpu.VMEM((6, 8, 8, 128), jnp.float32),
            pltpu.VMEM((BANDS * 16, 128), jnp.bfloat16),
            pltpu.VMEM((HOLDERS, 16, 128), jnp.bfloat16),
            pltpu.VMEM((PLANE, 16, 128), jnp.bfloat16),
            pltpu.VMEM((16, 128), jnp.bfloat16),
            pltpu.VMEM((SENDERS, 16, 128), jnp.bfloat16),
            pltpu.VMEM((16, 128), jnp.float32),
            pltpu.VMEM((PLANE, 16, 128), jnp.float32),
            pltpu.SemaphoreType.DMA((2, 3)),
            pltpu.SemaphoreType.DMA((2, 3)),
            pltpu.SemaphoreType.DMA((5,)),
            pltpu.SemaphoreType.DMA((5,)),
            pltpu.SemaphoreType.REGULAR((3,)),
        ],
        compiler_params=pltpu.CompilerParams(collective_id=1, has_side_effects=True),
        name="filter_rotate",
    )(orbitals, potential)


def body(orbitals, potential):
    count, size_x, size_y, size_z = orbitals.shape
    total_cells = size_x * size_y * size_z * lax.axis_size("gx") * lax.axis_size("gy")
    tiles, gram_rows = filter_rotate(orbitals, potential, float(total_cells))
    rotated = tiles.astype(jnp.float32).reshape(size_x, size_y, count, size_z).transpose(2, 0, 1, 3)
    return (rotated, gram_rows)


def solution(mesh):
    return jax.shard_map(
        body,
        mesh=mesh,
        in_specs=(P("band", "gx", "gy", None), P("gx", "gy", None)),
        out_specs=(P("band", "gx", "gy", None), P("band", None)),
        check_vma=False,
    )
```

```python
import functools

import jax
import jax.numpy as jnp
from jax import lax
from jax.experimental import pallas as pl
from jax.experimental.pallas import tpu as pltpu
from jax.sharding import PartitionSpec as P

stencil_coeffs = (
    -5369.0 / 1800.0,
    12.0 / 7.0,
    -15.0 / 56.0,
    10.0 / 189.0,
    -1.0 / 112.0,
    2.0 / 1925.0,
    -1.0 / 16632.0,
)
spacing = 0.5
low_edge = 5.0
high_edge = 46.0
bottom_edge = -6.5


def filter_scalars():
    half = (high_edge - low_edge) / 2.0
    center = (high_edge + low_edge) / 2.0
    sigma = half / (bottom_edge - center)
    sigma_two = 1.0 / (2.0 / sigma - sigma)
    return (half, center, sigma, sigma_two)


MESH = pl.DeviceIdType.MESH
BANDS = 32
OWNERS = 24
LAYERS = 16
SENDERS = 12
PLANE = 32
HOLDERS = 24
GRID_X = 8
GRID_Y = 4
FULL = 256


def owner_band(share):
    return (share // 3) * 4 + share % 3


def band_share(band):
    return (band // 4) * 3 + band % 4


def far_first(step, count):
    reach = (step + 1) // 2
    return count // 2 + reach * (2 * (step % 2) - 1)


def spot(across, row, layer):
    return {"band": (row // 2) * LAYERS + layer, "gx": across, "gy": row % 2}


def plane_partner(place, step):
    across = (place // GRID_Y + far_first(step // GRID_Y, GRID_X)) % GRID_X
    return across * GRID_Y + (place + far_first(step % GRID_Y, GRID_Y)) % GRID_Y


def await_arrivals(buffer, sem):
    pltpu.make_async_copy(buffer, buffer, sem).wait()


def split_parts(value):
    high = value.astype(jnp.bfloat16)
    rest = value - high.astype(jnp.float32)
    middle = rest.astype(jnp.bfloat16)
    return high, middle, (rest - middle.astype(jnp.float32)).astype(jnp.bfloat16)


def inverse_factor(matrix, rows_buf, cols_buf, panel_buf):
    tile, size = 8, 128
    count = size // tile
    lane = lax.broadcasted_iota(jnp.int32, (tile, size), 1)

    def full(value):
        return jnp.broadcast_to(value, (tile, size))

    tiles = [matrix[tile * t : tile * t + tile] for t in range(count)]
    done = []
    for now in range(count):
        begin, slot = tile * now, now % 2
        head = tiles[now]
        rows_buf[slot] = head
        for j in range(tile):
            cols_buf[slot, j] = full(head[:, begin + j : begin + j + 1])
        inside = (lane >= begin) & (lane < begin + tile)
        entry = {
            (i, j): full(cols_buf[slot, j, i : i + 1, :])
            for j in range(tile)
            for i in range(j, tile)
        }
        row = [
            jnp.where(
                inside,
                (lane == begin + i).astype(jnp.float32),
                full(rows_buf[slot, i : i + 1, :]),
            )
            for i in range(tile)
        ]
        follows = now + 1 < count
        if follows:
            after = tiles[now + 1]
            column = [full(after[:, begin + p : begin + p + 1]) for p in range(tile)]
            after = jnp.where(inside, 0.0, after)
        scales = []
        for p in range(tile):
            scale = lax.rsqrt(entry[p, p])
            scales.append(scale)
            for i in range(p + 1, tile):
                entry[i, p] = entry[i, p] * scale
            row[p] = row[p] * scale
            if follows:
                column[p] = column[p] * scale
                after = after - column[p] * row[p]
            for i in range(p + 1, tile):
                for j in range(p + 1, i + 1):
                    entry[i, j] = entry[i, j] - entry[i, p] * entry[j, p]
                row[i] = row[i] - entry[i, p] * row[p]
                if follows:
                    column[i] = column[i] - column[p] * entry[i, p]
            panel_buf[slot, p : p + 1, :] = row[p][:1]
        if follows:
            tiles[now + 1] = after
        done.append(jnp.where(lane < begin + tile, panel_buf[slot], 0.0))
        if now + 2 < count:
            solved = [None] * tile
            for p in range(tile - 1, -1, -1):
                value = row[p]
                for i in range(p + 1, tile):
                    value = value - entry[i, p] * solved[i]
                solved[p] = value * scales[p]
            for t in range(now + 2, count):
                value = jnp.where(inside, 0.0, tiles[t])
                for p in range(tile):
                    value = value - full(tiles[t][:, begin + p : begin + p + 1]) * solved[p]
                tiles[t] = value
    return jnp.concatenate(done, axis=0)


def full_dot(left, right, left_dim, right_dim):
    a, b, c = split_parts(left)
    d, e, f = split_parts(right)
    return lax.dot_general(
        jnp.concatenate([a, a, b, a, c, b], axis=left_dim),
        jnp.concatenate([d, e, d, f, d, e], axis=right_dim),
        (((left_dim,), (right_dim,)), ((), ())),
        preferred_element_type=jnp.float32,
    )


def along_z(own, shifted):
    total = 3.0 * stencil_coeffs[0] * own
    for m in range(1, 7):
        total = total + stencil_coeffs[m] * (pltpu.roll(own, m, 2) + pltpu.roll(own, 128 - m, 2))
    return shifted * own - 0.5 / spacing**2 * total


def across_xy(wide, around, at):
    column = jnp.concatenate([around, wide[6 + at], around], axis=0)
    total = jnp.zeros_like(around)
    for m in range(1, 7):
        near = wide[6 + at + m] + wide[6 + at - m]
        near = near + (column[8 + m : 16 + m] + column[8 - m : 16 - m])
        total = total + stencil_coeffs[m] * near
    return -0.5 / spacing**2 * total


def filter_rotate_kernel(
    cells,
    orbitals_ref,
    potential_ref,
    rotated_ref,
    gram_ref,
    gram,
    share,
    inverse,
    rows_buf,
    cols_buf,
    panel_buf,
    parcels,
    arrived,
    mine_ref,
    outgoing,
    halos,
    base,
    slope,
    inner,
    shares,
    partial,
    pieces,
    piece,
    layers,
    total,
    blocks,
    halo_send,
    halo_recv,
    send_sem,
    recv_sem,
    tokens,
):
    band = lax.axis_index("band")
    layer = band % LAYERS
    across = lax.axis_index("gx")
    half_y = lax.axis_index("gy")
    row = (band // LAYERS) * 2 + half_y
    place = across * GRID_Y + row
    owns = band % 4 != 3

    def holds_piece(spot_x, spot_y):
        return (spot_x + spot_y) % 4 != 3

    def piece_of(spot_x, spot_y):
        return spot_x * 3 + (spot_x + spot_y) % 4

    holds = holds_piece(across, row)
    own_piece = piece_of(across, row)

    def near(step_x, step_y, step_z):
        return spot(
            (across + step_x) % GRID_X, (row + step_y) % GRID_Y, (layer + step_z) % LAYERS
        )

    barrier = pltpu.get_barrier_semaphore()
    greeted = [near(0, 0, step) for step in (3, -3, 2, -2, 1, -1)]
    greeted += [near(0, side, step) for step in (2, -2, 1, -1, 0) for side in (1, 3)]
    greeted += [near(1, 0, 0), near(-1, 0, 0)]
    for device in greeted:
        pl.semaphore_signal(barrier, 1, device_id=device, device_id_type=MESH)

    def send_tokens(kind, devices):
        for device in devices:
            pl.semaphore_signal(tokens.at[kind], 1, device_id=device, device_id_type=MESH)

    def turn(at, carry):
        plane = jnp.swapaxes(orbitals_ref[:, at], 0, 1)
        base[6 + at] = plane
        rows_at = pl.ds(pl.multiple_of(at * 64, 64), 64)
        outgoing[0, rows_at] = plane.reshape(64, 128).astype(jnp.bfloat16)
        return carry

    lax.fori_loop(0, 6, turn, 0, unroll=2)
    pl.semaphore_wait(barrier, len(greeted))
    send_tokens(0, (near(0, 0, 3), near(0, 0, -3)))

    sides = (near(1, 0, 0), near(-1, 0, 0), {"gy": 1 - half_y})

    def halo_copy(turn_at, side):
        return pltpu.make_async_remote_copy(
            src_ref=outgoing.at[turn_at],
            dst_ref=halos.at[turn_at, side],
            send_sem=halo_send.at[turn_at, side],
            recv_sem=halo_recv.at[turn_at, side],
            device_id=sides[side],
            device_id_type=MESH,
        )

    def block_rows(at):
        return pl.ds(pl.multiple_of(at * 64, 64), 64)

    def inner_part(wide):
        def fill(at, carry):
            inner[at] = along_z(wide[6 + at], (potential_ref[at] - center)[:, None, :])
            return carry

        lax.fori_loop(0, 6, fill, 0, unroll=2)

    def halo_take(turn_at, wide):
        for side in range(2):
            halo_copy(turn_at, side).wait_recv()

        def widen(at, carry):
            for side in range(2):
                block = halos[turn_at, side, block_rows(at)]
                wide[12 * side + at] = block.astype(jnp.float32).reshape(8, 8, 128)
            return carry

        lax.fori_loop(0, 6, widen, 0, unroll=2)
        halo_copy(turn_at, 2).wait_recv()

    def shifted_ham(turn_at, wide, at):
        around = halos[turn_at, 2, block_rows(at)].astype(jnp.float32).reshape(8, 8, 128)
        return inner[at] + across_xy(wide, around, at)

    half, center, sigma, sigma_two = filter_scalars()
    for side in (2, 0, 1):
        halo_copy(0, side).start()
    inner_part(base)
    halo_take(0, base)
    pl.semaphore_wait(tokens.at[0], 2)
    send_tokens(1, (near(0, 0, 5), near(0, 0, -5)))

    def first_step(at, carry):
        result = sigma / half * shifted_ham(0, base, at)
        slope[6 + at] = result
        outgoing[1, block_rows(at)] = result.reshape(64, 128).astype(jnp.bfloat16)
        return carry

    lax.fori_loop(0, 6, first_step, 0, unroll=2)
    for side in (2, 0, 1):
        halo_copy(1, side).start()
    inner_part(slope)
    halo_take(1, slope)
    send_tokens(2, (near(3, 0, 0), near(-3, 0, 0)))

    def second_step(at, carry):
        result = 2.0 * sigma_two / half * shifted_ham(1, slope, at)
        result = result - sigma * sigma_two * base[6 + at]
        mine_ref[block_rows(at)] = result.reshape(64, 128).astype(jnp.bfloat16)
        return carry

    lax.fori_loop(0, 6, second_step, 0, unroll=2)

    def remote(source, target, phase, device):
        return pltpu.make_async_remote_copy(
            src_ref=source,
            dst_ref=target,
            send_sem=send_sem.at[phase],
            recv_sem=recv_sem.at[phase],
            device_id=device,
            device_id_type=MESH,
        )

    def cell_share(step, carry):
        to_row = (row + 1 + 2 * (step % 2)) % GRID_Y
        to_layer = (layer + far_first(step // 2, LAYERS)) % LAYERS
        other = (to_row // 2) * LAYERS + to_layer

        @pl.when(other % 4 != 3)
        def _():
            at = pl.multiple_of(band_share(other) * 16, 16)
            to = pl.multiple_of(band * 16, 16)
            remote(
                mine_ref.at[pl.ds(at, 16)],
                shares.at[pl.ds(to, 16)],
                0,
                {"band": other, "gy": 1 - half_y},
            ).start()

        return carry

    pl.semaphore_wait(tokens.at[1], 2)
    lax.fori_loop(0, BANDS, cell_share, 0)
    pl.semaphore_wait(tokens.at[2], 2)

    @pl.when(owns)
    def _():
        await_arrivals(shares, recv_sem.at[0])
        spread = shares[...].astype(jnp.float32).reshape(BANDS, 2, 8, 128)
        halves = [spread[:, half].reshape(FULL, 128) for half in range(2)]
        both = jnp.concatenate(halves, axis=1).astype(jnp.bfloat16)
        share[...] = both
        first = lax.dot_general(
            both[:128], both[:128], (((1,), (1,)), ((), ())), preferred_element_type=jnp.float32
        )
        second = lax.dot_general(
            both[128:], both, (((1,), (1,)), ((), ())), preferred_element_type=jnp.float32
        )
        blocked = jnp.concatenate([first, second[:, :128], second[:, 128:]], axis=0)
        partial[...] = blocked.astype(jnp.bfloat16).reshape(HOLDERS, 16, 128)

        def send_piece(step, carry):
            other = plane_partner(place, step)
            other_x, other_y = other // GRID_Y, other % GRID_Y

            @pl.when(holds_piece(other_x, other_y))
            def _():
                remote(
                    partial.at[piece_of(other_x, other_y)],
                    pieces.at[place],
                    1,
                    spot(other_x, other_y, layer),
                ).start()

            return carry

        lax.fori_loop(0, PLANE - 1, send_piece, 0)

    @pl.when(owns & holds)
    def _():
        pieces[place] = partial[own_piece]
        await_arrivals(pieces.at[pl.ds(0, PLANE - 1)], recv_sem.at[1])
        piece[...] = jnp.sum(pieces[...].astype(jnp.float32), axis=0).astype(jnp.bfloat16)
        at_layer = band_share(layer)

        def send_layer(step, carry):
            remote(
                piece,
                layers.at[at_layer],
                2,
                spot(across, row, (layer + far_first(step, LAYERS)) % LAYERS),
            ).start()
            return carry

        lax.fori_loop(0, LAYERS - 1, send_layer, 0)
        layers[at_layer] = piece[...]
        await_arrivals(layers.at[pl.ds(0, SENDERS - 1)], recv_sem.at[2])

    @pl.when(jnp.logical_not(owns) & holds)
    def _():
        await_arrivals(layers, recv_sem.at[2])

    @pl.when(holds)
    def _():
        total[...] = jnp.sum(layers[...].astype(jnp.float32), axis=0) / cells

        def send_total(step, carry):
            other = plane_partner(place, step)
            remote(
                total, blocks.at[own_piece], 3, spot(other // GRID_Y, other % GRID_Y, layer)
            ).start()
            return carry

        lax.fori_loop(0, PLANE - 1, send_total, 0)
        blocks[own_piece] = total[...]
        await_arrivals(blocks.at[pl.ds(0, HOLDERS - 1)], recv_sem.at[3])

    @pl.when(jnp.logical_not(holds))
    def _():
        await_arrivals(blocks.at[pl.ds(0, HOLDERS)], recv_sem.at[3])

    @pl.when(owns)
    def _():
        to = pl.multiple_of(band_share(band) * 16, 16)

        def send_parcels(side, weights, cells_of):
            turned = jnp.dot(weights, cells_of, preferred_element_type=jnp.float32)
            halves = [
                turned[:, 128 * h : 128 * h + 128].reshape(LAYERS, 1, 8, 128) for h in range(2)
            ]
            base_row = side * LAYERS * 16
            parcels[base_row : base_row + LAYERS * 16] = (
                jnp.concatenate(halves, axis=1).reshape(LAYERS * 16, 128).astype(jnp.bfloat16)
            )

            def send_parcel(step, carry):
                other = side * LAYERS + (layer + far_first(step, LAYERS)) % LAYERS
                at = pl.multiple_of(other * 16, 16)
                remote(
                    parcels.at[pl.ds(at, 16)],
                    arrived.at[pl.ds(to, 16)],
                    4,
                    {"band": other, "gy": 1 - half_y},
                ).start()
                return carry

            lax.fori_loop(0, LAYERS, send_parcel, 0)

        buffers = (rows_buf, cols_buf, panel_buf)
        corner = blocks[8:16].reshape(128, 128)
        upper = inverse_factor(blocks[0:8].reshape(128, 128), *buffers)
        send_parcels(0, upper.astype(jnp.bfloat16), share[:128])
        lower_left = full_dot(corner, upper, 1, 1)
        remaining = blocks[16:24].reshape(128, 128) - full_dot(lower_left, lower_left, 1, 1)
        carried = full_dot(lower_left, upper, 1, 0)
        lower = inverse_factor(remaining, *buffers)
        inverse[:, 128:] = lower.astype(jnp.bfloat16)
        inverse[:, :128] = (-full_dot(lower, carried, 1, 0)).astype(jnp.bfloat16)
        send_parcels(1, inverse[...], share[...])

    middle_block = blocks[8:16].reshape(128, 128)
    gram[:128, :128] = blocks[0:8].reshape(128, 128)
    gram[:128, 128:] = middle_block.T
    gram[128:, :128] = middle_block
    gram[128:, 128:] = blocks[16:24].reshape(128, 128)
    gram_ref[...] = gram[pl.ds(pl.multiple_of(band * 8, 8), 8), :]

    await_arrivals(arrived, recv_sem.at[4])
    rotated_ref[...] = arrived[...]

    @pl.when(owns)
    def _():
        await_arrivals(parcels, send_sem.at[4])

    @pl.when(owns & holds)
    def _():
        await_arrivals(partial.at[pl.ds(0, HOLDERS - 1)], send_sem.at[1])
        await_arrivals(pieces.at[pl.ds(0, LAYERS - 1)], send_sem.at[2])

    @pl.when(owns & jnp.logical_not(holds))
    def _():
        await_arrivals(partial, send_sem.at[1])

    await_arrivals(mine_ref, send_sem.at[0])
    for turn_at in range(2):
        for side in range(3):
            halo_copy(turn_at, side).wait_send()

    @pl.when(holds)
    def _():
        await_arrivals(blocks.at[pl.ds(0, PLANE - 1)], send_sem.at[3])


def filter_rotate(orbitals, potential, cells):
    return pl.pallas_call(
        functools.partial(filter_rotate_kernel, cells),
        out_shape=(
            jax.ShapeDtypeStruct((OWNERS * 16, 128), jnp.bfloat16),
            jax.ShapeDtypeStruct((8, FULL), jnp.float32),
        ),
        in_specs=[pl.BlockSpec(memory_space=pltpu.VMEM)] * 2,
        out_specs=(pl.BlockSpec(memory_space=pltpu.VMEM),) * 2,
        scratch_shapes=[
            pltpu.VMEM((FULL, FULL), jnp.float32),
            pltpu.VMEM((FULL, FULL), jnp.bfloat16),
            pltpu.VMEM((128, FULL), jnp.bfloat16),
            pltpu.VMEM((2, 8, 128), jnp.float32),
            pltpu.VMEM((2, 8, 8, 128), jnp.float32),
            pltpu.VMEM((2, 8, 128), jnp.float32),
            pltpu.VMEM((BANDS * 16, 128), jnp.bfloat16),
            pltpu.VMEM((OWNERS * 16, 128), jnp.bfloat16),
            pltpu.VMEM((384, 128), jnp.bfloat16),
            pltpu.VMEM((2, 384, 128), jnp.bfloat16),
            pltpu.VMEM((2, 3, 384, 128), jnp.bfloat16),
            pltpu.VMEM((18, 8, 8, 128), jnp.float32),
            pltpu.VMEM((18, 8, 8, 128), jnp.float32),
            pltpu.VMEM((6, 8, 8, 128), jnp.float32),
            pltpu.VMEM((BANDS * 16, 128), jnp.bfloat16),
            pltpu.VMEM((HOLDERS, 16, 128), jnp.bfloat16),
            pltpu.VMEM((PLANE, 16, 128), jnp.bfloat16),
            pltpu.VMEM((16, 128), jnp.bfloat16),
            pltpu.VMEM((SENDERS, 16, 128), jnp.bfloat16),
            pltpu.VMEM((16, 128), jnp.float32),
            pltpu.VMEM((PLANE, 16, 128), jnp.float32),
            pltpu.SemaphoreType.DMA((2, 3)),
            pltpu.SemaphoreType.DMA((2, 3)),
            pltpu.SemaphoreType.DMA((5,)),
            pltpu.SemaphoreType.DMA((5,)),
            pltpu.SemaphoreType.REGULAR((3,)),
        ],
        compiler_params=pltpu.CompilerParams(collective_id=1, has_side_effects=True),
        name="filter_rotate",
    )(orbitals, potential)


def body(orbitals, potential):
    count, size_x, size_y, size_z = orbitals.shape
    total_cells = size_x * size_y * size_z * lax.axis_size("gx") * lax.axis_size("gy")
    tiles, gram_rows = filter_rotate(orbitals, potential, float(total_cells))
    rotated = tiles.astype(jnp.float32).reshape(size_x, size_y, count, size_z).transpose(2, 0, 1, 3)
    return (rotated, gram_rows)


def solution(mesh):
    return jax.shard_map(
        body,
        mesh=mesh,
        in_specs=(P("band", "gx", "gy", None), P("gx", "gy", None)),
        out_specs=(P("band", "gx", "gy", None), P("band", None)),
        check_vma=False,
    )
```

```python
import functools

import jax
import jax.numpy as jnp
from jax import lax
from jax.experimental import pallas as pl
from jax.experimental.pallas import tpu as pltpu
from jax.sharding import PartitionSpec as P

stencil_coeffs = (
    -5369.0 / 1800.0,
    12.0 / 7.0,
    -15.0 / 56.0,
    10.0 / 189.0,
    -1.0 / 112.0,
    2.0 / 1925.0,
    -1.0 / 16632.0,
)
spacing = 0.5
low_edge = 5.0
high_edge = 46.0
bottom_edge = -6.5


def filter_scalars():
    half = (high_edge - low_edge) / 2.0
    center = (high_edge + low_edge) / 2.0
    sigma = half / (bottom_edge - center)
    sigma_two = 1.0 / (2.0 / sigma - sigma)
    return (half, center, sigma, sigma_two)


MESH = pl.DeviceIdType.MESH
BANDS = 32
OWNERS = 24
LAYERS = 16
SENDERS = 12
PLANE = 32
HOLDERS = 24
GRID_X = 8
GRID_Y = 4
FULL = 256


def owner_band(share):
    return (share // 3) * 4 + share % 3


def band_share(band):
    return (band // 4) * 3 + band % 4


def far_first(step, count):
    reach = (step + 1) // 2
    return count // 2 + reach * (2 * (step % 2) - 1)


def spot(across, row, layer):
    return {"band": (row // 2) * LAYERS + layer, "gx": across, "gy": row % 2}


def plane_partner(place, step):
    across = (place // GRID_Y + far_first(step // GRID_Y, GRID_X)) % GRID_X
    return across * GRID_Y + (place + far_first(step % GRID_Y, GRID_Y)) % GRID_Y


def await_arrivals(buffer, sem):
    pltpu.make_async_copy(buffer, buffer, sem).wait()


def split_parts(value):
    high = value.astype(jnp.bfloat16)
    rest = value - high.astype(jnp.float32)
    middle = rest.astype(jnp.bfloat16)
    return high, middle, (rest - middle.astype(jnp.float32)).astype(jnp.bfloat16)


def inverse_factor(matrix, rows_buf, cols_buf, panel_buf):
    tile, size = 8, 128
    count = size // tile
    lane = lax.broadcasted_iota(jnp.int32, (tile, size), 1)

    def full(value):
        return jnp.broadcast_to(value, (tile, size))

    tiles = [matrix[tile * t : tile * t + tile] for t in range(count)]
    done = []
    for now in range(count):
        begin, slot = tile * now, now % 2
        head = tiles[now]
        rows_buf[slot] = head
        for j in range(tile):
            cols_buf[slot, j] = full(head[:, begin + j : begin + j + 1])
        inside = (lane >= begin) & (lane < begin + tile)
        entry = {
            (i, j): full(cols_buf[slot, j, i : i + 1, :])
            for j in range(tile)
            for i in range(j, tile)
        }
        row = [
            jnp.where(
                inside,
                (lane == begin + i).astype(jnp.float32),
                full(rows_buf[slot, i : i + 1, :]),
            )
            for i in range(tile)
        ]
        follows = now + 1 < count
        if follows:
            after = tiles[now + 1]
            column = [full(after[:, begin + p : begin + p + 1]) for p in range(tile)]
            after = jnp.where(inside, 0.0, after)
        scales = []
        for p in range(tile):
            scale = lax.rsqrt(entry[p, p])
            scales.append(scale)
            for i in range(p + 1, tile):
                entry[i, p] = entry[i, p] * scale
            row[p] = row[p] * scale
            if follows:
                column[p] = column[p] * scale
                after = after - column[p] * row[p]
            for i in range(p + 1, tile):
                for j in range(p + 1, i + 1):
                    entry[i, j] = entry[i, j] - entry[i, p] * entry[j, p]
                row[i] = row[i] - entry[i, p] * row[p]
                if follows:
                    column[i] = column[i] - column[p] * entry[i, p]
            panel_buf[slot, p : p + 1, :] = row[p][:1]
        if follows:
            tiles[now + 1] = after
        done.append(jnp.where(lane < begin + tile, panel_buf[slot], 0.0))
        if now + 2 < count:
            solved = [None] * tile
            for p in range(tile - 1, -1, -1):
                value = row[p]
                for i in range(p + 1, tile):
                    value = value - entry[i, p] * solved[i]
                solved[p] = value * scales[p]
            for t in range(now + 2, count):
                value = jnp.where(inside, 0.0, tiles[t])
                for p in range(tile):
                    value = value - full(tiles[t][:, begin + p : begin + p + 1]) * solved[p]
                tiles[t] = value
    return jnp.concatenate(done, axis=0)


def full_dot(left, right, left_dim, right_dim):
    a, b, c = split_parts(left)
    d, e, f = split_parts(right)
    return lax.dot_general(
        jnp.concatenate([a, a, b, a, c, b], axis=left_dim),
        jnp.concatenate([d, e, d, f, d, e], axis=right_dim),
        (((left_dim,), (right_dim,)), ((), ())),
        preferred_element_type=jnp.float32,
    )


def along_z(own, shifted):
    total = 3.0 * stencil_coeffs[0] * own
    for m in range(1, 7):
        total = total + stencil_coeffs[m] * (pltpu.roll(own, m, 2) + pltpu.roll(own, 128 - m, 2))
    return shifted * own - 0.5 / spacing**2 * total


def along_x(wide, at):
    total = stencil_coeffs[1] * (wide[7 + at] + wide[5 + at])
    for m in range(2, 7):
        total = total + stencil_coeffs[m] * (wide[6 + at + m] + wide[6 + at - m])
    return -0.5 / spacing**2 * total


def along_y(own, around):
    column = jnp.concatenate([around, own, around], axis=0)
    total = stencil_coeffs[1] * (column[9:17] + column[7:15])
    for m in range(2, 7):
        total = total + stencil_coeffs[m] * (column[8 + m : 16 + m] + column[8 - m : 16 - m])
    return -0.5 / spacing**2 * total


def filter_rotate_kernel(
    cells,
    orbitals_hbm,
    potential_hbm,
    rotated_hbm,
    gram_hbm,
    orbitals_ref,
    potential_ref,
    gram_rows,
    gram,
    share,
    inverse,
    rows_buf,
    cols_buf,
    panel_buf,
    parcels,
    arrived,
    mine_ref,
    outgoing,
    halos,
    base,
    slope,
    inner,
    shares,
    partial,
    pieces,
    piece,
    layers,
    total,
    blocks,
    halo_send,
    halo_recv,
    send_sem,
    recv_sem,
    local_sem,
    tokens,
):
    load_orbitals = pltpu.make_async_copy(orbitals_hbm, orbitals_ref, local_sem.at[0])
    load_orbitals.start()
    load_potential = pltpu.make_async_copy(potential_hbm, potential_ref, local_sem.at[1])
    load_potential.start()
    band = lax.axis_index("band")
    layer = band % LAYERS
    across = lax.axis_index("gx")
    half_y = lax.axis_index("gy")
    row = (band // LAYERS) * 2 + half_y
    place = across * GRID_Y + row
    owns = band % 4 != 3

    def holds_piece(spot_x, spot_y):
        return (spot_x + spot_y) % 4 != 3

    def piece_of(spot_x, spot_y):
        return spot_x * 3 + (spot_x + spot_y) % 4

    holds = holds_piece(across, row)
    own_piece = piece_of(across, row)

    def near(step_x, step_y, step_z):
        return spot(
            (across + step_x) % GRID_X, (row + step_y) % GRID_Y, (layer + step_z) % LAYERS
        )

    barrier = pltpu.get_barrier_semaphore()
    greeted = [near(0, 0, step) for step in (3, -3, 2, -2, 1, -1)]
    greeted += [near(0, side, step) for step in (2, -2, 1, -1, 0) for side in (1, 3)]
    greeted += [near(1, 0, 0), near(-1, 0, 0)]
    for device in greeted:
        pl.semaphore_signal(barrier, 1, device_id=device, device_id_type=MESH)

    def send_tokens(kind, devices):
        for device in devices:
            pl.semaphore_signal(tokens.at[kind], 1, device_id=device, device_id_type=MESH)

    def turn(at, carry):
        plane = jnp.swapaxes(orbitals_ref[:, at], 0, 1)
        base[6 + at] = plane
        rows_at = pl.ds(pl.multiple_of(at * 64, 64), 64)
        outgoing[0, rows_at] = plane.reshape(64, 128).astype(jnp.bfloat16)
        return carry

    load_orbitals.wait()
    lax.fori_loop(0, 6, turn, 0, unroll=2)
    load_potential.wait()
    pl.semaphore_wait(barrier, len(greeted))
    send_tokens(0, (near(0, 0, 3), near(0, 0, -3)))

    sides = (near(1, 0, 0), near(-1, 0, 0), {"gy": 1 - half_y})

    def halo_copy(turn_at, side):
        return pltpu.make_async_remote_copy(
            src_ref=outgoing.at[turn_at],
            dst_ref=halos.at[turn_at, side],
            send_sem=halo_send.at[turn_at, side],
            recv_sem=halo_recv.at[turn_at, side],
            device_id=sides[side],
            device_id_type=MESH,
        )

    def block_rows(at):
        return pl.ds(pl.multiple_of(at * 64, 64), 64)

    def inner_part(wide):
        def fill(at, carry):
            inner[at] = along_z(wide[6 + at], (potential_ref[at] - center)[:, None, :])
            return carry

        lax.fori_loop(0, 6, fill, 0, unroll=2)

    def halo_take(turn_at, wide):
        for side in range(2):
            halo_copy(turn_at, side).wait_recv()

        def widen(at, carry):
            for side in range(2):
                block = halos[turn_at, side, block_rows(at)]
                wide[12 * side + at] = block.astype(jnp.float32).reshape(8, 8, 128)
            return carry

        lax.fori_loop(0, 6, widen, 0, unroll=2)

        def add_x(at, carry):
            inner[at] = inner[at] + along_x(wide, at)
            return carry

        lax.fori_loop(0, 6, add_x, 0, unroll=2)
        halo_copy(turn_at, 2).wait_recv()

    def shifted_ham(turn_at, wide, at):
        around = halos[turn_at, 2, block_rows(at)].astype(jnp.float32).reshape(8, 8, 128)
        return inner[at] + along_y(wide[6 + at], around)

    half, center, sigma, sigma_two = filter_scalars()
    for side in (2, 0, 1):
        halo_copy(0, side).start()
    inner_part(base)
    halo_take(0, base)
    pl.semaphore_wait(tokens.at[0], 2)
    send_tokens(1, (near(0, 0, 5), near(0, 0, -5)))

    def first_step(at, carry):
        result = sigma / half * shifted_ham(0, base, at)
        slope[6 + at] = result
        outgoing[1, block_rows(at)] = result.reshape(64, 128).astype(jnp.bfloat16)
        return carry

    lax.fori_loop(0, 6, first_step, 0, unroll=2)
    for side in (2, 0, 1):
        halo_copy(1, side).start()
    inner_part(slope)
    halo_take(1, slope)
    send_tokens(2, (near(3, 0, 0), near(-3, 0, 0)))

    def second_step(at, carry):
        result = 2.0 * sigma_two / half * shifted_ham(1, slope, at)
        result = result - sigma * sigma_two * base[6 + at]
        mine_ref[block_rows(at)] = result.reshape(64, 128).astype(jnp.bfloat16)
        return carry

    lax.fori_loop(0, 6, second_step, 0, unroll=2)

    def remote(source, target, phase, device):
        return pltpu.make_async_remote_copy(
            src_ref=source,
            dst_ref=target,
            send_sem=send_sem.at[phase],
            recv_sem=recv_sem.at[phase],
            device_id=device,
            device_id_type=MESH,
        )

    def cell_share(step, carry):
        to_row = (row + 1 + 2 * (step % 2)) % GRID_Y
        to_layer = (layer + far_first(step // 2, LAYERS)) % LAYERS
        other = (to_row // 2) * LAYERS + to_layer

        @pl.when(other % 4 != 3)
        def _():
            at = pl.multiple_of(band_share(other) * 16, 16)
            to = pl.multiple_of(band * 16, 16)
            remote(
                mine_ref.at[pl.ds(at, 16)],
                shares.at[pl.ds(to, 16)],
                0,
                {"band": other, "gy": 1 - half_y},
            ).start()

        return carry

    pl.semaphore_wait(tokens.at[1], 2)
    lax.fori_loop(0, BANDS, cell_share, 0)
    pl.semaphore_wait(tokens.at[2], 2)

    @pl.when(owns)
    def _():
        await_arrivals(shares, recv_sem.at[0])
        spread = shares[...].astype(jnp.float32).reshape(BANDS, 2, 8, 128)
        halves = [spread[:, half].reshape(FULL, 128) for half in range(2)]
        both = jnp.concatenate(halves, axis=1).astype(jnp.bfloat16)
        share[...] = both
        first = lax.dot_general(
            both[:128], both[:128], (((1,), (1,)), ((), ())), preferred_element_type=jnp.float32
        )
        second = lax.dot_general(
            both[128:], both, (((1,), (1,)), ((), ())), preferred_element_type=jnp.float32
        )
        blocked = jnp.concatenate([first, second[:, :128], second[:, 128:]], axis=0)
        partial[...] = blocked.astype(jnp.bfloat16).reshape(HOLDERS, 16, 128)

        def send_piece(step, carry):
            other = plane_partner(place, step)
            other_x, other_y = other // GRID_Y, other % GRID_Y

            @pl.when(holds_piece(other_x, other_y))
            def _():
                remote(
                    partial.at[piece_of(other_x, other_y)],
                    pieces.at[place],
                    1,
                    spot(other_x, other_y, layer),
                ).start()

            return carry

        lax.fori_loop(0, PLANE - 1, send_piece, 0)

    @pl.when(owns & holds)
    def _():
        pieces[place] = partial[own_piece]
        await_arrivals(pieces.at[pl.ds(0, PLANE - 1)], recv_sem.at[1])
        piece[...] = jnp.sum(pieces[...].astype(jnp.float32), axis=0).astype(jnp.bfloat16)
        at_layer = band_share(layer)

        def send_layer(step, carry):
            remote(
                piece,
                layers.at[at_layer],
                2,
                spot(across, row, (layer + far_first(step, LAYERS)) % LAYERS),
            ).start()
            return carry

        lax.fori_loop(0, LAYERS - 1, send_layer, 0)
        layers[at_layer] = piece[...]
        await_arrivals(layers.at[pl.ds(0, SENDERS - 1)], recv_sem.at[2])

    @pl.when(jnp.logical_not(owns) & holds)
    def _():
        await_arrivals(layers, recv_sem.at[2])

    @pl.when(holds)
    def _():
        total[...] = jnp.sum(layers[...].astype(jnp.float32), axis=0) / cells

        def send_total(step, carry):
            other = plane_partner(place, step)
            remote(
                total, blocks.at[own_piece], 3, spot(other // GRID_Y, other % GRID_Y, layer)
            ).start()
            return carry

        lax.fori_loop(0, PLANE - 1, send_total, 0)
        blocks[own_piece] = total[...]
        await_arrivals(blocks.at[pl.ds(0, HOLDERS - 1)], recv_sem.at[3])

    @pl.when(jnp.logical_not(holds))
    def _():
        await_arrivals(blocks.at[pl.ds(0, HOLDERS)], recv_sem.at[3])

    @pl.when(owns)
    def _():
        to = pl.multiple_of(band_share(band) * 16, 16)

        def send_parcels(side, weights, cells_of):
            turned = jnp.dot(weights, cells_of, preferred_element_type=jnp.float32)
            halves = [
                turned[:, 128 * h : 128 * h + 128].reshape(LAYERS, 1, 8, 128) for h in range(2)
            ]
            base_row = side * LAYERS * 16
            parcels[base_row : base_row + LAYERS * 16] = (
                jnp.concatenate(halves, axis=1).reshape(LAYERS * 16, 128).astype(jnp.bfloat16)
            )

            def send_parcel(step, carry):
                other = side * LAYERS + (layer + far_first(step, LAYERS)) % LAYERS
                at = pl.multiple_of(other * 16, 16)
                remote(
                    parcels.at[pl.ds(at, 16)],
                    arrived.at[pl.ds(to, 16)],
                    4,
                    {"band": other, "gy": 1 - half_y},
                ).start()
                return carry

            lax.fori_loop(0, LAYERS, send_parcel, 0)

        buffers = (rows_buf, cols_buf, panel_buf)
        corner = blocks[8:16].reshape(128, 128)
        upper = inverse_factor(blocks[0:8].reshape(128, 128), *buffers)
        send_parcels(0, upper.astype(jnp.bfloat16), share[:128])
        lower_left = full_dot(corner, upper, 1, 1)
        remaining = blocks[16:24].reshape(128, 128) - full_dot(lower_left, lower_left, 1, 1)
        carried = full_dot(lower_left, upper, 1, 0)
        lower = inverse_factor(remaining, *buffers)
        inverse[:, 128:] = lower.astype(jnp.bfloat16)
        inverse[:, :128] = (-full_dot(lower, carried, 1, 0)).astype(jnp.bfloat16)
        send_parcels(1, inverse[...], share[...])

    middle_block = blocks[8:16].reshape(128, 128)
    gram[:128, :128] = blocks[0:8].reshape(128, 128)
    gram[:128, 128:] = middle_block.T
    gram[128:, :128] = middle_block
    gram[128:, 128:] = blocks[16:24].reshape(128, 128)
    gram_rows[...] = gram[pl.ds(pl.multiple_of(band * 8, 8), 8), :]
    store_gram = pltpu.make_async_copy(gram_rows, gram_hbm, local_sem.at[2])
    store_gram.start()

    @pl.when(owns & holds)
    def _():
        await_arrivals(partial.at[pl.ds(0, HOLDERS - 1)], send_sem.at[1])
        await_arrivals(pieces.at[pl.ds(0, LAYERS - 1)], send_sem.at[2])

    @pl.when(owns & jnp.logical_not(holds))
    def _():
        await_arrivals(partial, send_sem.at[1])

    await_arrivals(mine_ref, send_sem.at[0])
    for turn_at in range(2):
        for side in range(3):
            halo_copy(turn_at, side).wait_send()

    @pl.when(holds)
    def _():
        await_arrivals(blocks.at[pl.ds(0, PLANE - 1)], send_sem.at[3])

    @pl.when(owns)
    def _():
        await_arrivals(parcels, send_sem.at[4])

    await_arrivals(arrived, recv_sem.at[4])
    store_rotated = pltpu.make_async_copy(arrived, rotated_hbm, local_sem.at[3])
    store_rotated.start()
    store_gram.wait()
    store_rotated.wait()


def filter_rotate(orbitals, potential, cells):
    return pl.pallas_call(
        functools.partial(filter_rotate_kernel, cells),
        out_shape=(
            jax.ShapeDtypeStruct((OWNERS * 16, 128), jnp.bfloat16),
            jax.ShapeDtypeStruct((8, FULL), jnp.float32),
        ),
        in_specs=[pl.BlockSpec(memory_space=pl.ANY)] * 2,
        out_specs=(pl.BlockSpec(memory_space=pl.ANY),) * 2,
        scratch_shapes=[
            pltpu.VMEM((8, 6, 8, 128), jnp.float32),
            pltpu.VMEM((6, 8, 128), jnp.float32),
            pltpu.VMEM((8, FULL), jnp.float32),
            pltpu.VMEM((FULL, FULL), jnp.float32),
            pltpu.VMEM((FULL, FULL), jnp.bfloat16),
            pltpu.VMEM((128, FULL), jnp.bfloat16),
            pltpu.VMEM((2, 8, 128), jnp.float32),
            pltpu.VMEM((2, 8, 8, 128), jnp.float32),
            pltpu.VMEM((2, 8, 128), jnp.float32),
            pltpu.VMEM((BANDS * 16, 128), jnp.bfloat16),
            pltpu.VMEM((OWNERS * 16, 128), jnp.bfloat16),
            pltpu.VMEM((384, 128), jnp.bfloat16),
            pltpu.VMEM((2, 384, 128), jnp.bfloat16),
            pltpu.VMEM((2, 3, 384, 128), jnp.bfloat16),
            pltpu.VMEM((18, 8, 8, 128), jnp.float32),
            pltpu.VMEM((18, 8, 8, 128), jnp.float32),
            pltpu.VMEM((6, 8, 8, 128), jnp.float32),
            pltpu.VMEM((BANDS * 16, 128), jnp.bfloat16),
            pltpu.VMEM((HOLDERS, 16, 128), jnp.bfloat16),
            pltpu.VMEM((PLANE, 16, 128), jnp.bfloat16),
            pltpu.VMEM((16, 128), jnp.bfloat16),
            pltpu.VMEM((SENDERS, 16, 128), jnp.bfloat16),
            pltpu.VMEM((16, 128), jnp.float32),
            pltpu.VMEM((PLANE, 16, 128), jnp.float32),
            pltpu.SemaphoreType.DMA((2, 3)),
            pltpu.SemaphoreType.DMA((2, 3)),
            pltpu.SemaphoreType.DMA((5,)),
            pltpu.SemaphoreType.DMA((5,)),
            pltpu.SemaphoreType.DMA((4,)),
            pltpu.SemaphoreType.REGULAR((3,)),
        ],
        compiler_params=pltpu.CompilerParams(collective_id=1, has_side_effects=True),
        name="filter_rotate",
    )(orbitals, potential)


def body(orbitals, potential):
    count, size_x, size_y, size_z = orbitals.shape
    total_cells = size_x * size_y * size_z * lax.axis_size("gx") * lax.axis_size("gy")
    tiles, gram_rows = filter_rotate(orbitals, potential, float(total_cells))
    rotated = tiles.astype(jnp.float32).reshape(size_x, size_y, count, size_z).transpose(2, 0, 1, 3)
    return (rotated, gram_rows)


def solution(mesh):
    return jax.shard_map(
        body,
        mesh=mesh,
        in_specs=(P("band", "gx", "gy", None), P("gx", "gy", None)),
        out_specs=(P("band", "gx", "gy", None), P("band", None)),
        check_vma=False,
    )
```

```python
import functools

import jax
import jax.numpy as jnp
from jax import lax
from jax.experimental import pallas as pl
from jax.experimental.pallas import tpu as pltpu
from jax.sharding import PartitionSpec as P

stencil_coeffs = (
    -5369.0 / 1800.0,
    12.0 / 7.0,
    -15.0 / 56.0,
    10.0 / 189.0,
    -1.0 / 112.0,
    2.0 / 1925.0,
    -1.0 / 16632.0,
)
spacing = 0.5
low_edge = 5.0
high_edge = 46.0
bottom_edge = -6.5


def filter_scalars():
    half = (high_edge - low_edge) / 2.0
    center = (high_edge + low_edge) / 2.0
    sigma = half / (bottom_edge - center)
    sigma_two = 1.0 / (2.0 / sigma - sigma)
    return (half, center, sigma, sigma_two)


MESH = pl.DeviceIdType.MESH
BANDS = 32
OWNERS = 24
LAYERS = 16
SENDERS = 12
PLANE = 32
HOLDERS = 24
GRID_X = 8
GRID_Y = 4
FULL = 256


def owner_band(share):
    return (share // 3) * 4 + share % 3


def band_share(band):
    return (band // 4) * 3 + band % 4


def far_first(step, count):
    reach = (step + 1) // 2
    return count // 2 + reach * (2 * (step % 2) - 1)


def spot(across, row, layer):
    return {"band": (row // 2) * LAYERS + layer, "gx": across, "gy": row % 2}


def plane_partner(place, step):
    across = (place // GRID_Y + far_first(step // GRID_Y, GRID_X)) % GRID_X
    return across * GRID_Y + (place + far_first(step % GRID_Y, GRID_Y)) % GRID_Y


def await_arrivals(buffer, sem):
    pltpu.make_async_copy(buffer, buffer, sem).wait()


def split_parts(value):
    high = value.astype(jnp.bfloat16)
    rest = value - high.astype(jnp.float32)
    middle = rest.astype(jnp.bfloat16)
    return high, middle, (rest - middle.astype(jnp.float32)).astype(jnp.bfloat16)


def inverse_factor(matrix, rows_buf, cols_buf, panel_buf):
    tile, size = 8, 128
    count = size // tile
    lane = lax.broadcasted_iota(jnp.int32, (tile, size), 1)

    def full(value):
        return jnp.broadcast_to(value, (tile, size))

    tiles = [matrix[tile * t : tile * t + tile] for t in range(count)]
    done = []
    for now in range(count):
        begin, slot = tile * now, now % 2
        head = tiles[now]
        rows_buf[slot] = head
        for j in range(tile):
            cols_buf[slot, j] = full(head[:, begin + j : begin + j + 1])
        inside = (lane >= begin) & (lane < begin + tile)
        entry = {
            (i, j): full(cols_buf[slot, j, i : i + 1, :])
            for j in range(tile)
            for i in range(j, tile)
        }
        row = [
            jnp.where(
                inside,
                (lane == begin + i).astype(jnp.float32),
                full(rows_buf[slot, i : i + 1, :]),
            )
            for i in range(tile)
        ]
        follows = now + 1 < count
        if follows:
            after = tiles[now + 1]
            column = [full(after[:, begin + p : begin + p + 1]) for p in range(tile)]
            after = jnp.where(inside, 0.0, after)
        scales = []
        for p in range(tile):
            scale = lax.rsqrt(entry[p, p])
            scales.append(scale)
            for i in range(p + 1, tile):
                entry[i, p] = entry[i, p] * scale
            row[p] = row[p] * scale
            if follows:
                column[p] = column[p] * scale
                after = after - column[p] * row[p]
            for i in range(p + 1, tile):
                for j in range(p + 1, i + 1):
                    entry[i, j] = entry[i, j] - entry[i, p] * entry[j, p]
                row[i] = row[i] - entry[i, p] * row[p]
                if follows:
                    column[i] = column[i] - column[p] * entry[i, p]
            panel_buf[slot, p : p + 1, :] = row[p][:1]
        if follows:
            tiles[now + 1] = after
        done.append(jnp.where(lane < begin + tile, panel_buf[slot], 0.0))
        if now + 2 < count:
            solved = [None] * tile
            for p in range(tile - 1, -1, -1):
                value = row[p]
                for i in range(p + 1, tile):
                    value = value - entry[i, p] * solved[i]
                solved[p] = value * scales[p]
            for t in range(now + 2, count):
                value = jnp.where(inside, 0.0, tiles[t])
                for p in range(tile):
                    value = value - full(tiles[t][:, begin + p : begin + p + 1]) * solved[p]
                tiles[t] = value
    return jnp.concatenate(done, axis=0)


def full_dot(left, right, left_dim, right_dim):
    a, b, c = split_parts(left)
    d, e, f = split_parts(right)
    return lax.dot_general(
        jnp.concatenate([a, a, b, a, c, b], axis=left_dim),
        jnp.concatenate([d, e, d, f, d, e], axis=right_dim),
        (((left_dim,), (right_dim,)), ((), ())),
        preferred_element_type=jnp.float32,
    )


def along_z(own, shifted):
    total = 3.0 * stencil_coeffs[0] * own
    for m in range(1, 7):
        total = total + stencil_coeffs[m] * (pltpu.roll(own, m, 2) + pltpu.roll(own, 128 - m, 2))
    return shifted * own - 0.5 / spacing**2 * total


def along_x(wide, at):
    total = stencil_coeffs[1] * (wide[7 + at] + wide[5 + at])
    for m in range(2, 7):
        total = total + stencil_coeffs[m] * (wide[6 + at + m] + wide[6 + at - m])
    return -0.5 / spacing**2 * total


def along_y(own, around):
    column = jnp.concatenate([around, own, around], axis=0)
    total = stencil_coeffs[1] * (column[9:17] + column[7:15])
    for m in range(2, 7):
        total = total + stencil_coeffs[m] * (column[8 + m : 16 + m] + column[8 - m : 16 - m])
    return -0.5 / spacing**2 * total


def filter_rotate_kernel(
    cells,
    orbitals_hbm,
    potential_hbm,
    rotated_hbm,
    gram_hbm,
    orbitals_ref,
    potential_ref,
    gram_rows,
    gram,
    share,
    inverse,
    rows_buf,
    cols_buf,
    panel_buf,
    parcels,
    arrived,
    mine_ref,
    outgoing,
    halos,
    base,
    slope,
    inner,
    shares,
    partial,
    pieces,
    piece,
    layers,
    total,
    blocks,
    halo_send,
    halo_recv,
    send_sem,
    recv_sem,
    local_sem,
    tokens,
):
    load_orbitals = pltpu.make_async_copy(orbitals_hbm, orbitals_ref, local_sem.at[0])
    load_orbitals.start()
    load_potential = pltpu.make_async_copy(potential_hbm, potential_ref, local_sem.at[1])
    load_potential.start()
    band = lax.axis_index("band")
    layer = band % LAYERS
    across = lax.axis_index("gx")
    half_y = lax.axis_index("gy")
    row = (band // LAYERS) * 2 + half_y
    place = across * GRID_Y + row
    owns = band % 4 != 3

    def holds_piece(spot_x, spot_y):
        return (spot_x + spot_y) % 4 != 3

    def piece_of(spot_x, spot_y):
        return spot_x * 3 + (spot_x + spot_y) % 4

    holds = holds_piece(across, row)
    own_piece = piece_of(across, row)

    def near(step_x, step_y, step_z):
        return spot(
            (across + step_x) % GRID_X, (row + step_y) % GRID_Y, (layer + step_z) % LAYERS
        )

    barrier = pltpu.get_barrier_semaphore()
    greeted = [near(0, 0, step) for step in (3, -3, 2, -2, 1, -1)]
    greeted += [near(0, side, step) for step in (2, -2, 1, -1, 0) for side in (1, 3)]
    greeted += [near(1, 0, 0), near(-1, 0, 0)]
    for device in greeted:
        pl.semaphore_signal(barrier, 1, device_id=device, device_id_type=MESH)

    def send_tokens(kind, devices):
        for device in devices:
            pl.semaphore_signal(tokens.at[kind], 1, device_id=device, device_id_type=MESH)

    def turn(at, carry):
        plane = jnp.swapaxes(orbitals_ref[:, at], 0, 1)
        base[6 + at] = plane
        rows_at = pl.ds(pl.multiple_of(at * 64, 64), 64)
        outgoing[0, rows_at] = plane.reshape(64, 128).astype(jnp.bfloat16)
        return carry

    load_orbitals.wait()
    lax.fori_loop(0, 6, turn, 0, unroll=2)
    load_potential.wait()
    pl.semaphore_wait(barrier, len(greeted))
    send_tokens(0, (near(0, 0, 3), near(0, 0, -3)))

    sides = (near(1, 0, 0), near(-1, 0, 0), {"gy": 1 - half_y})

    def halo_copy(turn_at, side):
        return pltpu.make_async_remote_copy(
            src_ref=outgoing.at[turn_at],
            dst_ref=halos.at[turn_at, side],
            send_sem=halo_send.at[turn_at, side],
            recv_sem=halo_recv.at[turn_at, side],
            device_id=sides[side],
            device_id_type=MESH,
        )

    def block_rows(at):
        return pl.ds(pl.multiple_of(at * 64, 64), 64)

    def inner_part(wide):
        def fill(at, carry):
            inner[at] = along_z(wide[6 + at], (potential_ref[at] - center)[:, None, :])
            return carry

        lax.fori_loop(0, 6, fill, 0, unroll=2)

    def halo_take(turn_at, wide):
        for side in range(2):
            halo_copy(turn_at, side).wait_recv()

        def widen(at, carry):
            for side in range(2):
                block = halos[turn_at, side, block_rows(at)]
                wide[12 * side + at] = block.astype(jnp.float32).reshape(8, 8, 128)
            return carry

        lax.fori_loop(0, 6, widen, 0, unroll=2)

        def add_x(at, carry):
            inner[at] = inner[at] + along_x(wide, at)
            return carry

        lax.fori_loop(0, 6, add_x, 0, unroll=2)
        halo_copy(turn_at, 2).wait_recv()

    def shifted_ham(turn_at, wide, at):
        around = halos[turn_at, 2, block_rows(at)].astype(jnp.float32).reshape(8, 8, 128)
        return inner[at] + along_y(wide[6 + at], around)

    half, center, sigma, sigma_two = filter_scalars()
    for side in (2, 0, 1):
        halo_copy(0, side).start()
    inner_part(base)
    halo_take(0, base)
    pl.semaphore_wait(tokens.at[0], 2)
    send_tokens(1, (near(0, 0, 5), near(0, 0, -5)))

    def first_step(at, carry):
        result = sigma / half * shifted_ham(0, base, at)
        slope[6 + at] = result
        outgoing[1, block_rows(at)] = result.reshape(64, 128).astype(jnp.bfloat16)
        return carry

    lax.fori_loop(0, 6, first_step, 0, unroll=2)
    for side in (2, 0, 1):
        halo_copy(1, side).start()
    inner_part(slope)
    halo_take(1, slope)
    send_tokens(2, (near(3, 0, 0), near(-3, 0, 0)))

    def second_step(at, carry):
        result = 2.0 * sigma_two / half * shifted_ham(1, slope, at)
        result = result - sigma * sigma_two * base[6 + at]
        mine_ref[block_rows(at)] = result.reshape(64, 128).astype(jnp.bfloat16)
        return carry

    lax.fori_loop(0, 6, second_step, 0, unroll=2)

    def remote(source, target, phase, device):
        return pltpu.make_async_remote_copy(
            src_ref=source,
            dst_ref=target,
            send_sem=send_sem.at[phase],
            recv_sem=recv_sem.at[phase],
            device_id=device,
            device_id_type=MESH,
        )

    def cell_share(step, carry):
        to_row = (row + 1 + 2 * (step % 2)) % GRID_Y
        to_layer = (layer + far_first(step // 2, LAYERS)) % LAYERS
        other = (to_row // 2) * LAYERS + to_layer

        @pl.when(other % 4 != 3)
        def _():
            at = pl.multiple_of(band_share(other) * 16, 16)
            to = pl.multiple_of(band * 16, 16)
            remote(
                mine_ref.at[pl.ds(at, 16)],
                shares.at[pl.ds(to, 16)],
                0,
                {"band": other, "gy": 1 - half_y},
            ).start()

        return carry

    pl.semaphore_wait(tokens.at[1], 2)
    lax.fori_loop(0, BANDS, cell_share, 0)
    pl.semaphore_wait(tokens.at[2], 2)

    @pl.when(owns)
    def _():
        await_arrivals(shares, recv_sem.at[0])
        spread = shares[...].astype(jnp.float32).reshape(BANDS, 2, 8, 128)
        halves = [spread[:, half].reshape(FULL, 128) for half in range(2)]
        both = jnp.concatenate(halves, axis=1).astype(jnp.bfloat16)
        share[...] = both
        first = lax.dot_general(
            both[:128], both[:128], (((1,), (1,)), ((), ())), preferred_element_type=jnp.float32
        )
        second = lax.dot_general(
            both[128:], both, (((1,), (1,)), ((), ())), preferred_element_type=jnp.float32
        )
        blocked = jnp.concatenate([first, second[:, :128], second[:, 128:]], axis=0)
        partial[...] = blocked.astype(jnp.bfloat16).reshape(HOLDERS, 16, 128)

        def send_piece(step, carry):
            other = plane_partner(place, step)
            other_x, other_y = other // GRID_Y, other % GRID_Y

            @pl.when(holds_piece(other_x, other_y))
            def _():
                remote(
                    partial.at[piece_of(other_x, other_y)],
                    pieces.at[place],
                    1,
                    spot(other_x, other_y, layer),
                ).start()

            return carry

        lax.fori_loop(0, PLANE - 1, send_piece, 0)

    @pl.when(owns & holds)
    def _():
        pieces[place] = partial[own_piece]
        await_arrivals(pieces.at[pl.ds(0, PLANE - 1)], recv_sem.at[1])
        piece[...] = jnp.sum(pieces[...].astype(jnp.float32), axis=0).astype(jnp.bfloat16)
        at_layer = band_share(layer)

        def send_layer(step, carry):
            remote(
                piece,
                layers.at[at_layer],
                2,
                spot(across, row, (layer + far_first(step, LAYERS)) % LAYERS),
            ).start()
            return carry

        lax.fori_loop(0, LAYERS - 1, send_layer, 0)
        layers[at_layer] = piece[...]
        await_arrivals(layers.at[pl.ds(0, SENDERS - 1)], recv_sem.at[2])

    @pl.when(jnp.logical_not(owns) & holds)
    def _():
        await_arrivals(layers, recv_sem.at[2])

    @pl.when(holds)
    def _():
        total[...] = jnp.sum(layers[...].astype(jnp.float32), axis=0) / cells

        def send_total(step, carry):
            other = plane_partner(place, step)
            remote(
                total, blocks.at[own_piece], 3, spot(other // GRID_Y, other % GRID_Y, layer)
            ).start()
            return carry

        lax.fori_loop(0, PLANE - 1, send_total, 0)
        blocks[own_piece] = total[...]
        await_arrivals(blocks.at[pl.ds(0, HOLDERS - 1)], recv_sem.at[3])

    @pl.when(jnp.logical_not(holds))
    def _():
        await_arrivals(blocks.at[pl.ds(0, HOLDERS)], recv_sem.at[3])

    @pl.when(owns)
    def _():
        to = pl.multiple_of(band_share(band) * 16, 16)

        def send_parcels(side, weights, cells_of):
            turned = jnp.dot(weights, cells_of, preferred_element_type=jnp.float32)
            halves = [
                turned[:, 128 * h : 128 * h + 128].reshape(LAYERS, 1, 8, 128) for h in range(2)
            ]
            base_row = side * LAYERS * 16
            parcels[base_row : base_row + LAYERS * 16] = (
                jnp.concatenate(halves, axis=1).reshape(LAYERS * 16, 128).astype(jnp.bfloat16)
            )

            def send_parcel(step, carry):
                other = side * LAYERS + (layer + far_first(step, LAYERS)) % LAYERS
                at = pl.multiple_of(other * 16, 16)
                remote(
                    parcels.at[pl.ds(at, 16)],
                    arrived.at[pl.ds(to, 16)],
                    4,
                    {"band": other, "gy": 1 - half_y},
                ).start()
                return carry

            lax.fori_loop(0, LAYERS, send_parcel, 0)

        buffers = (rows_buf, cols_buf, panel_buf)
        corner = blocks[8:16].reshape(128, 128)
        upper = inverse_factor(blocks[0:8].reshape(128, 128), *buffers)
        send_parcels(0, upper.astype(jnp.bfloat16), share[:128])
        lower_left = full_dot(corner, upper, 1, 1)
        remaining = blocks[16:24].reshape(128, 128) - full_dot(lower_left, lower_left, 1, 1)
        carried = full_dot(lower_left, upper, 1, 0)
        lower = inverse_factor(remaining, *buffers)
        inverse[:, 128:] = lower.astype(jnp.bfloat16)
        inverse[:, :128] = (-full_dot(lower, carried, 1, 0)).astype(jnp.bfloat16)
        send_parcels(1, inverse[...], share[...])

    middle_block = blocks[8:16].reshape(128, 128)
    gram[:128, :128] = blocks[0:8].reshape(128, 128)
    gram[:128, 128:] = middle_block.T
    gram[128:, :128] = middle_block
    gram[128:, 128:] = blocks[16:24].reshape(128, 128)
    gram_rows[...] = gram[pl.ds(pl.multiple_of(band * 8, 8), 8), :]
    store_gram = pltpu.make_async_copy(gram_rows, gram_hbm, local_sem.at[2])
    store_gram.start()

    @pl.when(owns & holds)
    def _():
        await_arrivals(partial.at[pl.ds(0, HOLDERS - 1)], send_sem.at[1])
        await_arrivals(pieces.at[pl.ds(0, LAYERS - 1)], send_sem.at[2])

    @pl.when(owns & jnp.logical_not(holds))
    def _():
        await_arrivals(partial, send_sem.at[1])

    await_arrivals(mine_ref, send_sem.at[0])
    for turn_at in range(2):
        for side in range(3):
            halo_copy(turn_at, side).wait_send()

    @pl.when(holds)
    def _():
        await_arrivals(blocks.at[pl.ds(0, PLANE - 1)], send_sem.at[3])

    @pl.when(owns)
    def _():
        await_arrivals(parcels, send_sem.at[4])

    await_arrivals(arrived, recv_sem.at[4])
    store_rotated = pltpu.make_async_copy(arrived, rotated_hbm, local_sem.at[3])
    store_rotated.start()
    store_gram.wait()
    store_rotated.wait()


def filter_rotate(orbitals, potential, cells):
    return pl.pallas_call(
        functools.partial(filter_rotate_kernel, cells),
        out_shape=(
            jax.ShapeDtypeStruct((OWNERS * 16, 128), jnp.bfloat16),
            jax.ShapeDtypeStruct((8, FULL), jnp.float32),
        ),
        in_specs=[pl.BlockSpec(memory_space=pl.ANY)] * 2,
        out_specs=(pl.BlockSpec(memory_space=pl.ANY),) * 2,
        scratch_shapes=[
            pltpu.VMEM((8, 6, 8, 128), jnp.float32),
            pltpu.VMEM((6, 8, 128), jnp.float32),
            pltpu.VMEM((8, FULL), jnp.float32),
            pltpu.VMEM((FULL, FULL), jnp.float32),
            pltpu.VMEM((FULL, FULL), jnp.bfloat16),
            pltpu.VMEM((128, FULL), jnp.bfloat16),
            pltpu.VMEM((2, 8, 128), jnp.float32),
            pltpu.VMEM((2, 8, 8, 128), jnp.float32),
            pltpu.VMEM((2, 8, 128), jnp.float32),
            pltpu.VMEM((BANDS * 16, 128), jnp.bfloat16),
            pltpu.VMEM((OWNERS * 16, 128), jnp.bfloat16),
            pltpu.VMEM((384, 128), jnp.bfloat16),
            pltpu.VMEM((2, 384, 128), jnp.bfloat16),
            pltpu.VMEM((2, 3, 384, 128), jnp.bfloat16),
            pltpu.VMEM((18, 8, 8, 128), jnp.float32),
            pltpu.VMEM((18, 8, 8, 128), jnp.float32),
            pltpu.VMEM((6, 8, 8, 128), jnp.float32),
            pltpu.VMEM((BANDS * 16, 128), jnp.bfloat16),
            pltpu.VMEM((HOLDERS, 16, 128), jnp.bfloat16),
            pltpu.VMEM((PLANE, 16, 128), jnp.bfloat16),
            pltpu.VMEM((16, 128), jnp.bfloat16),
            pltpu.VMEM((SENDERS, 16, 128), jnp.bfloat16),
            pltpu.VMEM((16, 128), jnp.float32),
            pltpu.VMEM((PLANE, 16, 128), jnp.float32),
            pltpu.SemaphoreType.DMA((2, 3)),
            pltpu.SemaphoreType.DMA((2, 3)),
            pltpu.SemaphoreType.DMA((5,)),
            pltpu.SemaphoreType.DMA((5,)),
            pltpu.SemaphoreType.DMA((4,)),
            pltpu.SemaphoreType.REGULAR((3,)),
        ],
        compiler_params=pltpu.CompilerParams(collective_id=1, has_side_effects=True),
        name="filter_rotate",
    )(orbitals, potential)


def place_kernel(tiles_ref, rows_ref, rotated_ref, gram_ref):
    gram_ref[...] = rows_ref[...]
    for at in range(6):
        plane = tiles_ref[64 * at : 64 * at + 64].astype(jnp.float32).reshape(8, 8, 128)
        rotated_ref[:, at] = jnp.swapaxes(plane, 0, 1)


def place_outputs(tiles, rows, shape):
    return pl.pallas_call(
        place_kernel,
        out_shape=(
            jax.ShapeDtypeStruct(shape, jnp.float32),
            jax.ShapeDtypeStruct(rows.shape, jnp.float32),
        ),
        in_specs=[pl.BlockSpec(memory_space=pltpu.VMEM)] * 2,
        out_specs=(pl.BlockSpec(memory_space=pltpu.VMEM),) * 2,
        name="place_outputs",
    )(tiles, rows)


def body(orbitals, potential):
    count, size_x, size_y, size_z = orbitals.shape
    total_cells = size_x * size_y * size_z * lax.axis_size("gx") * lax.axis_size("gy")
    tiles, gram_rows = filter_rotate(orbitals, potential, float(total_cells))
    return place_outputs(tiles, gram_rows, orbitals.shape)


def solution(mesh):
    return jax.shard_map(
        body,
        mesh=mesh,
        in_specs=(P("band", "gx", "gy", None), P("gx", "gy", None)),
        out_specs=(P("band", "gx", "gy", None), P("band", None)),
        check_vma=False,
    )
```

```python
import functools

import jax
import jax.numpy as jnp
from jax import lax
from jax.experimental import pallas as pl
from jax.experimental.pallas import tpu as pltpu
from jax.sharding import PartitionSpec as P

stencil_coeffs = (
    -5369.0 / 1800.0,
    12.0 / 7.0,
    -15.0 / 56.0,
    10.0 / 189.0,
    -1.0 / 112.0,
    2.0 / 1925.0,
    -1.0 / 16632.0,
)
spacing = 0.5
low_edge = 5.0
high_edge = 46.0
bottom_edge = -6.5


def filter_scalars():
    half = (high_edge - low_edge) / 2.0
    center = (high_edge + low_edge) / 2.0
    sigma = half / (bottom_edge - center)
    sigma_two = 1.0 / (2.0 / sigma - sigma)
    return (half, center, sigma, sigma_two)


MESH = pl.DeviceIdType.MESH
BANDS = 32
OWNERS = 24
LAYERS = 16
SENDERS = 12
PLANE = 32
HOLDERS = 24
GRID_X = 8
GRID_Y = 4
FULL = 256


def owner_band(share):
    return (share // 3) * 4 + share % 3


def band_share(band):
    return (band // 4) * 3 + band % 4


def far_first(step, count):
    reach = (step + 1) // 2
    return count // 2 + reach * (2 * (step % 2) - 1)


def spot(across, row, layer):
    return {"band": (row // 2) * LAYERS + layer, "gx": across, "gy": row % 2}


def plane_partner(place, step):
    across = (place // GRID_Y + far_first(step // GRID_Y, GRID_X)) % GRID_X
    return across * GRID_Y + (place + far_first(step % GRID_Y, GRID_Y)) % GRID_Y


def await_arrivals(buffer, sem):
    pltpu.make_async_copy(buffer, buffer, sem).wait()


def split_parts(value):
    high = value.astype(jnp.bfloat16)
    rest = value - high.astype(jnp.float32)
    middle = rest.astype(jnp.bfloat16)
    return high, middle, (rest - middle.astype(jnp.float32)).astype(jnp.bfloat16)


def inverse_factor(matrix, rows_buf, cols_buf, panel_buf):
    tile, size = 8, 128
    count = size // tile
    lane = lax.broadcasted_iota(jnp.int32, (tile, size), 1)

    def full(value):
        return jnp.broadcast_to(value, (tile, size))

    tiles = [matrix[tile * t : tile * t + tile] for t in range(count)]
    done = []
    for now in range(count):
        begin, slot = tile * now, now % 2
        head = tiles[now]
        rows_buf[slot] = head
        for j in range(tile):
            cols_buf[slot, j] = full(head[:, begin + j : begin + j + 1])
        inside = (lane >= begin) & (lane < begin + tile)
        entry = {
            (i, j): full(cols_buf[slot, j, i : i + 1, :])
            for j in range(tile)
            for i in range(j, tile)
        }
        row = [
            jnp.where(
                inside,
                (lane == begin + i).astype(jnp.float32),
                full(rows_buf[slot, i : i + 1, :]),
            )
            for i in range(tile)
        ]
        follows = now + 1 < count
        if follows:
            after = tiles[now + 1]
            column = [full(after[:, begin + p : begin + p + 1]) for p in range(tile)]
            after = jnp.where(inside, 0.0, after)
        scales = []
        for p in range(tile):
            scale = lax.rsqrt(entry[p, p])
            scales.append(scale)
            for i in range(p + 1, tile):
                entry[i, p] = entry[i, p] * scale
            row[p] = row[p] * scale
            if follows:
                column[p] = column[p] * scale
                after = after - column[p] * row[p]
            for i in range(p + 1, tile):
                for j in range(p + 1, i + 1):
                    entry[i, j] = entry[i, j] - entry[i, p] * entry[j, p]
                row[i] = row[i] - entry[i, p] * row[p]
                if follows:
                    column[i] = column[i] - column[p] * entry[i, p]
            panel_buf[slot, p : p + 1, :] = row[p][:1]
        if follows:
            tiles[now + 1] = after
        done.append(jnp.where(lane < begin + tile, panel_buf[slot], 0.0))
        if now + 2 < count:
            solved = [None] * tile
            for p in range(tile - 1, -1, -1):
                value = row[p]
                for i in range(p + 1, tile):
                    value = value - entry[i, p] * solved[i]
                solved[p] = value * scales[p]
            for t in range(now + 2, count):
                value = jnp.where(inside, 0.0, tiles[t])
                for p in range(tile):
                    value = value - full(tiles[t][:, begin + p : begin + p + 1]) * solved[p]
                tiles[t] = value
    return jnp.concatenate(done, axis=0)


def full_dot(left, right, left_dim, right_dim):
    a, b, c = split_parts(left)
    d, e, f = split_parts(right)
    return lax.dot_general(
        jnp.concatenate([a, a, b, a, c, b], axis=left_dim),
        jnp.concatenate([d, e, d, f, d, e], axis=right_dim),
        (((left_dim,), (right_dim,)), ((), ())),
        preferred_element_type=jnp.float32,
    )


def along_z(own, shifted):
    total = 3.0 * stencil_coeffs[0] * own
    for m in range(1, 7):
        total = total + stencil_coeffs[m] * (pltpu.roll(own, m, 2) + pltpu.roll(own, 128 - m, 2))
    return shifted * own - 0.5 / spacing**2 * total


def along_x(wide, at):
    total = stencil_coeffs[1] * (wide[7 + at] + wide[5 + at])
    for m in range(2, 7):
        total = total + stencil_coeffs[m] * (wide[6 + at + m] + wide[6 + at - m])
    return -0.5 / spacing**2 * total


def along_y(own, around):
    column = jnp.concatenate([around, own, around], axis=0)
    total = stencil_coeffs[1] * (column[9:17] + column[7:15])
    for m in range(2, 7):
        total = total + stencil_coeffs[m] * (column[8 + m : 16 + m] + column[8 - m : 16 - m])
    return -0.5 / spacing**2 * total


def filter_rotate_kernel(
    cells,
    orbitals_hbm,
    potential_hbm,
    rotated_ref,
    gram_ref,
    orbitals_ref,
    potential_ref,
    gram,
    share,
    inverse,
    rows_buf,
    cols_buf,
    panel_buf,
    parcels,
    arrived,
    mine_ref,
    outgoing,
    halos,
    base,
    slope,
    inner,
    shares,
    partial,
    pieces,
    piece,
    layers,
    total,
    blocks,
    halo_send,
    halo_recv,
    send_sem,
    recv_sem,
    local_sem,
    tokens,
):
    load_orbitals = pltpu.make_async_copy(orbitals_hbm, orbitals_ref, local_sem.at[0])
    load_orbitals.start()
    load_potential = pltpu.make_async_copy(potential_hbm, potential_ref, local_sem.at[1])
    load_potential.start()
    band = lax.axis_index("band")
    layer = band % LAYERS
    across = lax.axis_index("gx")
    half_y = lax.axis_index("gy")
    row = (band // LAYERS) * 2 + half_y
    place = across * GRID_Y + row
    owns = band % 4 != 3

    def holds_piece(spot_x, spot_y):
        return (spot_x + spot_y) % 4 != 3

    def piece_of(spot_x, spot_y):
        return spot_x * 3 + (spot_x + spot_y) % 4

    holds = holds_piece(across, row)
    own_piece = piece_of(across, row)

    def near(step_x, step_y, step_z):
        return spot(
            (across + step_x) % GRID_X, (row + step_y) % GRID_Y, (layer + step_z) % LAYERS
        )

    barrier = pltpu.get_barrier_semaphore()
    greeted = [near(0, 0, step) for step in (3, -3, 2, -2, 1, -1)]
    greeted += [near(0, side, step) for step in (2, -2, 1, -1, 0) for side in (1, 3)]
    greeted += [near(1, 0, 0), near(-1, 0, 0)]
    for device in greeted:
        pl.semaphore_signal(barrier, 1, device_id=device, device_id_type=MESH)

    def send_tokens(kind, devices):
        for device in devices:
            pl.semaphore_signal(tokens.at[kind], 1, device_id=device, device_id_type=MESH)

    def turn(at, carry):
        plane = jnp.swapaxes(orbitals_ref[:, at], 0, 1)
        base[6 + at] = plane
        rows_at = pl.ds(pl.multiple_of(at * 64, 64), 64)
        outgoing[0, rows_at] = plane.reshape(64, 128).astype(jnp.bfloat16)
        return carry

    load_orbitals.wait()
    lax.fori_loop(0, 6, turn, 0, unroll=2)
    load_potential.wait()
    pl.semaphore_wait(barrier, len(greeted))
    send_tokens(0, (near(0, 0, 3), near(0, 0, -3)))

    sides = (near(1, 0, 0), near(-1, 0, 0), {"gy": 1 - half_y})

    def halo_copy(turn_at, side):
        return pltpu.make_async_remote_copy(
            src_ref=outgoing.at[turn_at],
            dst_ref=halos.at[turn_at, side],
            send_sem=halo_send.at[turn_at, side],
            recv_sem=halo_recv.at[turn_at, side],
            device_id=sides[side],
            device_id_type=MESH,
        )

    def block_rows(at):
        return pl.ds(pl.multiple_of(at * 64, 64), 64)

    def inner_part(wide):
        def fill(at, carry):
            inner[at] = along_z(wide[6 + at], (potential_ref[at] - center)[:, None, :])
            return carry

        lax.fori_loop(0, 6, fill, 0, unroll=2)

    def halo_take(turn_at, wide):
        for side in range(2):
            halo_copy(turn_at, side).wait_recv()

        def widen(at, carry):
            for side in range(2):
                block = halos[turn_at, side, block_rows(at)]
                wide[12 * side + at] = block.astype(jnp.float32).reshape(8, 8, 128)
            return carry

        lax.fori_loop(0, 6, widen, 0, unroll=2)

        def add_x(at, carry):
            inner[at] = inner[at] + along_x(wide, at)
            return carry

        lax.fori_loop(0, 6, add_x, 0, unroll=2)
        halo_copy(turn_at, 2).wait_recv()

    def shifted_ham(turn_at, wide, at):
        around = halos[turn_at, 2, block_rows(at)].astype(jnp.float32).reshape(8, 8, 128)
        return inner[at] + along_y(wide[6 + at], around)

    half, center, sigma, sigma_two = filter_scalars()
    for side in (2, 0, 1):
        halo_copy(0, side).start()
    inner_part(base)
    halo_take(0, base)
    pl.semaphore_wait(tokens.at[0], 2)
    send_tokens(1, (near(0, 0, 5), near(0, 0, -5)))

    def first_step(at, carry):
        result = sigma / half * shifted_ham(0, base, at)
        slope[6 + at] = result
        outgoing[1, block_rows(at)] = result.reshape(64, 128).astype(jnp.bfloat16)
        return carry

    lax.fori_loop(0, 6, first_step, 0, unroll=2)
    for side in (2, 0, 1):
        halo_copy(1, side).start()
    inner_part(slope)
    halo_take(1, slope)
    send_tokens(2, (near(3, 0, 0), near(-3, 0, 0)))

    def second_step(at, carry):
        result = 2.0 * sigma_two / half * shifted_ham(1, slope, at)
        result = result - sigma * sigma_two * base[6 + at]
        mine_ref[block_rows(at)] = result.reshape(64, 128).astype(jnp.bfloat16)
        return carry

    lax.fori_loop(0, 6, second_step, 0, unroll=2)

    def remote(source, target, phase, device):
        return pltpu.make_async_remote_copy(
            src_ref=source,
            dst_ref=target,
            send_sem=send_sem.at[phase],
            recv_sem=recv_sem.at[phase],
            device_id=device,
            device_id_type=MESH,
        )

    def cell_share(step, carry):
        to_row = (row + 1 + 2 * (step % 2)) % GRID_Y
        to_layer = (layer + far_first(step // 2, LAYERS)) % LAYERS
        other = (to_row // 2) * LAYERS + to_layer

        @pl.when(other % 4 != 3)
        def _():
            at = pl.multiple_of(band_share(other) * 16, 16)
            to = pl.multiple_of(band * 16, 16)
            remote(
                mine_ref.at[pl.ds(at, 16)],
                shares.at[pl.ds(to, 16)],
                0,
                {"band": other, "gy": 1 - half_y},
            ).start()

        return carry

    pl.semaphore_wait(tokens.at[1], 2)
    lax.fori_loop(0, BANDS, cell_share, 0)
    pl.semaphore_wait(tokens.at[2], 2)

    @pl.when(owns)
    def _():
        await_arrivals(shares, recv_sem.at[0])
        spread = shares[...].astype(jnp.float32).reshape(BANDS, 2, 8, 128)
        halves = [spread[:, half].reshape(FULL, 128) for half in range(2)]
        both = jnp.concatenate(halves, axis=1).astype(jnp.bfloat16)
        share[...] = both
        first = lax.dot_general(
            both[:128], both[:128], (((1,), (1,)), ((), ())), preferred_element_type=jnp.float32
        )
        second = lax.dot_general(
            both[128:], both, (((1,), (1,)), ((), ())), preferred_element_type=jnp.float32
        )
        blocked = jnp.concatenate([first, second[:, :128], second[:, 128:]], axis=0)
        partial[...] = blocked.astype(jnp.bfloat16).reshape(HOLDERS, 16, 128)

        def send_piece(step, carry):
            other = plane_partner(place, step)
            other_x, other_y = other // GRID_Y, other % GRID_Y

            @pl.when(holds_piece(other_x, other_y))
            def _():
                remote(
                    partial.at[piece_of(other_x, other_y)],
                    pieces.at[place],
                    1,
                    spot(other_x, other_y, layer),
                ).start()

            return carry

        lax.fori_loop(0, PLANE - 1, send_piece, 0)

    @pl.when(owns & holds)
    def _():
        pieces[place] = partial[own_piece]
        await_arrivals(pieces.at[pl.ds(0, PLANE - 1)], recv_sem.at[1])
        piece[...] = jnp.sum(pieces[...].astype(jnp.float32), axis=0).astype(jnp.bfloat16)
        at_layer = band_share(layer)

        def send_layer(step, carry):
            remote(
                piece,
                layers.at[at_layer],
                2,
                spot(across, row, (layer + far_first(step, LAYERS)) % LAYERS),
            ).start()
            return carry

        lax.fori_loop(0, LAYERS - 1, send_layer, 0)
        layers[at_layer] = piece[...]
        await_arrivals(layers.at[pl.ds(0, SENDERS - 1)], recv_sem.at[2])

    @pl.when(jnp.logical_not(owns) & holds)
    def _():
        await_arrivals(layers, recv_sem.at[2])

    @pl.when(holds)
    def _():
        total[...] = jnp.sum(layers[...].astype(jnp.float32), axis=0) / cells

        def send_total(step, carry):
            other = plane_partner(place, step)
            remote(
                total, blocks.at[own_piece], 3, spot(other // GRID_Y, other % GRID_Y, layer)
            ).start()
            return carry

        lax.fori_loop(0, PLANE - 1, send_total, 0)
        blocks[own_piece] = total[...]
        await_arrivals(blocks.at[pl.ds(0, HOLDERS - 1)], recv_sem.at[3])

    @pl.when(jnp.logical_not(holds))
    def _():
        await_arrivals(blocks.at[pl.ds(0, HOLDERS)], recv_sem.at[3])

    @pl.when(owns)
    def _():
        to = pl.multiple_of(band_share(band) * 16, 16)

        def send_parcels(side, weights, cells_of):
            turned = jnp.dot(weights, cells_of, preferred_element_type=jnp.float32)
            halves = [
                turned[:, 128 * h : 128 * h + 128].reshape(LAYERS, 1, 8, 128) for h in range(2)
            ]
            base_row = side * LAYERS * 16
            parcels[base_row : base_row + LAYERS * 16] = (
                jnp.concatenate(halves, axis=1).reshape(LAYERS * 16, 128).astype(jnp.bfloat16)
            )

            def send_parcel(step, carry):
                other = side * LAYERS + (layer + far_first(step, LAYERS)) % LAYERS
                at = pl.multiple_of(other * 16, 16)
                remote(
                    parcels.at[pl.ds(at, 16)],
                    arrived.at[pl.ds(to, 16)],
                    4,
                    {"band": other, "gy": 1 - half_y},
                ).start()
                return carry

            lax.fori_loop(0, LAYERS, send_parcel, 0)

        buffers = (rows_buf, cols_buf, panel_buf)
        corner = blocks[8:16].reshape(128, 128)
        upper = inverse_factor(blocks[0:8].reshape(128, 128), *buffers)
        send_parcels(0, upper.astype(jnp.bfloat16), share[:128])
        lower_left = full_dot(corner, upper, 1, 1)
        remaining = blocks[16:24].reshape(128, 128) - full_dot(lower_left, lower_left, 1, 1)
        carried = full_dot(lower_left, upper, 1, 0)
        lower = inverse_factor(remaining, *buffers)
        inverse[:, 128:] = lower.astype(jnp.bfloat16)
        inverse[:, :128] = (-full_dot(lower, carried, 1, 0)).astype(jnp.bfloat16)
        send_parcels(1, inverse[...], share[...])

    middle_block = blocks[8:16].reshape(128, 128)
    gram[:128, :128] = blocks[0:8].reshape(128, 128)
    gram[:128, 128:] = middle_block.T
    gram[128:, :128] = middle_block
    gram[128:, 128:] = blocks[16:24].reshape(128, 128)
    gram_ref[...] = gram[pl.ds(pl.multiple_of(band * 8, 8), 8), :]

    @pl.when(owns & holds)
    def _():
        await_arrivals(partial.at[pl.ds(0, HOLDERS - 1)], send_sem.at[1])
        await_arrivals(pieces.at[pl.ds(0, LAYERS - 1)], send_sem.at[2])

    @pl.when(owns & jnp.logical_not(holds))
    def _():
        await_arrivals(partial, send_sem.at[1])

    await_arrivals(mine_ref, send_sem.at[0])
    for turn_at in range(2):
        for side in range(3):
            halo_copy(turn_at, side).wait_send()

    @pl.when(holds)
    def _():
        await_arrivals(blocks.at[pl.ds(0, PLANE - 1)], send_sem.at[3])

    @pl.when(owns)
    def _():
        await_arrivals(parcels, send_sem.at[4])

    await_arrivals(arrived, recv_sem.at[4])
    rotated_ref[...] = arrived[...]


def filter_rotate(orbitals, potential, cells):
    return pl.pallas_call(
        functools.partial(filter_rotate_kernel, cells),
        out_shape=(
            pltpu.VMEM((OWNERS * 16, 128), jnp.bfloat16),
            pltpu.VMEM((8, FULL), jnp.float32),
        ),
        in_specs=[pl.BlockSpec(memory_space=pl.ANY)] * 2,
        out_specs=(pl.BlockSpec(memory_space=pltpu.VMEM),) * 2,
        scratch_shapes=[
            pltpu.VMEM((8, 6, 8, 128), jnp.float32),
            pltpu.VMEM((6, 8, 128), jnp.float32),
            pltpu.VMEM((FULL, FULL), jnp.float32),
            pltpu.VMEM((FULL, FULL), jnp.bfloat16),
            pltpu.VMEM((128, FULL), jnp.bfloat16),
            pltpu.VMEM((2, 8, 128), jnp.float32),
            pltpu.VMEM((2, 8, 8, 128), jnp.float32),
            pltpu.VMEM((2, 8, 128), jnp.float32),
            pltpu.VMEM((BANDS * 16, 128), jnp.bfloat16),
            pltpu.VMEM((OWNERS * 16, 128), jnp.bfloat16),
            pltpu.VMEM((384, 128), jnp.bfloat16),
            pltpu.VMEM((2, 384, 128), jnp.bfloat16),
            pltpu.VMEM((2, 3, 384, 128), jnp.bfloat16),
            pltpu.VMEM((18, 8, 8, 128), jnp.float32),
            pltpu.VMEM((18, 8, 8, 128), jnp.float32),
            pltpu.VMEM((6, 8, 8, 128), jnp.float32),
            pltpu.VMEM((BANDS * 16, 128), jnp.bfloat16),
            pltpu.VMEM((HOLDERS, 16, 128), jnp.bfloat16),
            pltpu.VMEM((PLANE, 16, 128), jnp.bfloat16),
            pltpu.VMEM((16, 128), jnp.bfloat16),
            pltpu.VMEM((SENDERS, 16, 128), jnp.bfloat16),
            pltpu.VMEM((16, 128), jnp.float32),
            pltpu.VMEM((PLANE, 16, 128), jnp.float32),
            pltpu.SemaphoreType.DMA((2, 3)),
            pltpu.SemaphoreType.DMA((2, 3)),
            pltpu.SemaphoreType.DMA((5,)),
            pltpu.SemaphoreType.DMA((5,)),
            pltpu.SemaphoreType.DMA((2,)),
            pltpu.SemaphoreType.REGULAR((3,)),
        ],
        compiler_params=pltpu.CompilerParams(collective_id=1, has_side_effects=True),
        name="filter_rotate",
    )(orbitals, potential)


def place_kernel(tiles_ref, rows_ref, rotated_ref, gram_ref):
    gram_ref[...] = rows_ref[...]
    for at in range(6):
        plane = tiles_ref[64 * at : 64 * at + 64].astype(jnp.float32).reshape(8, 8, 128)
        rotated_ref[:, at] = jnp.swapaxes(plane, 0, 1)


def place_outputs(tiles, rows, shape):
    return pl.pallas_call(
        place_kernel,
        out_shape=(
            jax.ShapeDtypeStruct(shape, jnp.float32),
            jax.ShapeDtypeStruct(rows.shape, jnp.float32),
        ),
        in_specs=[pl.BlockSpec(memory_space=pltpu.VMEM)] * 2,
        out_specs=(pl.BlockSpec(memory_space=pltpu.VMEM),) * 2,
        name="place_outputs",
    )(*(pltpu.with_memory_space_constraint(part, pltpu.VMEM) for part in (tiles, rows)))


def body(orbitals, potential):
    count, size_x, size_y, size_z = orbitals.shape
    total_cells = size_x * size_y * size_z * lax.axis_size("gx") * lax.axis_size("gy")
    tiles, gram_rows = filter_rotate(orbitals, potential, float(total_cells))
    return place_outputs(tiles, gram_rows, orbitals.shape)


def solution(mesh):
    return jax.shard_map(
        body,
        mesh=mesh,
        in_specs=(P("band", "gx", "gy", None), P("gx", "gy", None)),
        out_specs=(P("band", "gx", "gy", None), P("band", None)),
        check_vma=False,
    )
```

```python
import functools

import jax
import jax.numpy as jnp
from jax import lax
from jax.experimental import pallas as pl
from jax.experimental.pallas import tpu as pltpu
from jax.sharding import PartitionSpec as P

stencil_coeffs = (
    -5369.0 / 1800.0,
    12.0 / 7.0,
    -15.0 / 56.0,
    10.0 / 189.0,
    -1.0 / 112.0,
    2.0 / 1925.0,
    -1.0 / 16632.0,
)
spacing = 0.5
low_edge = 5.0
high_edge = 46.0
bottom_edge = -6.5


def filter_scalars():
    half = (high_edge - low_edge) / 2.0
    center = (high_edge + low_edge) / 2.0
    sigma = half / (bottom_edge - center)
    sigma_two = 1.0 / (2.0 / sigma - sigma)
    return (half, center, sigma, sigma_two)


MESH = pl.DeviceIdType.MESH
BANDS = 32
OWNERS = 24
LAYERS = 16
SENDERS = 12
PLANE = 32
HOLDERS = 24
GRID_X = 8
GRID_Y = 4
FULL = 256


def owner_band(share):
    return (share // 3) * 4 + share % 3


def band_share(band):
    return (band // 4) * 3 + band % 4


def far_first(step, count):
    reach = (step + 1) // 2
    return count // 2 + reach * (2 * (step % 2) - 1)


def spot(across, row, layer):
    return {"band": (row // 2) * LAYERS + layer, "gx": across, "gy": row % 2}


def plane_partner(place, step):
    across = (place // GRID_Y + far_first(step // GRID_Y, GRID_X)) % GRID_X
    return across * GRID_Y + (place + far_first(step % GRID_Y, GRID_Y)) % GRID_Y


def await_arrivals(buffer, sem):
    pltpu.make_async_copy(buffer, buffer, sem).wait()


def split_parts(value):
    high = value.astype(jnp.bfloat16)
    rest = value - high.astype(jnp.float32)
    middle = rest.astype(jnp.bfloat16)
    return high, middle, (rest - middle.astype(jnp.float32)).astype(jnp.bfloat16)


def inverse_factor(matrix, rows_buf, cols_buf, panel_buf):
    tile, size = 8, 128
    count = size // tile
    lane = lax.broadcasted_iota(jnp.int32, (tile, size), 1)

    def full(value):
        return jnp.broadcast_to(value, (tile, size))

    tiles = [matrix[tile * t : tile * t + tile] for t in range(count)]
    done = []
    for now in range(count):
        begin, slot = tile * now, now % 2
        head = tiles[now]
        rows_buf[slot] = head
        for j in range(tile):
            cols_buf[slot, j] = full(head[:, begin + j : begin + j + 1])
        inside = (lane >= begin) & (lane < begin + tile)
        entry = {
            (i, j): full(cols_buf[slot, j, i : i + 1, :])
            for j in range(tile)
            for i in range(j, tile)
        }
        row = [
            jnp.where(
                inside,
                (lane == begin + i).astype(jnp.float32),
                full(rows_buf[slot, i : i + 1, :]),
            )
            for i in range(tile)
        ]
        follows = now + 1 < count
        if follows:
            after = tiles[now + 1]
            column = [full(after[:, begin + p : begin + p + 1]) for p in range(tile)]
            after = jnp.where(inside, 0.0, after)
        scales = []
        for p in range(tile):
            scale = lax.rsqrt(entry[p, p])
            scales.append(scale)
            for i in range(p + 1, tile):
                entry[i, p] = entry[i, p] * scale
            row[p] = row[p] * scale
            if follows:
                column[p] = column[p] * scale
                after = after - column[p] * row[p]
            for i in range(p + 1, tile):
                for j in range(p + 1, i + 1):
                    entry[i, j] = entry[i, j] - entry[i, p] * entry[j, p]
                row[i] = row[i] - entry[i, p] * row[p]
                if follows:
                    column[i] = column[i] - column[p] * entry[i, p]
            panel_buf[slot, p : p + 1, :] = row[p][:1]
        if follows:
            tiles[now + 1] = after
        done.append(jnp.where(lane < begin + tile, panel_buf[slot], 0.0))
        if now + 2 < count:
            solved = [None] * tile
            for p in range(tile - 1, -1, -1):
                value = row[p]
                for i in range(p + 1, tile):
                    value = value - entry[i, p] * solved[i]
                solved[p] = value * scales[p]
            for t in range(now + 2, count):
                value = jnp.where(inside, 0.0, tiles[t])
                for p in range(tile):
                    value = value - full(tiles[t][:, begin + p : begin + p + 1]) * solved[p]
                tiles[t] = value
    return jnp.concatenate(done, axis=0)


def full_dot(left, right, left_dim, right_dim):
    a, b, c = split_parts(left)
    d, e, f = split_parts(right)
    return lax.dot_general(
        jnp.concatenate([a, a, b, a, c, b], axis=left_dim),
        jnp.concatenate([d, e, d, f, d, e], axis=right_dim),
        (((left_dim,), (right_dim,)), ((), ())),
        preferred_element_type=jnp.float32,
    )


def along_z(own, shifted):
    total = 3.0 * stencil_coeffs[0] * own
    for m in range(1, 7):
        total = total + stencil_coeffs[m] * (pltpu.roll(own, m, 2) + pltpu.roll(own, 128 - m, 2))
    return shifted * own - 0.5 / spacing**2 * total


def along_x(wide, at):
    total = stencil_coeffs[1] * (wide[7 + at] + wide[5 + at])
    for m in range(2, 7):
        total = total + stencil_coeffs[m] * (wide[6 + at + m] + wide[6 + at - m])
    return -0.5 / spacing**2 * total


def along_y(own, around):
    column = jnp.concatenate([around, own, around], axis=0)
    total = stencil_coeffs[1] * (column[9:17] + column[7:15])
    for m in range(2, 7):
        total = total + stencil_coeffs[m] * (column[8 + m : 16 + m] + column[8 - m : 16 - m])
    return -0.5 / spacing**2 * total


def filter_rotate_kernel(
    cells,
    orbitals_hbm,
    potential_hbm,
    rotated_ref,
    gram_ref,
    orbitals_ref,
    potential_ref,
    gram,
    share,
    inverse,
    rows_buf,
    cols_buf,
    panel_buf,
    parcels,
    arrived,
    mine_ref,
    outgoing,
    halos,
    base,
    slope,
    inner,
    shares,
    partial,
    pieces,
    piece,
    layers,
    total,
    blocks,
    halo_send,
    halo_recv,
    send_sem,
    recv_sem,
    local_sem,
    tokens,
):
    load_orbitals = pltpu.make_async_copy(orbitals_hbm, orbitals_ref, local_sem.at[0])
    load_orbitals.start()
    load_potential = pltpu.make_async_copy(potential_hbm, potential_ref, local_sem.at[1])
    load_potential.start()
    band = lax.axis_index("band")
    layer = band % LAYERS
    across = lax.axis_index("gx")
    half_y = lax.axis_index("gy")
    row = (band // LAYERS) * 2 + half_y
    place = across * GRID_Y + row
    owns = band % 4 != 3

    def holds_piece(spot_x, spot_y):
        return (spot_x + spot_y) % 4 != 3

    def piece_of(spot_x, spot_y):
        return spot_x * 3 + (spot_x + spot_y) % 4

    holds = holds_piece(across, row)
    own_piece = piece_of(across, row)
    leads = own_piece < 8

    def near(step_x, step_y, step_z):
        return spot(
            (across + step_x) % GRID_X, (row + step_y) % GRID_Y, (layer + step_z) % LAYERS
        )

    barrier = pltpu.get_barrier_semaphore()
    greeted = [near(0, 0, step) for step in (3, -3, 2, -2, 1, -1)]
    greeted += [near(0, side, step) for step in (2, -2, 1, -1, 0) for side in (1, 3)]
    greeted += [near(1, 0, 0), near(-1, 0, 0)]
    for device in greeted:
        pl.semaphore_signal(barrier, 1, device_id=device, device_id_type=MESH)

    def send_tokens(kind, devices):
        for device in devices:
            pl.semaphore_signal(tokens.at[kind], 1, device_id=device, device_id_type=MESH)

    def turn(at, carry):
        plane = jnp.swapaxes(orbitals_ref[:, at], 0, 1)
        base[6 + at] = plane
        rows_at = pl.ds(pl.multiple_of(at * 64, 64), 64)
        outgoing[0, rows_at] = plane.reshape(64, 128).astype(jnp.bfloat16)
        return carry

    load_orbitals.wait()
    lax.fori_loop(0, 6, turn, 0, unroll=2)
    load_potential.wait()
    pl.semaphore_wait(barrier, len(greeted))
    send_tokens(0, (near(0, 0, 3), near(0, 0, -3)))

    sides = (near(1, 0, 0), near(-1, 0, 0), {"gy": 1 - half_y})

    def halo_copy(turn_at, side):
        return pltpu.make_async_remote_copy(
            src_ref=outgoing.at[turn_at],
            dst_ref=halos.at[turn_at, side],
            send_sem=halo_send.at[turn_at, side],
            recv_sem=halo_recv.at[turn_at, side],
            device_id=sides[side],
            device_id_type=MESH,
        )

    def block_rows(at):
        return pl.ds(pl.multiple_of(at * 64, 64), 64)

    def inner_part(wide):
        def fill(at, carry):
            inner[at] = along_z(wide[6 + at], (potential_ref[at] - center)[:, None, :])
            return carry

        lax.fori_loop(0, 6, fill, 0, unroll=2)

    def halo_take(turn_at, wide):
        for side in range(2):
            halo_copy(turn_at, side).wait_recv()

        def widen(at, carry):
            for side in range(2):
                block = halos[turn_at, side, block_rows(at)]
                wide[12 * side + at] = block.astype(jnp.float32).reshape(8, 8, 128)
            return carry

        lax.fori_loop(0, 6, widen, 0, unroll=2)

        def add_x(at, carry):
            inner[at] = inner[at] + along_x(wide, at)
            return carry

        lax.fori_loop(0, 6, add_x, 0, unroll=2)
        halo_copy(turn_at, 2).wait_recv()

    def shifted_ham(turn_at, wide, at):
        around = halos[turn_at, 2, block_rows(at)].astype(jnp.float32).reshape(8, 8, 128)
        return inner[at] + along_y(wide[6 + at], around)

    half, center, sigma, sigma_two = filter_scalars()
    for side in (2, 0, 1):
        halo_copy(0, side).start()
    inner_part(base)
    halo_take(0, base)
    pl.semaphore_wait(tokens.at[0], 2)
    send_tokens(1, (near(0, 0, 5), near(0, 0, -5)))

    def first_step(at, carry):
        result = sigma / half * shifted_ham(0, base, at)
        slope[6 + at] = result
        outgoing[1, block_rows(at)] = result.reshape(64, 128).astype(jnp.bfloat16)
        return carry

    lax.fori_loop(0, 6, first_step, 0, unroll=2)
    for side in (2, 0, 1):
        halo_copy(1, side).start()
    inner_part(slope)
    halo_take(1, slope)
    send_tokens(2, (near(3, 0, 0), near(-3, 0, 0)))

    def second_step(at, carry):
        result = 2.0 * sigma_two / half * shifted_ham(1, slope, at)
        result = result - sigma * sigma_two * base[6 + at]
        mine_ref[block_rows(at)] = result.reshape(64, 128).astype(jnp.bfloat16)
        return carry

    lax.fori_loop(0, 6, second_step, 0, unroll=2)

    def remote(source, target, phase, device):
        return pltpu.make_async_remote_copy(
            src_ref=source,
            dst_ref=target,
            send_sem=send_sem.at[phase],
            recv_sem=recv_sem.at[phase],
            device_id=device,
            device_id_type=MESH,
        )

    def cell_share(step, carry):
        to_row = (row + 1 + 2 * (step % 2)) % GRID_Y
        to_layer = (layer + far_first(step // 2, LAYERS)) % LAYERS
        other = (to_row // 2) * LAYERS + to_layer

        @pl.when(other % 4 != 3)
        def _():
            at = pl.multiple_of(band_share(other) * 16, 16)
            to = pl.multiple_of(band * 16, 16)
            remote(
                mine_ref.at[pl.ds(at, 16)],
                shares.at[pl.ds(to, 16)],
                0,
                {"band": other, "gy": 1 - half_y},
            ).start()

        return carry

    pl.semaphore_wait(tokens.at[1], 2)
    lax.fori_loop(0, BANDS, cell_share, 0)
    pl.semaphore_wait(tokens.at[2], 2)

    @pl.when(owns)
    def _():
        await_arrivals(shares, recv_sem.at[0])
        spread = shares[...].astype(jnp.float32).reshape(BANDS, 2, 8, 128)
        halves = [spread[:, half].reshape(FULL, 128) for half in range(2)]
        both = jnp.concatenate(halves, axis=1).astype(jnp.bfloat16)
        share[...] = both
        first = lax.dot_general(
            both[:128], both[:128], (((1,), (1,)), ((), ())), preferred_element_type=jnp.float32
        )
        second = lax.dot_general(
            both[128:], both, (((1,), (1,)), ((), ())), preferred_element_type=jnp.float32
        )
        blocked = jnp.concatenate([first, second[:, :128], second[:, 128:]], axis=0)
        partial[...] = blocked.astype(jnp.bfloat16).reshape(HOLDERS, 16, 128)

        def send_piece(step, carry):
            other = plane_partner(place, step)
            other_x, other_y = other // GRID_Y, other % GRID_Y

            @pl.when(holds_piece(other_x, other_y))
            def _():
                remote(
                    partial.at[piece_of(other_x, other_y)],
                    pieces.at[place],
                    1,
                    spot(other_x, other_y, layer),
                ).start()

            return carry

        lax.fori_loop(0, PLANE - 1, send_piece, 0)

    @pl.when(owns & holds)
    def _():
        pieces[place] = partial[own_piece]
        await_arrivals(pieces.at[pl.ds(0, PLANE - 1)], recv_sem.at[1])
        piece[...] = jnp.sum(pieces[...].astype(jnp.float32), axis=0).astype(jnp.bfloat16)
        at_layer = band_share(layer)

        def send_layer(step, carry):
            remote(
                piece,
                layers.at[at_layer],
                2,
                spot(across, row, (layer + far_first(step, LAYERS)) % LAYERS),
            ).start()
            return carry

        lax.fori_loop(0, LAYERS - 1, send_layer, 0)
        layers[at_layer] = piece[...]
        await_arrivals(layers.at[pl.ds(0, SENDERS - 1)], recv_sem.at[2])

    @pl.when(jnp.logical_not(owns) & holds)
    def _():
        await_arrivals(layers, recv_sem.at[2])

    @pl.when(holds)
    def _():
        total[...] = jnp.sum(layers[...].astype(jnp.float32), axis=0) / cells

        def send_totals(phase):
            def send_total(step, carry):
                other = plane_partner(place, step)
                remote(
                    total,
                    blocks.at[own_piece],
                    phase,
                    spot(other // GRID_Y, other % GRID_Y, layer),
                ).start()
                return carry

            lax.fori_loop(0, PLANE - 1, send_total, 0)

        @pl.when(leads)
        def _():
            send_totals(3)

        @pl.when(jnp.logical_not(leads))
        def _():
            send_totals(5)

        blocks[own_piece] = total[...]

    def await_blocks(own, begin, count, phase):
        @pl.when(own)
        def _():
            await_arrivals(blocks.at[pl.ds(begin, count - 1)], recv_sem.at[phase])

        @pl.when(jnp.logical_not(own))
        def _():
            await_arrivals(blocks.at[pl.ds(begin, count)], recv_sem.at[phase])

    await_blocks(holds & leads, 0, 8, 3)

    def await_rest():
        await_blocks(holds & jnp.logical_not(leads), 8, 16, 5)

    @pl.when(owns)
    def _():
        to = pl.multiple_of(band_share(band) * 16, 16)

        def send_parcels(side, weights, cells_of):
            turned = jnp.dot(weights, cells_of, preferred_element_type=jnp.float32)
            halves = [
                turned[:, 128 * h : 128 * h + 128].reshape(LAYERS, 1, 8, 128) for h in range(2)
            ]
            base_row = side * LAYERS * 16
            parcels[base_row : base_row + LAYERS * 16] = (
                jnp.concatenate(halves, axis=1).reshape(LAYERS * 16, 128).astype(jnp.bfloat16)
            )

            def send_parcel(step, carry):
                other = side * LAYERS + (layer + far_first(step, LAYERS)) % LAYERS
                at = pl.multiple_of(other * 16, 16)
                remote(
                    parcels.at[pl.ds(at, 16)],
                    arrived.at[pl.ds(to, 16)],
                    4,
                    {"band": other, "gy": 1 - half_y},
                ).start()
                return carry

            lax.fori_loop(0, LAYERS, send_parcel, 0)

        buffers = (rows_buf, cols_buf, panel_buf)
        upper = inverse_factor(blocks[0:8].reshape(128, 128), *buffers)
        send_parcels(0, upper.astype(jnp.bfloat16), share[:128])
        await_rest()
        lower_left = full_dot(blocks[8:16].reshape(128, 128), upper, 1, 1)
        remaining = blocks[16:24].reshape(128, 128) - full_dot(lower_left, lower_left, 1, 1)
        carried = full_dot(lower_left, upper, 1, 0)
        lower = inverse_factor(remaining, *buffers)
        inverse[:, 128:] = lower.astype(jnp.bfloat16)
        inverse[:, :128] = (-full_dot(lower, carried, 1, 0)).astype(jnp.bfloat16)
        send_parcels(1, inverse[...], share[...])

    @pl.when(jnp.logical_not(owns))
    def _():
        await_rest()

    middle_block = blocks[8:16].reshape(128, 128)
    gram[:128, :128] = blocks[0:8].reshape(128, 128)
    gram[:128, 128:] = middle_block.T
    gram[128:, :128] = middle_block
    gram[128:, 128:] = blocks[16:24].reshape(128, 128)
    gram_ref[...] = gram[pl.ds(pl.multiple_of(band * 8, 8), 8), :]

    @pl.when(owns & holds)
    def _():
        await_arrivals(partial.at[pl.ds(0, HOLDERS - 1)], send_sem.at[1])
        await_arrivals(pieces.at[pl.ds(0, LAYERS - 1)], send_sem.at[2])

    @pl.when(owns & jnp.logical_not(holds))
    def _():
        await_arrivals(partial, send_sem.at[1])

    await_arrivals(mine_ref, send_sem.at[0])
    for turn_at in range(2):
        for side in range(3):
            halo_copy(turn_at, side).wait_send()

    @pl.when(holds & leads)
    def _():
        await_arrivals(blocks.at[pl.ds(0, PLANE - 1)], send_sem.at[3])

    @pl.when(holds & jnp.logical_not(leads))
    def _():
        await_arrivals(blocks.at[pl.ds(0, PLANE - 1)], send_sem.at[5])

    @pl.when(owns)
    def _():
        await_arrivals(parcels, send_sem.at[4])

    await_arrivals(arrived, recv_sem.at[4])
    rotated_ref[...] = arrived[...]


def filter_rotate(orbitals, potential, cells):
    return pl.pallas_call(
        functools.partial(filter_rotate_kernel, cells),
        out_shape=(
            pltpu.VMEM((OWNERS * 16, 128), jnp.bfloat16),
            pltpu.VMEM((8, FULL), jnp.float32),
        ),
        in_specs=[pl.BlockSpec(memory_space=pl.ANY)] * 2,
        out_specs=(pl.BlockSpec(memory_space=pltpu.VMEM),) * 2,
        scratch_shapes=[
            pltpu.VMEM((8, 6, 8, 128), jnp.float32),
            pltpu.VMEM((6, 8, 128), jnp.float32),
            pltpu.VMEM((FULL, FULL), jnp.float32),
            pltpu.VMEM((FULL, FULL), jnp.bfloat16),
            pltpu.VMEM((128, FULL), jnp.bfloat16),
            pltpu.VMEM((2, 8, 128), jnp.float32),
            pltpu.VMEM((2, 8, 8, 128), jnp.float32),
            pltpu.VMEM((2, 8, 128), jnp.float32),
            pltpu.VMEM((BANDS * 16, 128), jnp.bfloat16),
            pltpu.VMEM((OWNERS * 16, 128), jnp.bfloat16),
            pltpu.VMEM((384, 128), jnp.bfloat16),
            pltpu.VMEM((2, 384, 128), jnp.bfloat16),
            pltpu.VMEM((2, 3, 384, 128), jnp.bfloat16),
            pltpu.VMEM((18, 8, 8, 128), jnp.float32),
            pltpu.VMEM((18, 8, 8, 128), jnp.float32),
            pltpu.VMEM((6, 8, 8, 128), jnp.float32),
            pltpu.VMEM((BANDS * 16, 128), jnp.bfloat16),
            pltpu.VMEM((HOLDERS, 16, 128), jnp.bfloat16),
            pltpu.VMEM((PLANE, 16, 128), jnp.bfloat16),
            pltpu.VMEM((16, 128), jnp.bfloat16),
            pltpu.VMEM((SENDERS, 16, 128), jnp.bfloat16),
            pltpu.VMEM((16, 128), jnp.float32),
            pltpu.VMEM((PLANE, 16, 128), jnp.float32),
            pltpu.SemaphoreType.DMA((2, 3)),
            pltpu.SemaphoreType.DMA((2, 3)),
            pltpu.SemaphoreType.DMA((6,)),
            pltpu.SemaphoreType.DMA((6,)),
            pltpu.SemaphoreType.DMA((2,)),
            pltpu.SemaphoreType.REGULAR((3,)),
        ],
        compiler_params=pltpu.CompilerParams(collective_id=1, has_side_effects=True),
        name="filter_rotate",
    )(orbitals, potential)


def place_kernel(tiles_ref, rows_ref, rotated_ref, gram_ref):
    gram_ref[...] = rows_ref[...]
    for at in range(6):
        plane = tiles_ref[64 * at : 64 * at + 64].astype(jnp.float32).reshape(8, 8, 128)
        rotated_ref[:, at] = jnp.swapaxes(plane, 0, 1)


def place_outputs(tiles, rows, shape):
    return pl.pallas_call(
        place_kernel,
        out_shape=(
            jax.ShapeDtypeStruct(shape, jnp.float32),
            jax.ShapeDtypeStruct(rows.shape, jnp.float32),
        ),
        in_specs=[pl.BlockSpec(memory_space=pltpu.VMEM)] * 2,
        out_specs=(pl.BlockSpec(memory_space=pltpu.VMEM),) * 2,
        name="place_outputs",
    )(*(pltpu.with_memory_space_constraint(part, pltpu.VMEM) for part in (tiles, rows)))


def body(orbitals, potential):
    count, size_x, size_y, size_z = orbitals.shape
    total_cells = size_x * size_y * size_z * lax.axis_size("gx") * lax.axis_size("gy")
    tiles, gram_rows = filter_rotate(orbitals, potential, float(total_cells))
    return place_outputs(tiles, gram_rows, orbitals.shape)


def solution(mesh):
    return jax.shard_map(
        body,
        mesh=mesh,
        in_specs=(P("band", "gx", "gy", None), P("gx", "gy", None)),
        out_specs=(P("band", "gx", "gy", None), P("band", None)),
        check_vma=False,
    )
```

```python
import functools

import jax
import jax.numpy as jnp
from jax import lax
from jax.experimental import pallas as pl
from jax.experimental.pallas import tpu as pltpu
from jax.sharding import PartitionSpec as P

stencil_coeffs = (
    -5369.0 / 1800.0,
    12.0 / 7.0,
    -15.0 / 56.0,
    10.0 / 189.0,
    -1.0 / 112.0,
    2.0 / 1925.0,
    -1.0 / 16632.0,
)
spacing = 0.5
low_edge = 5.0
high_edge = 46.0
bottom_edge = -6.5


def filter_scalars():
    half = (high_edge - low_edge) / 2.0
    center = (high_edge + low_edge) / 2.0
    sigma = half / (bottom_edge - center)
    sigma_two = 1.0 / (2.0 / sigma - sigma)
    return (half, center, sigma, sigma_two)


MESH = pl.DeviceIdType.MESH
BANDS = 32
OWNERS = 24
LAYERS = 16
SENDERS = 12
PLANE = 32
HOLDERS = 24
GRID_X = 8
GRID_Y = 4
FULL = 256


def owner_band(share):
    return (share // 3) * 4 + share % 3


def band_share(band):
    return (band // 4) * 3 + band % 4


def far_first(step, count):
    reach = (step + 1) // 2
    return count // 2 + reach * (2 * (step % 2) - 1)


def spot(across, row, layer):
    return {"band": (row // 2) * LAYERS + layer, "gx": across, "gy": row % 2}


def plane_partner(place, step):
    across = (place // GRID_Y + far_first(step // GRID_Y, GRID_X)) % GRID_X
    return across * GRID_Y + (place + far_first(step % GRID_Y, GRID_Y)) % GRID_Y


def await_arrivals(buffer, sem):
    pltpu.make_async_copy(buffer, buffer, sem).wait()


def split_parts(value):
    high = value.astype(jnp.bfloat16)
    rest = value - high.astype(jnp.float32)
    middle = rest.astype(jnp.bfloat16)
    return high, middle, (rest - middle.astype(jnp.float32)).astype(jnp.bfloat16)


def inverse_factor(matrix, rows_buf, cols_buf, panel_buf, at_half=None):
    tile, size = 8, 128
    count = size // tile
    lane = lax.broadcasted_iota(jnp.int32, (tile, size), 1)

    def full(value):
        return jnp.broadcast_to(value, (tile, size))

    tiles = [matrix[tile * t : tile * t + tile] for t in range(count)]
    done = []
    for now in range(count):
        begin, slot = tile * now, now % 2
        head = tiles[now]
        rows_buf[slot] = head
        for j in range(tile):
            cols_buf[slot, j] = full(head[:, begin + j : begin + j + 1])
        inside = (lane >= begin) & (lane < begin + tile)
        entry = {
            (i, j): full(cols_buf[slot, j, i : i + 1, :])
            for j in range(tile)
            for i in range(j, tile)
        }
        row = [
            jnp.where(
                inside,
                (lane == begin + i).astype(jnp.float32),
                full(rows_buf[slot, i : i + 1, :]),
            )
            for i in range(tile)
        ]
        follows = now + 1 < count
        if follows:
            after = tiles[now + 1]
            column = [full(after[:, begin + p : begin + p + 1]) for p in range(tile)]
            after = jnp.where(inside, 0.0, after)
        scales = []
        for p in range(tile):
            scale = lax.rsqrt(entry[p, p])
            scales.append(scale)
            for i in range(p + 1, tile):
                entry[i, p] = entry[i, p] * scale
            row[p] = row[p] * scale
            if follows:
                column[p] = column[p] * scale
                after = after - column[p] * row[p]
            for i in range(p + 1, tile):
                for j in range(p + 1, i + 1):
                    entry[i, j] = entry[i, j] - entry[i, p] * entry[j, p]
                row[i] = row[i] - entry[i, p] * row[p]
                if follows:
                    column[i] = column[i] - column[p] * entry[i, p]
            panel_buf[slot, p : p + 1, :] = row[p][:1]
        if follows:
            tiles[now + 1] = after
        done.append(jnp.where(lane < begin + tile, panel_buf[slot], 0.0))
        if now + 2 < count:
            solved = [None] * tile
            for p in range(tile - 1, -1, -1):
                value = row[p]
                for i in range(p + 1, tile):
                    value = value - entry[i, p] * solved[i]
                solved[p] = value * scales[p]
            for t in range(now + 2, count):
                value = jnp.where(inside, 0.0, tiles[t])
                for p in range(tile):
                    value = value - full(tiles[t][:, begin + p : begin + p + 1]) * solved[p]
                tiles[t] = value
        if at_half is not None and 2 * (now + 1) == count:
            at_half(jnp.concatenate(done, axis=0))
    return jnp.concatenate(done, axis=0)


def full_dot(left, right, left_dim, right_dim):
    a, b, c = split_parts(left)
    d, e, f = split_parts(right)
    return lax.dot_general(
        jnp.concatenate([a, a, b, a, c, b], axis=left_dim),
        jnp.concatenate([d, e, d, f, d, e], axis=right_dim),
        (((left_dim,), (right_dim,)), ((), ())),
        preferred_element_type=jnp.float32,
    )


def along_z(own, shifted):
    total = 3.0 * stencil_coeffs[0] * own
    for m in range(1, 7):
        total = total + stencil_coeffs[m] * (pltpu.roll(own, m, 2) + pltpu.roll(own, 128 - m, 2))
    return shifted * own - 0.5 / spacing**2 * total


def along_x(wide, at):
    total = stencil_coeffs[1] * (wide[7 + at] + wide[5 + at])
    for m in range(2, 7):
        total = total + stencil_coeffs[m] * (wide[6 + at + m] + wide[6 + at - m])
    return -0.5 / spacing**2 * total


def along_y(own, around):
    column = jnp.concatenate([around, own, around], axis=0)
    total = stencil_coeffs[1] * (column[9:17] + column[7:15])
    for m in range(2, 7):
        total = total + stencil_coeffs[m] * (column[8 + m : 16 + m] + column[8 - m : 16 - m])
    return -0.5 / spacing**2 * total


def filter_rotate_kernel(
    cells,
    orbitals_hbm,
    potential_hbm,
    rotated_ref,
    gram_ref,
    orbitals_ref,
    potential_ref,
    gram,
    share,
    rows_buf,
    cols_buf,
    panel_buf,
    parcels,
    arrived,
    mine_ref,
    outgoing,
    halos,
    base,
    slope,
    inner,
    shares,
    partial,
    pieces,
    piece,
    layers,
    total,
    blocks,
    halo_send,
    halo_recv,
    send_sem,
    recv_sem,
    local_sem,
    tokens,
):
    load_orbitals = pltpu.make_async_copy(orbitals_hbm, orbitals_ref, local_sem.at[0])
    load_orbitals.start()
    load_potential = pltpu.make_async_copy(potential_hbm, potential_ref, local_sem.at[1])
    load_potential.start()
    band = lax.axis_index("band")
    layer = band % LAYERS
    across = lax.axis_index("gx")
    half_y = lax.axis_index("gy")
    row = (band // LAYERS) * 2 + half_y
    place = across * GRID_Y + row
    owns = band % 4 != 3

    def holds_piece(spot_x, spot_y):
        return (spot_x + spot_y) % 4 != 3

    def piece_of(spot_x, spot_y):
        return spot_x * 3 + (spot_x + spot_y) % 4

    holds = holds_piece(across, row)
    own_piece = piece_of(across, row)

    def near(step_x, step_y, step_z):
        return spot(
            (across + step_x) % GRID_X, (row + step_y) % GRID_Y, (layer + step_z) % LAYERS
        )

    barrier = pltpu.get_barrier_semaphore()
    greeted = [near(0, 0, step) for step in (3, -3, 2, -2, 1, -1)]
    greeted += [near(0, side, step) for step in (2, -2, 1, -1, 0) for side in (1, 3)]
    greeted += [near(1, 0, 0), near(-1, 0, 0)]
    for device in greeted:
        pl.semaphore_signal(barrier, 1, device_id=device, device_id_type=MESH)

    def send_tokens(kind, devices):
        for device in devices:
            pl.semaphore_signal(tokens.at[kind], 1, device_id=device, device_id_type=MESH)

    def turn(at, carry):
        plane = jnp.swapaxes(orbitals_ref[:, at], 0, 1)
        base[6 + at] = plane
        rows_at = pl.ds(pl.multiple_of(at * 64, 64), 64)
        outgoing[0, rows_at] = plane.reshape(64, 128).astype(jnp.bfloat16)
        return carry

    load_orbitals.wait()
    lax.fori_loop(0, 6, turn, 0, unroll=2)
    load_potential.wait()
    pl.semaphore_wait(barrier, len(greeted))
    send_tokens(0, (near(0, 0, 3), near(0, 0, -3)))

    sides = (near(1, 0, 0), near(-1, 0, 0), {"gy": 1 - half_y})

    def halo_copy(turn_at, side):
        return pltpu.make_async_remote_copy(
            src_ref=outgoing.at[turn_at],
            dst_ref=halos.at[turn_at, side],
            send_sem=halo_send.at[turn_at, side],
            recv_sem=halo_recv.at[turn_at, side],
            device_id=sides[side],
            device_id_type=MESH,
        )

    def block_rows(at):
        return pl.ds(pl.multiple_of(at * 64, 64), 64)

    def inner_part(wide):
        def fill(at, carry):
            inner[at] = along_z(wide[6 + at], (potential_ref[at] - center)[:, None, :])
            return carry

        lax.fori_loop(0, 6, fill, 0, unroll=2)

    def halo_take(turn_at, wide):
        for side in range(2):
            halo_copy(turn_at, side).wait_recv()

        def widen(at, carry):
            for side in range(2):
                block = halos[turn_at, side, block_rows(at)]
                wide[12 * side + at] = block.astype(jnp.float32).reshape(8, 8, 128)
            return carry

        lax.fori_loop(0, 6, widen, 0, unroll=2)

        def add_x(at, carry):
            inner[at] = inner[at] + along_x(wide, at)
            return carry

        lax.fori_loop(0, 6, add_x, 0, unroll=2)
        halo_copy(turn_at, 2).wait_recv()

    def shifted_ham(turn_at, wide, at):
        around = halos[turn_at, 2, block_rows(at)].astype(jnp.float32).reshape(8, 8, 128)
        return inner[at] + along_y(wide[6 + at], around)

    half, center, sigma, sigma_two = filter_scalars()
    for side in (2, 0, 1):
        halo_copy(0, side).start()
    inner_part(base)
    halo_take(0, base)
    pl.semaphore_wait(tokens.at[0], 2)
    send_tokens(1, (near(0, 0, 5), near(0, 0, -5)))

    def first_step(at, carry):
        result = sigma / half * shifted_ham(0, base, at)
        slope[6 + at] = result
        outgoing[1, block_rows(at)] = result.reshape(64, 128).astype(jnp.bfloat16)
        return carry

    lax.fori_loop(0, 6, first_step, 0, unroll=2)
    for side in (2, 0, 1):
        halo_copy(1, side).start()
    inner_part(slope)
    halo_take(1, slope)
    send_tokens(2, (near(3, 0, 0), near(-3, 0, 0)))

    def second_step(at, carry):
        result = 2.0 * sigma_two / half * shifted_ham(1, slope, at)
        result = result - sigma * sigma_two * base[6 + at]
        mine_ref[block_rows(at)] = result.reshape(64, 128).astype(jnp.bfloat16)
        return carry

    lax.fori_loop(0, 6, second_step, 0, unroll=2)

    def remote(source, target, phase, device):
        return pltpu.make_async_remote_copy(
            src_ref=source,
            dst_ref=target,
            send_sem=send_sem.at[phase],
            recv_sem=recv_sem.at[phase],
            device_id=device,
            device_id_type=MESH,
        )

    def cell_share(step, carry):
        to_row = (row + 1 + 2 * (step % 2)) % GRID_Y
        to_layer = (layer + far_first(step // 2, LAYERS)) % LAYERS
        other = (to_row // 2) * LAYERS + to_layer

        @pl.when(other % 4 != 3)
        def _():
            at = pl.multiple_of(band_share(other) * 16, 16)
            to = pl.multiple_of(band * 16, 16)
            remote(
                mine_ref.at[pl.ds(at, 16)],
                shares.at[pl.ds(to, 16)],
                0,
                {"band": other, "gy": 1 - half_y},
            ).start()

        return carry

    pl.semaphore_wait(tokens.at[1], 2)
    lax.fori_loop(0, BANDS, cell_share, 0)
    pl.semaphore_wait(tokens.at[2], 2)

    @pl.when(owns)
    def _():
        await_arrivals(shares, recv_sem.at[0])
        spread = shares[...].astype(jnp.float32).reshape(BANDS, 2, 8, 128)
        halves = [spread[:, half].reshape(FULL, 128) for half in range(2)]
        both = jnp.concatenate(halves, axis=1).astype(jnp.bfloat16)
        share[...] = both
        first = lax.dot_general(
            both[:128], both[:128], (((1,), (1,)), ((), ())), preferred_element_type=jnp.float32
        )
        second = lax.dot_general(
            both[128:], both, (((1,), (1,)), ((), ())), preferred_element_type=jnp.float32
        )
        blocked = jnp.concatenate([first, second[:, :128], second[:, 128:]], axis=0)
        partial[...] = blocked.astype(jnp.bfloat16).reshape(HOLDERS, 16, 128)

        def send_piece(step, carry):
            other = plane_partner(place, step)
            other_x, other_y = other // GRID_Y, other % GRID_Y

            @pl.when(holds_piece(other_x, other_y))
            def _():
                remote(
                    partial.at[piece_of(other_x, other_y)],
                    pieces.at[place],
                    1,
                    spot(other_x, other_y, layer),
                ).start()

            return carry

        lax.fori_loop(0, PLANE - 1, send_piece, 0)

    @pl.when(owns & holds)
    def _():
        pieces[place] = partial[own_piece]
        await_arrivals(pieces.at[pl.ds(0, PLANE - 1)], recv_sem.at[1])
        piece[...] = jnp.sum(pieces[...].astype(jnp.float32), axis=0).astype(jnp.bfloat16)
        at_layer = band_share(layer)

        def send_layer(step, carry):
            remote(
                piece,
                layers.at[at_layer],
                2,
                spot(across, row, (layer + far_first(step, LAYERS)) % LAYERS),
            ).start()
            return carry

        lax.fori_loop(0, LAYERS - 1, send_layer, 0)
        layers[at_layer] = piece[...]
        await_arrivals(layers.at[pl.ds(0, SENDERS - 1)], recv_sem.at[2])

    @pl.when(jnp.logical_not(owns) & holds)
    def _():
        await_arrivals(layers, recv_sem.at[2])

    @pl.when(holds)
    def _():
        total[...] = jnp.sum(layers[...].astype(jnp.float32), axis=0) / cells

        def send_total(step, carry):
            other = plane_partner(place, step)
            remote(
                total, blocks.at[own_piece], 3, spot(other // GRID_Y, other % GRID_Y, layer)
            ).start()
            return carry

        lax.fori_loop(0, PLANE - 1, send_total, 0)
        blocks[own_piece] = total[...]
        await_arrivals(blocks.at[pl.ds(0, HOLDERS - 1)], recv_sem.at[3])

    @pl.when(jnp.logical_not(holds))
    def _():
        await_arrivals(blocks.at[pl.ds(0, HOLDERS)], recv_sem.at[3])

    @pl.when(owns)
    def _():
        to = pl.multiple_of(band_share(band) * 16, 16)

        def send_parcels(first, count, weights, cells_of):
            turned = jnp.dot(weights, cells_of, preferred_element_type=jnp.float32)
            halves = [
                turned[:, 128 * h : 128 * h + 128].reshape(count, 1, 8, 128) for h in range(2)
            ]
            parcels[first * 16 : (first + count) * 16] = (
                jnp.concatenate(halves, axis=1).reshape(count * 16, 128).astype(jnp.bfloat16)
            )

            def send_parcel(step, carry):
                offset = (layer + far_first(step, LAYERS)) % LAYERS
                low = first % LAYERS

                @pl.when((offset >= low) & (offset < low + count))
                def _():
                    other = (first // LAYERS) * LAYERS + offset
                    at = pl.multiple_of(other * 16, 16)
                    remote(
                        parcels.at[pl.ds(at, 16)],
                        arrived.at[pl.ds(to, 16)],
                        4,
                        {"band": other, "gy": 1 - half_y},
                    ).start()

                return carry

            lax.fori_loop(0, LAYERS, send_parcel, 0)

        buffers = (rows_buf, cols_buf, panel_buf)
        upper = inverse_factor(blocks[0:8].reshape(128, 128), *buffers)
        send_parcels(0, 16, upper.astype(jnp.bfloat16), share[:128])
        corner = blocks[8:16].reshape(128, 128)
        lower_left = full_dot(corner, upper, 1, 1)
        remaining = blocks[16:24].reshape(128, 128) - full_dot(lower_left, lower_left, 1, 1)
        carried = full_dot(lower_left, upper, 1, 0)

        def send_lower(first, rows):
            left = -full_dot(rows, carried, 1, 0)
            weights = jnp.concatenate([left, rows], axis=1).astype(jnp.bfloat16)
            send_parcels(first, 8, weights, share[...])

        lower = inverse_factor(remaining, *buffers, lambda rows: send_lower(16, rows))
        send_lower(24, lower[64:])

    middle_block = blocks[8:16].reshape(128, 128)
    gram[:128, :128] = blocks[0:8].reshape(128, 128)
    gram[:128, 128:] = middle_block.T
    gram[128:, :128] = middle_block
    gram[128:, 128:] = blocks[16:24].reshape(128, 128)
    gram_ref[...] = gram[pl.ds(pl.multiple_of(band * 8, 8), 8), :]

    @pl.when(owns & holds)
    def _():
        await_arrivals(partial.at[pl.ds(0, HOLDERS - 1)], send_sem.at[1])
        await_arrivals(pieces.at[pl.ds(0, LAYERS - 1)], send_sem.at[2])

    @pl.when(owns & jnp.logical_not(holds))
    def _():
        await_arrivals(partial, send_sem.at[1])

    await_arrivals(mine_ref, send_sem.at[0])
    for turn_at in range(2):
        for side in range(3):
            halo_copy(turn_at, side).wait_send()

    @pl.when(holds)
    def _():
        await_arrivals(blocks.at[pl.ds(0, PLANE - 1)], send_sem.at[3])

    @pl.when(owns)
    def _():
        await_arrivals(parcels, send_sem.at[4])

    await_arrivals(arrived, recv_sem.at[4])
    rotated_ref[...] = arrived[...]


def filter_rotate(orbitals, potential, cells):
    return pl.pallas_call(
        functools.partial(filter_rotate_kernel, cells),
        out_shape=(
            pltpu.VMEM((OWNERS * 16, 128), jnp.bfloat16),
            pltpu.VMEM((8, FULL), jnp.float32),
        ),
        in_specs=[pl.BlockSpec(memory_space=pl.ANY)] * 2,
        out_specs=(pl.BlockSpec(memory_space=pltpu.VMEM),) * 2,
        scratch_shapes=[
            pltpu.VMEM((8, 6, 8, 128), jnp.float32),
            pltpu.VMEM((6, 8, 128), jnp.float32),
            pltpu.VMEM((FULL, FULL), jnp.float32),
            pltpu.VMEM((FULL, FULL), jnp.bfloat16),
            pltpu.VMEM((2, 8, 128), jnp.float32),
            pltpu.VMEM((2, 8, 8, 128), jnp.float32),
            pltpu.VMEM((2, 8, 128), jnp.float32),
            pltpu.VMEM((BANDS * 16, 128), jnp.bfloat16),
            pltpu.VMEM((OWNERS * 16, 128), jnp.bfloat16),
            pltpu.VMEM((384, 128), jnp.bfloat16),
            pltpu.VMEM((2, 384, 128), jnp.bfloat16),
            pltpu.VMEM((2, 3, 384, 128), jnp.bfloat16),
            pltpu.VMEM((18, 8, 8, 128), jnp.float32),
            pltpu.VMEM((18, 8, 8, 128), jnp.float32),
            pltpu.VMEM((6, 8, 8, 128), jnp.float32),
            pltpu.VMEM((BANDS * 16, 128), jnp.bfloat16),
            pltpu.VMEM((HOLDERS, 16, 128), jnp.bfloat16),
            pltpu.VMEM((PLANE, 16, 128), jnp.bfloat16),
            pltpu.VMEM((16, 128), jnp.bfloat16),
            pltpu.VMEM((SENDERS, 16, 128), jnp.bfloat16),
            pltpu.VMEM((16, 128), jnp.float32),
            pltpu.VMEM((PLANE, 16, 128), jnp.float32),
            pltpu.SemaphoreType.DMA((2, 3)),
            pltpu.SemaphoreType.DMA((2, 3)),
            pltpu.SemaphoreType.DMA((5,)),
            pltpu.SemaphoreType.DMA((5,)),
            pltpu.SemaphoreType.DMA((2,)),
            pltpu.SemaphoreType.REGULAR((3,)),
        ],
        compiler_params=pltpu.CompilerParams(collective_id=1, has_side_effects=True),
        name="filter_rotate",
    )(orbitals, potential)


def place_kernel(tiles_ref, rows_ref, rotated_ref, gram_ref):
    gram_ref[...] = rows_ref[...]
    for at in range(6):
        plane = tiles_ref[64 * at : 64 * at + 64].astype(jnp.float32).reshape(8, 8, 128)
        rotated_ref[:, at] = jnp.swapaxes(plane, 0, 1)


def place_outputs(tiles, rows, shape):
    return pl.pallas_call(
        place_kernel,
        out_shape=(
            jax.ShapeDtypeStruct(shape, jnp.float32),
            jax.ShapeDtypeStruct(rows.shape, jnp.float32),
        ),
        in_specs=[pl.BlockSpec(memory_space=pltpu.VMEM)] * 2,
        out_specs=(pl.BlockSpec(memory_space=pltpu.VMEM),) * 2,
        name="place_outputs",
    )(*(pltpu.with_memory_space_constraint(part, pltpu.VMEM) for part in (tiles, rows)))


def body(orbitals, potential):
    count, size_x, size_y, size_z = orbitals.shape
    total_cells = size_x * size_y * size_z * lax.axis_size("gx") * lax.axis_size("gy")
    tiles, gram_rows = filter_rotate(orbitals, potential, float(total_cells))
    return place_outputs(tiles, gram_rows, orbitals.shape)


def solution(mesh):
    return jax.shard_map(
        body,
        mesh=mesh,
        in_specs=(P("band", "gx", "gy", None), P("gx", "gy", None)),
        out_specs=(P("band", "gx", "gy", None), P("band", None)),
        check_vma=False,
    )
```

```python
import functools

import jax
import jax.numpy as jnp
from jax import lax
from jax.experimental import pallas as pl
from jax.experimental.pallas import tpu as pltpu
from jax.sharding import PartitionSpec as P

stencil_coeffs = (
    -5369.0 / 1800.0,
    12.0 / 7.0,
    -15.0 / 56.0,
    10.0 / 189.0,
    -1.0 / 112.0,
    2.0 / 1925.0,
    -1.0 / 16632.0,
)
spacing = 0.5
low_edge = 5.0
high_edge = 46.0
bottom_edge = -6.5


def filter_scalars():
    half = (high_edge - low_edge) / 2.0
    center = (high_edge + low_edge) / 2.0
    sigma = half / (bottom_edge - center)
    sigma_two = 1.0 / (2.0 / sigma - sigma)
    return (half, center, sigma, sigma_two)


MESH = pl.DeviceIdType.MESH
BANDS = 32
OWNERS = 24
LAYERS = 16
SENDERS = 12
PLANE = 32
HOLDERS = 24
GRID_X = 8
GRID_Y = 4
FULL = 256


def owner_band(share):
    return (share // 3) * 4 + share % 3


def band_share(band):
    return (band // 4) * 3 + band % 4


def far_first(step, count):
    reach = (step + 1) // 2
    return count // 2 + reach * (2 * (step % 2) - 1)


def spot(across, row, layer):
    return {"band": (row // 2) * LAYERS + layer, "gx": across, "gy": row % 2}


def plane_partner(place, step):
    across = (place // GRID_Y + far_first(step // GRID_Y, GRID_X)) % GRID_X
    return across * GRID_Y + (place + far_first(step % GRID_Y, GRID_Y)) % GRID_Y


def await_arrivals(buffer, sem):
    pltpu.make_async_copy(buffer, buffer, sem).wait()


def split_parts(value):
    high = value.astype(jnp.bfloat16)
    rest = value - high.astype(jnp.float32)
    middle = rest.astype(jnp.bfloat16)
    return high, middle, (rest - middle.astype(jnp.float32)).astype(jnp.bfloat16)


def inverse_factor(matrix, rows_buf, cols_buf, panel_buf, part_ready=None):
    tile, size = 8, 128
    count = size // tile
    lane = lax.broadcasted_iota(jnp.int32, (tile, size), 1)

    def full(value):
        return jnp.broadcast_to(value, (tile, size))

    tiles = [matrix[tile * t : tile * t + tile] for t in range(count)]
    done = []
    for now in range(count):
        begin, slot = tile * now, now % 2
        head = tiles[now]
        rows_buf[slot] = head
        for j in range(tile):
            cols_buf[slot, j] = full(head[:, begin + j : begin + j + 1])
        inside = (lane >= begin) & (lane < begin + tile)
        entry = {
            (i, j): full(cols_buf[slot, j, i : i + 1, :])
            for j in range(tile)
            for i in range(j, tile)
        }
        row = [
            jnp.where(
                inside,
                (lane == begin + i).astype(jnp.float32),
                full(rows_buf[slot, i : i + 1, :]),
            )
            for i in range(tile)
        ]
        follows = now + 1 < count
        if follows:
            after = tiles[now + 1]
            column = [full(after[:, begin + p : begin + p + 1]) for p in range(tile)]
            after = jnp.where(inside, 0.0, after)
        scales = []
        for p in range(tile):
            scale = lax.rsqrt(entry[p, p])
            scales.append(scale)
            for i in range(p + 1, tile):
                entry[i, p] = entry[i, p] * scale
            row[p] = row[p] * scale
            if follows:
                column[p] = column[p] * scale
                after = after - column[p] * row[p]
            for i in range(p + 1, tile):
                for j in range(p + 1, i + 1):
                    entry[i, j] = entry[i, j] - entry[i, p] * entry[j, p]
                row[i] = row[i] - entry[i, p] * row[p]
                if follows:
                    column[i] = column[i] - column[p] * entry[i, p]
            panel_buf[slot, p : p + 1, :] = row[p][:1]
        if follows:
            tiles[now + 1] = after
        done.append(jnp.where(lane < begin + tile, panel_buf[slot], 0.0))
        if now + 2 < count:
            solved = [None] * tile
            for p in range(tile - 1, -1, -1):
                value = row[p]
                for i in range(p + 1, tile):
                    value = value - entry[i, p] * solved[i]
                solved[p] = value * scales[p]
            for t in range(now + 2, count):
                value = jnp.where(inside, 0.0, tiles[t])
                for p in range(tile):
                    value = value - full(tiles[t][:, begin + p : begin + p + 1]) * solved[p]
                tiles[t] = value
        if part_ready is not None:
            part_ready(done)
    return jnp.concatenate(done, axis=0)


def full_dot(left, right, left_dim, right_dim):
    a, b, c = split_parts(left)
    d, e, f = split_parts(right)
    return lax.dot_general(
        jnp.concatenate([a, a, b, a, c, b], axis=left_dim),
        jnp.concatenate([d, e, d, f, d, e], axis=right_dim),
        (((left_dim,), (right_dim,)), ((), ())),
        preferred_element_type=jnp.float32,
    )


def along_z(own, shifted):
    total = 3.0 * stencil_coeffs[0] * own
    for m in range(1, 7):
        total = total + stencil_coeffs[m] * (pltpu.roll(own, m, 2) + pltpu.roll(own, 128 - m, 2))
    return shifted * own - 0.5 / spacing**2 * total


def along_x(wide, at):
    total = stencil_coeffs[1] * (wide[7 + at] + wide[5 + at])
    for m in range(2, 7):
        total = total + stencil_coeffs[m] * (wide[6 + at + m] + wide[6 + at - m])
    return -0.5 / spacing**2 * total


def along_y(own, around):
    column = jnp.concatenate([around, own, around], axis=0)
    total = stencil_coeffs[1] * (column[9:17] + column[7:15])
    for m in range(2, 7):
        total = total + stencil_coeffs[m] * (column[8 + m : 16 + m] + column[8 - m : 16 - m])
    return -0.5 / spacing**2 * total


def filter_rotate_kernel(
    cells,
    orbitals_hbm,
    potential_hbm,
    rotated_ref,
    gram_ref,
    orbitals_ref,
    potential_ref,
    gram,
    share,
    rows_buf,
    cols_buf,
    panel_buf,
    parcels,
    arrived,
    mine_ref,
    outgoing,
    halos,
    base,
    slope,
    inner,
    shares,
    partial,
    pieces,
    piece,
    layers,
    total,
    blocks,
    halo_send,
    halo_recv,
    send_sem,
    recv_sem,
    local_sem,
    tokens,
):
    load_orbitals = pltpu.make_async_copy(orbitals_hbm, orbitals_ref, local_sem.at[0])
    load_orbitals.start()
    load_potential = pltpu.make_async_copy(potential_hbm, potential_ref, local_sem.at[1])
    load_potential.start()
    band = lax.axis_index("band")
    layer = band % LAYERS
    across = lax.axis_index("gx")
    half_y = lax.axis_index("gy")
    row = (band // LAYERS) * 2 + half_y
    place = across * GRID_Y + row
    owns = band % 4 != 3

    def holds_piece(spot_x, spot_y):
        return (spot_x + spot_y) % 4 != 3

    def piece_of(spot_x, spot_y):
        return spot_x * 3 + (spot_x + spot_y) % 4

    holds = holds_piece(across, row)
    own_piece = piece_of(across, row)

    def near(step_x, step_y, step_z):
        return spot(
            (across + step_x) % GRID_X, (row + step_y) % GRID_Y, (layer + step_z) % LAYERS
        )

    barrier = pltpu.get_barrier_semaphore()
    greeted = [near(0, 0, step) for step in (3, -3, 2, -2, 1, -1)]
    greeted += [near(0, side, step) for step in (2, -2, 1, -1, 0) for side in (1, 3)]
    greeted += [near(1, 0, 0), near(-1, 0, 0)]
    for device in greeted:
        pl.semaphore_signal(barrier, 1, device_id=device, device_id_type=MESH)

    def send_tokens(kind, devices):
        for device in devices:
            pl.semaphore_signal(tokens.at[kind], 1, device_id=device, device_id_type=MESH)

    def turn(at, carry):
        plane = jnp.swapaxes(orbitals_ref[:, at], 0, 1)
        base[6 + at] = plane
        rows_at = pl.ds(pl.multiple_of(at * 64, 64), 64)
        outgoing[0, rows_at] = plane.reshape(64, 128).astype(jnp.bfloat16)
        return carry

    load_orbitals.wait()
    lax.fori_loop(0, 6, turn, 0, unroll=2)
    load_potential.wait()
    pl.semaphore_wait(barrier, len(greeted))
    send_tokens(0, (near(0, 0, 3), near(0, 0, -3)))

    sides = (near(1, 0, 0), near(-1, 0, 0), {"gy": 1 - half_y})

    def halo_copy(turn_at, side):
        return pltpu.make_async_remote_copy(
            src_ref=outgoing.at[turn_at],
            dst_ref=halos.at[turn_at, side],
            send_sem=halo_send.at[turn_at, side],
            recv_sem=halo_recv.at[turn_at, side],
            device_id=sides[side],
            device_id_type=MESH,
        )

    def block_rows(at):
        return pl.ds(pl.multiple_of(at * 64, 64), 64)

    def inner_part(wide):
        def fill(at, carry):
            inner[at] = along_z(wide[6 + at], (potential_ref[at] - center)[:, None, :])
            return carry

        lax.fori_loop(0, 6, fill, 0, unroll=2)

    def halo_take(turn_at, wide):
        for side in range(2):
            halo_copy(turn_at, side).wait_recv()

        def widen(at, carry):
            for side in range(2):
                block = halos[turn_at, side, block_rows(at)]
                wide[12 * side + at] = block.astype(jnp.float32).reshape(8, 8, 128)
            return carry

        lax.fori_loop(0, 6, widen, 0, unroll=2)

        def add_x(at, carry):
            inner[at] = inner[at] + along_x(wide, at)
            return carry

        lax.fori_loop(0, 6, add_x, 0, unroll=2)
        halo_copy(turn_at, 2).wait_recv()

    def shifted_ham(turn_at, wide, at):
        around = halos[turn_at, 2, block_rows(at)].astype(jnp.float32).reshape(8, 8, 128)
        return inner[at] + along_y(wide[6 + at], around)

    half, center, sigma, sigma_two = filter_scalars()
    for side in (2, 0, 1):
        halo_copy(0, side).start()
    inner_part(base)
    halo_take(0, base)
    pl.semaphore_wait(tokens.at[0], 2)
    send_tokens(1, (near(0, 0, 5), near(0, 0, -5)))

    def first_step(at, carry):
        result = sigma / half * shifted_ham(0, base, at)
        slope[6 + at] = result
        outgoing[1, block_rows(at)] = result.reshape(64, 128).astype(jnp.bfloat16)
        return carry

    lax.fori_loop(0, 6, first_step, 0, unroll=2)
    for side in (2, 0, 1):
        halo_copy(1, side).start()
    inner_part(slope)
    halo_take(1, slope)
    send_tokens(2, (near(3, 0, 0), near(-3, 0, 0)))

    def second_step(at, carry):
        result = 2.0 * sigma_two / half * shifted_ham(1, slope, at)
        result = result - sigma * sigma_two * base[6 + at]
        mine_ref[block_rows(at)] = result.reshape(64, 128).astype(jnp.bfloat16)
        return carry

    lax.fori_loop(0, 6, second_step, 0, unroll=2)

    def remote(source, target, phase, device):
        return pltpu.make_async_remote_copy(
            src_ref=source,
            dst_ref=target,
            send_sem=send_sem.at[phase],
            recv_sem=recv_sem.at[phase],
            device_id=device,
            device_id_type=MESH,
        )

    def cell_share(step, carry):
        to_row = (row + 1 + 2 * (step % 2)) % GRID_Y
        to_layer = (layer + far_first(step // 2, LAYERS)) % LAYERS
        other = (to_row // 2) * LAYERS + to_layer

        @pl.when(other % 4 != 3)
        def _():
            at = pl.multiple_of(band_share(other) * 16, 16)
            to = pl.multiple_of(band * 16, 16)
            remote(
                mine_ref.at[pl.ds(at, 16)],
                shares.at[pl.ds(to, 16)],
                0,
                {"band": other, "gy": 1 - half_y},
            ).start()

        return carry

    pl.semaphore_wait(tokens.at[1], 2)
    lax.fori_loop(0, BANDS, cell_share, 0)
    pl.semaphore_wait(tokens.at[2], 2)

    @pl.when(owns)
    def _():
        await_arrivals(shares, recv_sem.at[0])
        spread = shares[...].astype(jnp.float32).reshape(BANDS, 2, 8, 128)
        halves = [spread[:, half].reshape(FULL, 128) for half in range(2)]
        both = jnp.concatenate(halves, axis=1).astype(jnp.bfloat16)
        share[...] = both
        first = lax.dot_general(
            both[:128], both[:128], (((1,), (1,)), ((), ())), preferred_element_type=jnp.float32
        )
        second = lax.dot_general(
            both[128:], both, (((1,), (1,)), ((), ())), preferred_element_type=jnp.float32
        )
        blocked = jnp.concatenate([first, second[:, :128], second[:, 128:]], axis=0)
        partial[...] = blocked.astype(jnp.bfloat16).reshape(HOLDERS, 16, 128)

        def send_piece(step, carry):
            other = plane_partner(place, step)
            other_x, other_y = other // GRID_Y, other % GRID_Y

            @pl.when(holds_piece(other_x, other_y))
            def _():
                remote(
                    partial.at[piece_of(other_x, other_y)],
                    pieces.at[place],
                    1,
                    spot(other_x, other_y, layer),
                ).start()

            return carry

        lax.fori_loop(0, PLANE - 1, send_piece, 0)

    @pl.when(owns & holds)
    def _():
        pieces[place] = partial[own_piece]
        await_arrivals(pieces.at[pl.ds(0, PLANE - 1)], recv_sem.at[1])
        piece[...] = jnp.sum(pieces[...].astype(jnp.float32), axis=0).astype(jnp.bfloat16)
        at_layer = band_share(layer)

        def send_layer(step, carry):
            remote(
                piece,
                layers.at[at_layer],
                2,
                spot(across, row, (layer + far_first(step, LAYERS)) % LAYERS),
            ).start()
            return carry

        lax.fori_loop(0, LAYERS - 1, send_layer, 0)
        layers[at_layer] = piece[...]
        await_arrivals(layers.at[pl.ds(0, SENDERS - 1)], recv_sem.at[2])

    @pl.when(jnp.logical_not(owns) & holds)
    def _():
        await_arrivals(layers, recv_sem.at[2])

    @pl.when(holds)
    def _():
        total[...] = jnp.sum(layers[...].astype(jnp.float32), axis=0) / cells

        def send_total(step, carry):
            other = plane_partner(place, step)
            remote(
                total, blocks.at[own_piece], 3, spot(other // GRID_Y, other % GRID_Y, layer)
            ).start()
            return carry

        lax.fori_loop(0, PLANE - 1, send_total, 0)
        blocks[own_piece] = total[...]
        await_arrivals(blocks.at[pl.ds(0, HOLDERS - 1)], recv_sem.at[3])

    @pl.when(jnp.logical_not(holds))
    def _():
        await_arrivals(blocks.at[pl.ds(0, HOLDERS)], recv_sem.at[3])

    @pl.when(owns)
    def _():
        to = pl.multiple_of(band_share(band) * 16, 16)

        def send_parcels(first, count, weights, cells_of):
            turned = jnp.dot(weights, cells_of, preferred_element_type=jnp.float32)
            halves = [
                turned[:, 128 * h : 128 * h + 128].reshape(count, 1, 8, 128) for h in range(2)
            ]
            parcels[first * 16 : (first + count) * 16] = (
                jnp.concatenate(halves, axis=1).reshape(count * 16, 128).astype(jnp.bfloat16)
            )

            def send_parcel(step, carry):
                offset = (layer + far_first(step, LAYERS)) % LAYERS
                low = first % LAYERS

                @pl.when((offset >= low) & (offset < low + count))
                def _():
                    other = (first // LAYERS) * LAYERS + offset
                    at = pl.multiple_of(other * 16, 16)
                    remote(
                        parcels.at[pl.ds(at, 16)],
                        arrived.at[pl.ds(to, 16)],
                        4,
                        {"band": other, "gy": 1 - half_y},
                    ).start()

                return carry

            lax.fori_loop(0, LAYERS, send_parcel, 0)

        buffers = (rows_buf, cols_buf, panel_buf)
        upper = inverse_factor(blocks[0:8].reshape(128, 128), *buffers)
        send_parcels(0, 16, upper.astype(jnp.bfloat16), share[:128])
        corner = blocks[8:16].reshape(128, 128)
        lower_left = full_dot(corner, upper, 1, 1)
        remaining = blocks[16:24].reshape(128, 128) - full_dot(lower_left, lower_left, 1, 1)
        carried = full_dot(lower_left, upper, 1, 0)

        def send_lower(done):
            for begin, end in ((0, 8), (8, 12), (12, 16)):
                if len(done) == end:
                    rows = jnp.concatenate(done[begin:], axis=0)
                    left = -full_dot(rows, carried, 1, 0)
                    weights = jnp.concatenate([left, rows], axis=1).astype(jnp.bfloat16)
                    send_parcels(LAYERS + begin, end - begin, weights, share[...])

        inverse_factor(remaining, *buffers, send_lower)

    middle_block = blocks[8:16].reshape(128, 128)
    gram[:128, :128] = blocks[0:8].reshape(128, 128)
    gram[:128, 128:] = middle_block.T
    gram[128:, :128] = middle_block
    gram[128:, 128:] = blocks[16:24].reshape(128, 128)
    gram_ref[...] = gram[pl.ds(pl.multiple_of(band * 8, 8), 8), :]

    @pl.when(owns & holds)
    def _():
        await_arrivals(partial.at[pl.ds(0, HOLDERS - 1)], send_sem.at[1])
        await_arrivals(pieces.at[pl.ds(0, LAYERS - 1)], send_sem.at[2])

    @pl.when(owns & jnp.logical_not(holds))
    def _():
        await_arrivals(partial, send_sem.at[1])

    await_arrivals(mine_ref, send_sem.at[0])
    for turn_at in range(2):
        for side in range(3):
            halo_copy(turn_at, side).wait_send()

    @pl.when(holds)
    def _():
        await_arrivals(blocks.at[pl.ds(0, PLANE - 1)], send_sem.at[3])

    @pl.when(owns)
    def _():
        await_arrivals(parcels, send_sem.at[4])

    await_arrivals(arrived, recv_sem.at[4])
    rotated_ref[...] = arrived[...]


def filter_rotate(orbitals, potential, cells):
    return pl.pallas_call(
        functools.partial(filter_rotate_kernel, cells),
        out_shape=(
            pltpu.VMEM((OWNERS * 16, 128), jnp.bfloat16),
            pltpu.VMEM((8, FULL), jnp.float32),
        ),
        in_specs=[pl.BlockSpec(memory_space=pl.ANY)] * 2,
        out_specs=(pl.BlockSpec(memory_space=pltpu.VMEM),) * 2,
        scratch_shapes=[
            pltpu.VMEM((8, 6, 8, 128), jnp.float32),
            pltpu.VMEM((6, 8, 128), jnp.float32),
            pltpu.VMEM((FULL, FULL), jnp.float32),
            pltpu.VMEM((FULL, FULL), jnp.bfloat16),
            pltpu.VMEM((2, 8, 128), jnp.float32),
            pltpu.VMEM((2, 8, 8, 128), jnp.float32),
            pltpu.VMEM((2, 8, 128), jnp.float32),
            pltpu.VMEM((BANDS * 16, 128), jnp.bfloat16),
            pltpu.VMEM((OWNERS * 16, 128), jnp.bfloat16),
            pltpu.VMEM((384, 128), jnp.bfloat16),
            pltpu.VMEM((2, 384, 128), jnp.bfloat16),
            pltpu.VMEM((2, 3, 384, 128), jnp.bfloat16),
            pltpu.VMEM((18, 8, 8, 128), jnp.float32),
            pltpu.VMEM((18, 8, 8, 128), jnp.float32),
            pltpu.VMEM((6, 8, 8, 128), jnp.float32),
            pltpu.VMEM((BANDS * 16, 128), jnp.bfloat16),
            pltpu.VMEM((HOLDERS, 16, 128), jnp.bfloat16),
            pltpu.VMEM((PLANE, 16, 128), jnp.bfloat16),
            pltpu.VMEM((16, 128), jnp.bfloat16),
            pltpu.VMEM((SENDERS, 16, 128), jnp.bfloat16),
            pltpu.VMEM((16, 128), jnp.float32),
            pltpu.VMEM((PLANE, 16, 128), jnp.float32),
            pltpu.SemaphoreType.DMA((2, 3)),
            pltpu.SemaphoreType.DMA((2, 3)),
            pltpu.SemaphoreType.DMA((5,)),
            pltpu.SemaphoreType.DMA((5,)),
            pltpu.SemaphoreType.DMA((2,)),
            pltpu.SemaphoreType.REGULAR((3,)),
        ],
        compiler_params=pltpu.CompilerParams(collective_id=1, has_side_effects=True),
        name="filter_rotate",
    )(orbitals, potential)


def place_kernel(tiles_ref, rows_ref, rotated_ref, gram_ref):
    gram_ref[...] = rows_ref[...]
    for at in range(6):
        plane = tiles_ref[64 * at : 64 * at + 64].astype(jnp.float32).reshape(8, 8, 128)
        rotated_ref[:, at] = jnp.swapaxes(plane, 0, 1)


def place_outputs(tiles, rows, shape):
    return pl.pallas_call(
        place_kernel,
        out_shape=(
            jax.ShapeDtypeStruct(shape, jnp.float32),
            jax.ShapeDtypeStruct(rows.shape, jnp.float32),
        ),
        in_specs=[pl.BlockSpec(memory_space=pltpu.VMEM)] * 2,
        out_specs=(pl.BlockSpec(memory_space=pltpu.VMEM),) * 2,
        name="place_outputs",
    )(*(pltpu.with_memory_space_constraint(part, pltpu.VMEM) for part in (tiles, rows)))


def body(orbitals, potential):
    count, size_x, size_y, size_z = orbitals.shape
    total_cells = size_x * size_y * size_z * lax.axis_size("gx") * lax.axis_size("gy")
    tiles, gram_rows = filter_rotate(orbitals, potential, float(total_cells))
    return place_outputs(tiles, gram_rows, orbitals.shape)


def solution(mesh):
    return jax.shard_map(
        body,
        mesh=mesh,
        in_specs=(P("band", "gx", "gy", None), P("gx", "gy", None)),
        out_specs=(P("band", "gx", "gy", None), P("band", None)),
        check_vma=False,
    )
```
